32 devices in a mesh: section: 2 (over core), dp: 4 (over y, x), fsdp: 4 (over z).
Axes of the slice: x: 2, y: 2, z: 4, core: 2. Of those that a mesh axis runs over, the one named last changes fastest.
Arguments:
- token_ids: int32 [32, 128], P(('dp', 'fsdp')), may hold values from 0 to 31999
- next_ids: int32 [32, 128], P(('dp', 'fsdp')), may hold values from 0 to 31999
- seq_lengths: int32 [32], replicated, may hold values from 32 to 128, as said below
- embedding: float32 [32000, 768], P('fsdp'), may hold values from -6 to 6
- embedding_mom: float32 [32000, 768], P('fsdp'), may hold values from -2.9802322e-07 to 2.9802322e-07
- embedding_sec: float32 [32000, 768], P('fsdp'), may hold values from 3.6747965e-15 to 1.4699186e-14
- head_table: float32 [768, 32000], P(None, 'fsdp')
- head_mom: float32 [768, 32000], P(None, 'fsdp'), may hold values from -1.9073486e-06 to 1.9073486e-06
- head_sec: float32 [768, 32000], P(None, 'fsdp'), may hold values from 7.349593e-14 to 2.9398372e-13
- w_qkv: float32 [2, 768, 2304], P('section', 'fsdp'), may hold values from -0.21875 to 0.21875
- qkv_mom: float32 [2, 768, 2304], P('section', 'fsdp'), may hold values from -1.9073486e-06 to 1.9073486e-06
- qkv_sec: float32 [2, 768, 2304], P('section', 'fsdp'), may hold values from 7.349593e-14 to 2.9398372e-13
- w_out: float32 [2, 768, 768], P('section', 'fsdp'), may hold values from -0.875 to 0.875
- out_mom: float32 [2, 768, 768], P('section', 'fsdp'), may hold values from -1.9073486e-06 to 1.9073486e-06
- out_sec: float32 [2, 768, 768], P('section', 'fsdp'), may hold values from 7.349593e-14 to 2.9398372e-13
- w_gateup: float32 [2, 768, 6144], P('section', 'fsdp'), may hold values from -0.21875 to 0.21875
- gateup_mom: float32 [2, 768, 6144], P('section', 'fsdp'), may hold values from -1.9073486e-06 to 1.9073486e-06
- gateup_sec: float32 [2, 768, 6144], P('section', 'fsdp'), may hold values from 7.349593e-14 to 2.9398372e-13
- w_down: float32 [2, 3072, 768], P('section', 'fsdp'), may hold values from -0.109375 to 0.109375
- down_mom: float32 [2, 3072, 768], P('section', 'fsdp'), may hold values from -1.9073486e-06 to 1.9073486e-06
- down_sec: float32 [2, 3072, 768], P('section', 'fsdp'), may hold values from 7.349593e-14 to 2.9398372e-13
- gains: float32 [2, 3, 768], P('section', None, 'fsdp')
- gains_mom: float32 [2, 3, 768], P('section', None, 'fsdp'), may hold values from -9.536743e-06 to 9.536743e-06
- gains_sec: float32 [2, 3, 768], P('section', None, 'fsdp'), may hold values from 1.9108942e-12 to 7.349593e-12
Outputs:
- loss_sum: float32 [], replicated
- token_count: float32 [], replicated
- grad_norm: float32 [], replicated
- new_embedding: float32 [32000, 768], P('fsdp')
- new_embedding_mom: float32 [32000, 768], P('fsdp')
- new_embedding_sec: float32 [32000, 768], P('fsdp')
- embedding_bf16: bfloat16 [32000, 768], P('fsdp')
- new_head: float32 [768, 32000], P(None, 'fsdp')
- new_head_mom: float32 [768, 32000], P(None, 'fsdp')
- new_head_sec: float32 [768, 32000], P(None, 'fsdp')
- head_bf16: bfloat16 [768, 32000], P(None, 'fsdp')
- new_qkv: float32 [2, 768, 2304], P('section', 'fsdp')
- new_qkv_mom: float32 [2, 768, 2304], P('section', 'fsdp')
- new_qkv_sec: float32 [2, 768, 2304], P('section', 'fsdp')
- qkv_bf16: bfloat16 [2, 768, 2304], P('section', 'fsdp')
- new_out: float32 [2, 768, 768], P('section', 'fsdp')
- new_out_mom: float32 [2, 768, 768], P('section', 'fsdp')
- new_out_sec: float32 [2, 768, 768], P('section', 'fsdp')
- out_bf16: bfloat16 [2, 768, 768], P('section', 'fsdp')
- new_gateup: float32 [2, 768, 6144], P('section', 'fsdp')
- new_gateup_mom: float32 [2, 768, 6144], P('section', 'fsdp')
- new_gateup_sec: float32 [2, 768, 6144], P('section', 'fsdp')
- gateup_bf16: bfloat16 [2, 768, 6144], P('section', 'fsdp')
- new_down: float32 [2, 3072, 768], P('section', 'fsdp')
- new_down_mom: float32 [2, 3072, 768], P('section', 'fsdp')
- new_down_sec: float32 [2, 3072, 768], P('section', 'fsdp')
- down_bf16: bfloat16 [2, 3072, 768], P('section', 'fsdp')
- new_gains: float32 [2, 3, 768], P('section', None, 'fsdp')
- new_gains_mom: float32 [2, 3, 768], P('section', None, 'fsdp')
- new_gains_sec: float32 [2, 3, 768], P('section', None, 'fsdp')
The draws below stay inside these ranges and needn't reach their ends.
Inputs may be any that keep to these rules, and one draw needn't show every extreme that they name: Positions p < seq_lengths[i] of row i are real tokens, the rest padding; some row has all 128 positions real.
All inputs are finite; a program needn't handle non-finite values.
Results may differ from the reference program's by a relative error of at most 0.028.
The reference program's roundings to bfloat16 on the way count: a program that leaves them out, or rounds other values in their place, can miss the bound.
Values may be sent and summed in bfloat16 or wider, within the bound.
A program may use at most 704 MiB of HBM per device.

```python
import math
from functools import partial
import jax
import jax.numpy as jnp
import numpy as np
from jax import lax

D = 768
HEADS = 12
HEAD_DIM = 64
FF = 3072
VOCAB = 32000
ROW = 128
STEP_COUNT = 10
SECTIONS = 2
SEQS = 32
PARAMS = 68030976


def draw_seq_lengths(key, part):
    index = jnp.arange(SEQS, dtype=jnp.int32)
    base = ROW // 3 + (ROW - ROW // 3) * index // max(SEQS - 1, 1)
    jitter = jax.random.randint(key, (SEQS,), 0, ROW // 8 + 2, dtype=jnp.int32)
    values = jnp.clip(base - jitter, max(2, ROW // 4), ROW)
    values = values.at[0].set(max(2, ROW // 4))
    return values.at[SEQS - 1].set(ROW).astype(jnp.int32)


def draw_gains(key, part):
    column = jnp.arange(D, dtype=jnp.float32) / (D - 1)
    ramp = 0.6 + 1.2 * column
    noise = jax.random.uniform(key, (SECTIONS, 3, D), jnp.float32, 0.85, 1.15)
    return (ramp[None, None, :] * noise).astype(jnp.float32)


def draw_head_table(key, part):
    column = jnp.arange(VOCAB, dtype=jnp.float32) / (VOCAB - 1)
    base = jax.random.normal(key, (D, VOCAB), jnp.float32)
    ramp = 1.0 + 2.0 * column
    return (base * ramp[None, :] * D ** (-0.5)).astype(jnp.float32)


def set_ends(array, own_key, low, top_value):
    index_at = [jax.random.randint(jax.random.fold_in(own_key, axis), (), 0, length) for axis, length in enumerate(array.shape)]
    main_axis = array.shape.index(max(array.shape))
    beside = index_at[:main_axis] + [(index_at[main_axis] + 1) % array.shape[main_axis]] + index_at[main_axis + 1:]
    return array.at[tuple(index_at)].set(low).at[tuple(beside)].set(top_value)


def levels(key, shape, pieces, least, high):
    def one(dim, shards_of):
        heights = jax.random.uniform(jax.random.fold_in(jax.random.fold_in(key, 6), dim), (shards_of,), jnp.float32, least / len(pieces), high / len(pieces))
        return jnp.repeat(jnp.exp(heights), shape[dim] // shards_of).reshape((-1,) + (1,) * (len(shape) - dim - 1))

    gain = one(*pieces[0])
    for cut in pieces[1:]:
        gain = gain * one(*cut)
    return gain


def cumulative_ranks(number_of, skew):
    portions = [(1 << 20) // math.isqrt(standing ** skew) + 1 for standing in range(1, number_of + 1)]
    spread = 1 + sum(portions) // (1 << 30)
    return np.cumsum(np.array([max(1, weight // spread) for weight in portions]))


def ranked_ids(own_key, dims, amount, slope):
    listing = cumulative_ranks(amount, slope)
    ticket = jax.random.randint(jax.random.fold_in(own_key, 1), dims, 0, int(listing[amount - 1]))
    grade = jnp.searchsorted(jnp.asarray(listing, jnp.int32), ticket, side="right")
    return jax.random.permutation(jax.random.fold_in(own_key, 2), amount)[grade].astype(jnp.int32)


def bell_draw(own_key, extent, scale, most, shards=(), kind=jnp.bfloat16):
    array = scale * jax.random.normal(own_key, extent, jnp.float32)
    if shards:
        array = array * levels(own_key, extent, shards, -0.22, 0.18)
    return jnp.clip(array, -most, most).astype(kind)


def setup_inputs(seed: int = 0) -> dict:
    key_list = jax.random.split(jax.random.key(seed), 25)
    token_ids = set_ends(ranked_ids(key_list[0], (SEQS, ROW), VOCAB, 1), jax.random.fold_in(key_list[0], 3), 0, VOCAB - 1).astype(jnp.int32)
    next_ids = set_ends(ranked_ids(key_list[1], (SEQS, ROW), VOCAB, 1), jax.random.fold_in(key_list[1], 3), 0, VOCAB - 1).astype(jnp.int32)
    seq_lengths = draw_seq_lengths(jax.random.fold_in(key_list[24], 71), 0)
    embedding = bell_draw(key_list[3], (VOCAB, D), 1.0, 6.0, ((0, 4),), jnp.float32)
    embedding_mom = bell_draw(key_list[4], (VOCAB, D), (0.00018 * PARAMS ** -0.5), 2.980232238769531e-07, ((0, 4),), jnp.float32)
    embedding_sec = jnp.clip(jnp.exp(math.log(1.4699186149953053e-14) - 1.3862944 * jax.random.uniform(key_list[5], (VOCAB, D), jnp.float32) ** levels(key_list[5], (VOCAB, D), ((0, 4),), -0.2, 0.2)), 3.674796537488263e-15, 1.4699186149953053e-14)
    head_table = draw_head_table(jax.random.fold_in(key_list[24], 71), 0)
    head_mom = bell_draw(key_list[7], (D, VOCAB), (0.0011 * PARAMS ** -0.5), 1.9073486328125e-06, ((1, 4),), jnp.float32)
    head_sec = jnp.clip(jnp.exp(math.log(2.9398372299906106e-13) - 1.3862944 * jax.random.uniform(key_list[8], (D, VOCAB), jnp.float32) ** levels(key_list[8], (D, VOCAB), ((1, 4),), -0.2, 0.2)), 7.349593074976526e-14, 2.9398372299906106e-13)
    w_qkv = bell_draw(key_list[9], (SECTIONS, D, 3 * D), D ** -0.5, 0.21875, ((0, 2), (1, 4)), jnp.float32)
    qkv_mom = bell_draw(key_list[10], (SECTIONS, D, 3 * D), (0.0011 * PARAMS ** -0.5), 1.9073486328125e-06, ((0, 2), (1, 4)), jnp.float32)
    qkv_sec = jnp.clip(jnp.exp(math.log(2.9398372299906106e-13) - 1.3862944 * jax.random.uniform(key_list[11], (SECTIONS, D, 3 * D), jnp.float32) ** levels(key_list[11], (SECTIONS, D, 3 * D), ((0, 2), (1, 4)), -0.2, 0.2)), 7.349593074976526e-14, 2.9398372299906106e-13)
    w_out = bell_draw(key_list[12], (SECTIONS, D, D), (D // 16) ** -0.5, 0.875, ((0, 2), (1, 4)), jnp.float32)
    out_mom = bell_draw(key_list[13], (SECTIONS, D, D), (0.0011 * PARAMS ** -0.5), 1.9073486328125e-06, ((0, 2), (1, 4)), jnp.float32)
    out_sec = jnp.clip(jnp.exp(math.log(2.9398372299906106e-13) - 1.3862944 * jax.random.uniform(key_list[14], (SECTIONS, D, D), jnp.float32) ** levels(key_list[14], (SECTIONS, D, D), ((0, 2), (1, 4)), -0.2, 0.2)), 7.349593074976526e-14, 2.9398372299906106e-13)
    w_gateup = bell_draw(key_list[15], (SECTIONS, D, 2 * FF), D ** -0.5, 0.21875, ((0, 2), (1, 4)), jnp.float32)
    gateup_mom = bell_draw(key_list[16], (SECTIONS, D, 2 * FF), (0.0011 * PARAMS ** -0.5), 1.9073486328125e-06, ((0, 2), (1, 4)), jnp.float32)
    gateup_sec = jnp.clip(jnp.exp(math.log(2.9398372299906106e-13) - 1.3862944 * jax.random.uniform(key_list[17], (SECTIONS, D, 2 * FF), jnp.float32) ** levels(key_list[17], (SECTIONS, D, 2 * FF), ((0, 2), (1, 4)), -0.2, 0.2)), 7.349593074976526e-14, 2.9398372299906106e-13)
    w_down = bell_draw(key_list[18], (SECTIONS, FF, D), FF ** -0.5, 0.109375, ((0, 2), (1, 4)), jnp.float32)
    down_mom = bell_draw(key_list[19], (SECTIONS, FF, D), (0.0011 * PARAMS ** -0.5), 1.9073486328125e-06, ((0, 2), (1, 4)), jnp.float32)
    down_sec = jnp.clip(jnp.exp(math.log(2.9398372299906106e-13) - 1.3862944 * jax.random.uniform(key_list[20], (SECTIONS, FF, D), jnp.float32) ** levels(key_list[20], (SECTIONS, FF, D), ((0, 2), (1, 4)), -0.2, 0.2)), 7.349593074976526e-14, 2.9398372299906106e-13)
    gains = draw_gains(jax.random.fold_in(key_list[24], 71), 0)
    gains_mom = bell_draw(key_list[22], (SECTIONS, 3, D), (0.0055 * PARAMS ** -0.5), 9.5367431640625e-06, ((0, 2), (2, 4)), jnp.float32)
    gains_sec = jnp.clip(jnp.exp(math.log(7.34959315629169e-12) - 1.3470737 * jax.random.uniform(key_list[23], (SECTIONS, 3, D), jnp.float32) ** levels(key_list[23], (SECTIONS, 3, D), ((0, 2), (2, 4)), -0.2, 0.2)), 1.9108941859413697e-12, 7.34959315629169e-12)
    return dict(token_ids=token_ids, next_ids=next_ids, seq_lengths=seq_lengths, embedding=embedding, embedding_mom=embedding_mom, embedding_sec=embedding_sec, head_table=head_table, head_mom=head_mom, head_sec=head_sec, w_qkv=w_qkv, qkv_mom=qkv_mom, qkv_sec=qkv_sec, w_out=w_out, out_mom=out_mom, out_sec=out_sec, w_gateup=w_gateup, gateup_mom=gateup_mom, gateup_sec=gateup_sec, w_down=w_down, down_mom=down_mom, down_sec=down_sec, gains=gains, gains_mom=gains_mom, gains_sec=gains_sec)


EPS = 1e-05
MTP_WEIGHT = 0.3
CLIP = 0.01
BETA1 = 0.9
BETA2 = 0.95
ADAM_EPS = 1e-08
HIGHEST = lax.Precision.HIGHEST

@jax.custom_vjp
def low(v):
    return lax.optimization_barrier(v.astype(jnp.bfloat16)).astype(jnp.float32)

@jax.custom_vjp
def low_back(v):
    return v

def low_keep(v):
    return (low(v), None)

def low_pass(kept, grad):
    return (grad,)

def back_keep(v):
    return (v, None)

def back_low(kept, grad):
    return (low(grad),)
low.defvjp(low_keep, low_pass)
low_back.defvjp(back_keep, back_low)

def matmul_high(left, right):
    return jnp.dot(left, right, precision=HIGHEST)

def norm_apply(values, scale_gain):
    return values * lax.rsqrt(lax.optimization_barrier(jnp.mean(values * values, axis=-1, keepdims=True)) + EPS) * scale_gain

def rope_tables(row_count, head_width):
    half_width = head_width // 2
    position = jnp.arange(row_count, dtype=jnp.float32)[:, None]
    frequency = 10000.0 ** (-jnp.arange(half_width, dtype=jnp.float32) / half_width)
    angles = position * frequency[None, :]
    return (jnp.cos(angles), jnp.sin(angles))

def rotate(values, cosine, sine_table):
    half_width = values.shape[-1] // 2
    first, second = (values[..., :half_width], values[..., half_width:])
    return jnp.concatenate([first * cosine - second * sine_table, second * cosine + first * sine_table], axis=-1)

def layer_apply(inputs, w_qkv, w_out, w_gateup, w_down, attn_gain, ffn_gain):
    row_count = inputs.shape[0]
    normed = low(norm_apply(inputs, attn_gain))
    packed = low_back(matmul_high(normed, w_qkv))
    split = packed.reshape(row_count, 3, HEADS, HEAD_DIM).transpose(1, 2, 0, 3)
    cosine, sine_table = rope_tables(row_count, HEAD_DIM)
    queries = low(rotate(split[0], cosine, sine_table))
    keys_rot = low(rotate(split[1], cosine, sine_table))
    values_low = low(split[2])
    scores = low_back(jnp.einsum('hqd,hkd->hqk', queries, keys_rot, precision=HIGHEST) * HEAD_DIM ** (-0.5))
    position = jnp.arange(row_count)
    causal = position[:, None] >= position[None, :]
    scores = jnp.where(causal[None], scores, -1e+30)
    shifted = jnp.exp(scores - lax.optimization_barrier(jnp.max(scores, axis=-1, keepdims=True)))
    probs = low(shifted / lax.optimization_barrier(jnp.sum(shifted, axis=-1, keepdims=True)))
    mixed = jnp.einsum('hqk,hkd->hqd', probs, values_low, precision=HIGHEST)
    mixed = low(low_back(mixed.transpose(1, 0, 2).reshape(row_count, D)))
    after_attn = inputs + low_back(matmul_high(mixed, w_out))
    normed_ffn = low(norm_apply(after_attn, ffn_gain))
    gate_up = low_back(matmul_high(normed_ffn, w_gateup))
    hidden = low(jax.nn.silu(gate_up[:, :FF]) * gate_up[:, FF:])
    return after_attn + low_back(matmul_high(hidden, w_down))

def head_loss(rows_in, head_low, targets, weights_tok):
    logits = low_back(matmul_high(low(rows_in), head_low))
    highest = lax.optimization_barrier(jnp.max(logits, axis=-1, keepdims=True))
    lse = highest[:, 0] + jnp.log(lax.optimization_barrier(jnp.sum(jnp.exp(logits - highest), axis=-1)))
    picked = jnp.take_along_axis(logits, targets[:, None], axis=-1)[:, 0]
    return jnp.sum((lse - picked) * weights_tok)

def row_terms(lowered, tokens_row, next_row, length):
    table, head_low, w_qkv, w_out, w_gateup, w_down, gain_low = lowered
    state = table[tokens_row]
    state = layer_apply(state, w_qkv[0], w_out[0], w_gateup[0], w_down[0], gain_low[0, 0], gain_low[0, 1])
    state = low(low_back(state))
    state = layer_apply(state, w_qkv[1], w_out[1], w_gateup[1], w_down[1], gain_low[1, 0], gain_low[1, 1])
    final_state = norm_apply(state, gain_low[1, 2])
    position = jnp.arange(ROW)
    main = head_loss(final_state, head_low, next_row, (position < length).astype(jnp.float32))
    sent_state = low(low_back(final_state))
    merged = norm_apply(sent_state + table[next_row], gain_low[0, 2])
    shifted_targets = jnp.concatenate([next_row[1:], next_row[:1]])
    weights_mtp = (position < length - 1).astype(jnp.float32) * MTP_WEIGHT
    return main + head_loss(merged, head_low, shifted_targets, weights_mtp)

def adam_update(weight, grad, first_mom, second_mom, rate, decay):
    mom_new = BETA1 * first_mom + (1.0 - BETA1) * grad
    sec_new = BETA2 * second_mom + (1.0 - BETA2) * grad * grad
    mom_hat = mom_new / (1.0 - BETA1 ** STEP_COUNT)
    sec_hat = sec_new / (1.0 - BETA2 ** STEP_COUNT)
    weight_new = weight - rate * (mom_hat / (jnp.sqrt(sec_hat) + ADAM_EPS) + decay * weight)
    return (weight_new, mom_new, sec_new)

def reference(token_ids, next_ids, seq_lengths, embedding, embedding_mom, embedding_sec, head_table, head_mom, head_sec, w_qkv, qkv_mom, qkv_sec, w_out, out_mom, out_sec, w_gateup, gateup_mom, gateup_sec, w_down, down_mom, down_sec, gains, gains_mom, gains_sec):
    token_total = jnp.sum(seq_lengths).astype(jnp.float32)
    group = math.gcd(SEQS, max(1, 1024 // ROW))
    batches = (token_ids.reshape(SEQS // group, group, ROW), next_ids.reshape(SEQS // group, group, ROW), seq_lengths.reshape(SEQS // group, group))

    def total(params):
        lowered = tuple((low(item) for item in params))

        def one_group(carry, batch):
            tokens_blk, next_blk, length_blk = batch
            terms = jax.vmap(partial(row_terms, lowered))(tokens_blk, next_blk, length_blk)
            return (carry + jnp.sum(terms), None)
        result, _ = lax.scan(jax.checkpoint(one_group), jnp.zeros((), jnp.float32), batches)
        return result
    params = (embedding, head_table, w_qkv, w_out, w_gateup, w_down, gains)
    loss_sum, pullback = jax.vjp(total, params)
    grads, = pullback(jnp.ones((), jnp.float32) / token_total)
    squares = jnp.zeros((), jnp.float32)
    for item in grads:
        squares = squares + jnp.sum(item * item)
    grad_norm = jnp.sqrt(squares)
    clip_scale = CLIP / jnp.maximum(grad_norm, CLIP)
    moments = ((embedding_mom, embedding_sec), (head_mom, head_sec), (qkv_mom, qkv_sec), (out_mom, out_sec), (gateup_mom, gateup_sec), (down_mom, down_sec), (gains_mom, gains_sec))
    rates = (0.6, 0.03, 0.03, 0.12, 0.03, 0.03, 0.6)
    decays = (0.1, 0.1, 0.1, 0.1, 0.1, 0.1, 0.0)
    results = []
    for index in range(7):
        weight_new, mom_new, sec_new = adam_update(params[index], grads[index] * clip_scale, moments[index][0], moments[index][1], rates[index], decays[index])
        results.append((weight_new, mom_new, sec_new))
    outputs = [loss_sum, token_total, grad_norm]
    for index in range(6):
        outputs.extend([results[index][0], results[index][1], results[index][2], results[index][0].astype(jnp.bfloat16)])
    outputs.extend([results[6][0], results[6][1], results[6][2]])
    return tuple(outputs)
```

```python
import functools
import math

import jax
import jax.numpy as jnp
from jax import lax
from jax.experimental import pallas as pl
from jax.experimental.pallas import tpu as pltpu
from jax.sharding import PartitionSpec as P

D = 768
HEADS = 12
HEAD_DIM = 64
FF = 3072
ROW = 128
MB = 2
STEP_COUNT = 10
SHARE = 4


EPS = 1e-05
MTP_WEIGHT = 0.3
CLIP = 0.01
BETA1 = 0.9
BETA2 = 0.95
ADAM_EPS = 1e-08
LOW = jnp.bfloat16
WIDE = jnp.float32

MESH = pl.DeviceIdType.MESH

def weights_kernel(planes, replicas, units, rows, *refs):
    n = len(rows)
    own, full = refs[:n], refs[n:2*n]
    send, recv, local = refs[2*n:]
    z = lax.axis_index("fsdp")
    i = lax.axis_index("dp")
    half = replicas // 2
    low, top = i % 2, i // half
    q = top * 2 + low
    xn = i + 1 - 2 * low
    yn = (i + half) % replicas
    qx = top * 2 + 1 - low
    qy = (1 - top) * 2 + low
    barrier = pltpu.get_barrier_semaphore()
    for step in range(1, planes):
        pl.semaphore_signal(barrier, inc=1, device_id={"fsdp": (z + step) % planes}, device_id_type=MESH)
    pl.semaphore_signal(barrier, inc=1, device_id={"dp": xn}, device_id_type=MESH)
    pl.semaphore_signal(barrier, inc=1, device_id={"dp": yn}, device_id_type=MESH)
    pl.semaphore_wait(barrier, planes + 1)
    keep = []
    for m in range(n):
        c = pltpu.make_async_copy(own[m], full[m].at[pl.ds(pl.multiple_of(z * rows[m], 16), rows[m]), :], local.at[m])
        c.start()
        keep.append(c)
    per = 3 * (planes - 1) + (planes - 1)
    def cp(src, dst, k, dev):
        return pltpu.make_async_remote_copy(src_ref=src, dst_ref=dst, send_sem=send.at[k], recv_sem=recv.at[k], device_id=dev, device_id_type=MESH)
    def block(m, plane, quarter, cols):
        r = rows[m] // 4
        return full[m].at[pl.ds(pl.multiple_of(plane * rows[m] + quarter * r, 16), r), pl.ds(cols[0], cols[1])]
    first, second, third = [], [], []
    for u, (m, cols, order) in enumerate(units):
        r = rows[m] // 4
        group = []
        for step in range(1, planes):
            src = own[m].at[pl.ds(pl.multiple_of(q * r, 16), r), pl.ds(cols[0], cols[1])]
            c = cp(src, block(m, z, q, cols), u * per + step - 1, {"fsdp": (z + step) % planes})
            c.start()
            group.append(c)
        first.append(group)
    def phase2(u):
        m, cols, order = units[u]
        base = u * per + planes - 1
        group = []
        for step in range(1, planes):
            first[u][step - 1].wait_recv()
            b = block(m, (z + planes - step) % planes, q, cols)
            c = cp(b, b, base + step - 1, {"dp": xn if order == 0 else yn})
            c.start()
            group.append(c)
        second.append(group)
    def phase3(u):
        m, cols, order = units[u]
        base = u * per + 2 * (planes - 1)
        group = []
        for step in range(1, planes):
            second[u][step - 1].wait_recv()
            for w, quarter in enumerate((q, qx if order == 0 else qy)):
                b = block(m, (z + planes - step) % planes, quarter, cols)
                c = cp(b, b, base + 2 * (step - 1) + w, {"dp": yn if order == 0 else xn})
                c.start()
                group.append(c)
        third.append(group)
    total = len(units)
    for u in range(total):
        phase2(u)
        if u >= 1:
            phase3(u - 1)
    phase3(total - 1)
    for u in range(total):
        for c in third[u]:
            c.wait_recv()
    for u in range(total):
        for c in first[u] + second[u] + third[u]:
            c.wait_send()
    for c in keep:
        c.wait()

def gather_weights(planes, replicas, shards):
    rows = [w.shape[0] for w in shards]
    if any(r % (SHARE * 16) for r in rows):
        return [lax.all_gather(w, "fsdp", axis=0, tiled=True) for w in shards]
    units = []
    for m, w in enumerate(shards):
        width = w.shape[1]
        parts = 4 if width > 4096 else 2
        step = width // parts
        for p in range(parts):
            units.append((m, (p * step, step), p % 2))
    copies = len(units) * 4 * (planes - 1)
    return pl.pallas_call(
        functools.partial(weights_kernel, planes, replicas, units, rows),
        out_shape=[jax.ShapeDtypeStruct((planes * w.shape[0], w.shape[1]), w.dtype) for w in shards],
        in_specs=[pl.BlockSpec(memory_space=pl.ANY)] * len(shards),
        out_specs=[pl.BlockSpec(memory_space=pl.ANY)] * len(shards),
        scratch_shapes=[pltpu.SemaphoreType.DMA((copies,)), pltpu.SemaphoreType.DMA((copies,)), pltpu.SemaphoreType.DMA((len(shards),))],
        compiler_params=pltpu.CompilerParams(collective_id=1, has_side_effects=True),
        name="gather_weights",
    )(*shards)


def norm_fwd(values, scale_gain):
    inverse = lax.rsqrt(jnp.mean(values * values, axis=-1, keepdims=True) + EPS)
    return values * inverse * scale_gain


def norm_back(values, scale_gain, upstream):
    _, pullback = jax.vjp(norm_fwd, values, scale_gain)
    return pullback(upstream)


def rope_tables(row_count, head_width):
    half_width = head_width // 2
    position = jnp.arange(row_count, dtype=jnp.float32)[:, None]
    frequency = 10000.0 ** (-jnp.arange(half_width, dtype=jnp.float32) / half_width)
    angles = position * frequency[None, :]
    return (jnp.cos(angles), jnp.sin(angles))


def rotate(values, cosine, sine_table):
    half_width = values.shape[-1] // 2
    first, second = (values[..., :half_width], values[..., half_width:])
    return jnp.concatenate(
        [first * cosine - second * sine_table, second * cosine + first * sine_table], axis=-1
    )


def contract_rows(left, right):
    return lax.dot_general(
        left, right, (((0,), (0,)), ((), ())), preferred_element_type=jnp.float32
    )


def contract_cols(left, right):
    return lax.dot_general(
        left, right, (((1,), (1,)), ((), ())), preferred_element_type=jnp.float32
    )


def swiglu(gate_up):
    return jax.nn.silu(gate_up[:, :FF]) * gate_up[:, FF:]


def shift(block, axis, distance):
    count = lax.axis_size(axis)
    return lax.ppermute(block, axis, [(i, (i + distance) % count) for i in range(count)])


def swap(block, axis, mask):
    count = lax.axis_size(axis)
    return lax.ppermute(block, axis, [(i, i ^ mask) for i in range(count)])


def pick(array, index, axis=0):
    return lax.dynamic_index_in_dim(array, index, axis, keepdims=False)


def layer_fwd(inputs, weights):
    w_qkv, w_out, w_gateup, w_down, attn_gain, ffn_gain = weights
    normed = norm_fwd(inputs, attn_gain).astype(LOW)
    packed = jnp.dot(normed, w_qkv, preferred_element_type=WIDE)
    split = packed.reshape(MB, ROW, 3, HEADS, HEAD_DIM).transpose(2, 0, 3, 1, 4)
    split = split.reshape(3, MB * HEADS, ROW, HEAD_DIM)
    cosine, sine_table = rope_tables(ROW, HEAD_DIM)
    queries = rotate(split[0], cosine, sine_table).astype(LOW)
    keys_rot = rotate(split[1], cosine, sine_table).astype(LOW)
    values_low = split[2].astype(LOW)
    scores = jnp.einsum(
        "hqd,hkd->hqk", queries, keys_rot, preferred_element_type=WIDE
    ) * HEAD_DIM ** (-0.5)
    position = jnp.arange(ROW)
    causal = position[:, None] >= position[None, :]
    scores = jnp.where(causal[None], scores, -1e30)
    shifted = jnp.exp(scores - jnp.max(scores, axis=-1, keepdims=True))
    probs = shifted / jnp.sum(shifted, axis=-1, keepdims=True)
    probs_low = probs.astype(LOW)
    mixed = jnp.einsum("hqk,hkd->hqd", probs_low, values_low, preferred_element_type=WIDE)
    mixed = mixed.reshape(MB, HEADS, ROW, HEAD_DIM).transpose(0, 2, 1, 3)
    mixed_low = mixed.reshape(MB * ROW, D).astype(LOW)
    after_attn = inputs + jnp.dot(mixed_low, w_out, preferred_element_type=WIDE)
    normed_ffn = norm_fwd(after_attn, ffn_gain).astype(LOW)
    gate_up = jnp.dot(normed_ffn, w_gateup, preferred_element_type=WIDE)
    hidden = swiglu(gate_up).astype(LOW)
    output = after_attn + jnp.dot(hidden, w_down, preferred_element_type=WIDE)
    saved = (
        normed,
        queries,
        keys_rot,
        values_low,
        probs,
        probs_low,
        mixed_low,
        after_attn,
        normed_ffn,
        gate_up,
        hidden,
    )
    return (output, saved)


def layer_back(inputs, weights, saved, upstream):
    w_qkv, w_out, w_gateup, w_down, attn_gain, ffn_gain = weights
    (
        normed,
        queries,
        keys_rot,
        values_low,
        probs,
        probs_low,
        mixed_low,
        after_attn,
        normed_ffn,
        gate_up,
        hidden,
    ) = saved
    upstream_low = upstream.astype(LOW)
    grad_hidden = contract_cols(upstream_low, w_down)
    _, pullback = jax.vjp(swiglu, gate_up)
    grad_gu = pullback(grad_hidden)[0].astype(LOW)
    grad_nffn = contract_cols(grad_gu, w_gateup)
    back_ffn, grad_ffn_gain = norm_back(after_attn, ffn_gain, grad_nffn)
    grad_after = upstream + back_ffn
    after_low = grad_after.astype(LOW)
    grad_mixed = contract_cols(after_low, w_out).astype(LOW)
    grad_mixed = grad_mixed.reshape(MB, ROW, HEADS, HEAD_DIM).transpose(0, 2, 1, 3)
    grad_mixed = grad_mixed.reshape(MB * HEADS, ROW, HEAD_DIM)
    grad_probs = jnp.einsum("hqd,hkd->hqk", grad_mixed, values_low, preferred_element_type=WIDE)
    grad_values = jnp.einsum("hqk,hqd->hkd", probs_low, grad_mixed, preferred_element_type=WIDE)
    grad_scores = probs * (grad_probs - jnp.sum(probs * grad_probs, axis=-1, keepdims=True))
    grad_scores = grad_scores.astype(LOW)
    scale_attn = HEAD_DIM ** (-0.5)
    grad_query = (
        jnp.einsum("hqk,hkd->hqd", grad_scores, keys_rot, preferred_element_type=WIDE)
        * scale_attn
    )
    grad_key = (
        jnp.einsum("hqk,hqd->hkd", grad_scores, queries, preferred_element_type=WIDE)
        * scale_attn
    )
    cosine, sine_table = rope_tables(ROW, HEAD_DIM)
    grad_query = rotate(grad_query, cosine, -sine_table)
    grad_key = rotate(grad_key, cosine, -sine_table)
    grad_packed = jnp.stack([grad_query, grad_key, grad_values]).astype(LOW)
    grad_packed = grad_packed.reshape(3, MB, HEADS, ROW, HEAD_DIM).transpose(1, 3, 0, 2, 4)
    grad_packed = grad_packed.reshape(MB * ROW, 3 * D)
    grad_normed = contract_cols(grad_packed, w_qkv)
    back_attn, grad_attn_gain = norm_back(inputs, attn_gain, grad_normed)
    grad_inputs = grad_after + back_attn
    return (
        grad_inputs,
        (grad_packed, after_low, grad_gu, upstream_low),
        (grad_attn_gain, grad_ffn_gain),
    )


def plane_masks(replicas):
    return (0, 1, replicas // 2, 1 + replicas // 2)


def plane_rank(replicas):
    index = lax.axis_index("dp")
    return (index // (replicas // 2)) * 2 + index % 2


def everyone(block, replicas):
    return jnp.concatenate(
        [block] + [swap(block, "dp", mask) for mask in plane_masks(replicas)[1:]], axis=0
    )


def quarters(block, replicas):
    rank = plane_rank(replicas)
    width = block.shape[1] // SHARE
    pieces = []
    for offset, mask in enumerate(plane_masks(replicas)):
        piece = lax.dynamic_slice_in_dim(block, (rank ^ offset) * width, width, 1)
        pieces.append(swap(piece, "dp", mask) if mask else piece)
    return jnp.concatenate(pieces, axis=0)


def rows_to_owner(partial):
    planes = lax.axis_size("fsdp")
    me = lax.axis_index("fsdp")
    blocks = partial.reshape((planes, partial.shape[0] // planes) + partial.shape[1:])
    total = pick(blocks, me).astype(WIDE)
    for step in range(1, planes):
        total = total + shift(pick(blocks, (me + step) % planes), "fsdp", step).astype(WIDE)
    return total


def other_replicas(total, replicas):
    mask = 2
    while mask < replicas // 2:
        total = total + swap(total.astype(LOW), "dp", mask).astype(WIDE)
        mask *= 2
    return total


def columns_from_plane(piece, replicas):
    rank = plane_rank(replicas)
    height, width = piece.shape
    full = jnp.zeros((height, SHARE * width), piece.dtype)
    for offset, mask in enumerate(plane_masks(replicas)):
        block = swap(piece, "dp", mask) if mask else piece
        full = lax.dynamic_update_slice_in_dim(full, block, (rank ^ offset) * width, 1)
    return full


def bit_of(axis, mask):
    return (lax.axis_index(axis) // mask) % 2


def halve(block, axis, mask):
    bit = bit_of(axis, mask)
    pair = block.reshape((2, block.shape[0] // 2) + block.shape[1:])
    theirs = swap(pick(pair, 1 - bit), axis, mask)
    return (pick(pair, bit).astype(WIDE) + theirs.astype(WIDE)).astype(LOW)


def double(block, axis, mask):
    theirs = swap(block, axis, mask)
    bit = bit_of(axis, mask)
    return jnp.where(
        bit == 0,
        jnp.concatenate([block, theirs], axis=0),
        jnp.concatenate([theirs, block], axis=0),
    )


def mask_orders(replicas):
    masks = [1 << k for k in range(replicas.bit_length() - 1)]
    return (masks, masks[::-1])


def reduce_shared(block, replicas):
    mine = halve(block, "section", 1)
    pieces = []
    for part, order in zip(jnp.split(mine, 2, axis=0), mask_orders(replicas)):
        for mask in order:
            part = halve(part, "dp", mask)
        pieces.append(part)
    return pieces


def gather_shared(pieces, replicas):
    parts = []
    for part, order in zip(pieces, mask_orders(replicas)):
        for mask in order[::-1]:
            part = double(part, "dp", mask)
        parts.append(part)
    return double(jnp.concatenate(parts, axis=0), "section", 1)


def head_pass(rows_low, targets, weights_tok, head_low, vocab_start, token_total):
    planes = lax.axis_size("fsdp")
    gathered = jnp.concatenate(
        [rows_low] + [shift(rows_low, "fsdp", step) for step in range(1, planes)], axis=0
    )
    local_vocab = head_low.shape[1]
    columns = jnp.arange(local_vocab, dtype=jnp.int32)
    local_targets = targets - vocab_start
    hit = columns[None, :] == local_targets[:, None]
    logits = jnp.dot(gathered, head_low, preferred_element_type=WIDE)
    highest = jnp.max(logits, axis=-1)
    summed = jnp.sum(jnp.exp(logits - highest[:, None]), axis=-1)
    picked = jnp.sum(jnp.where(hit, logits, 0.0), axis=-1)
    stats = jnp.stack([highest, summed, picked]).reshape(3, planes, -1)
    parts = [stats] + [
        jnp.roll(shift(stats, "fsdp", step), step, axis=1) for step in range(1, planes)
    ]
    parts = jnp.stack(parts)
    peak = jnp.max(parts[:, 0], axis=0)
    total = jnp.sum(parts[:, 1] * jnp.exp(parts[:, 0] - peak[None]), axis=0)
    lse = (peak + jnp.log(total)).reshape(-1)
    loss_part = jnp.sum((lse - jnp.sum(parts[:, 2], axis=0).reshape(-1)) * weights_tok)
    factor = weights_tok / token_total
    onehot = hit.astype(WIDE)
    grads_low = ((jnp.exp(logits - lse[:, None]) - onehot) * factor[:, None]).astype(LOW)
    grad_head = contract_rows(gathered, grads_low).astype(LOW)
    partial = contract_cols(grads_low, head_low).reshape(planes, -1, D)
    grad_rows = partial[0]
    for step in range(1, planes):
        grad_rows = grad_rows + shift(partial[step].astype(LOW), "fsdp", planes - step).astype(WIDE)
    return (loss_part, grad_head, grad_rows)


def adam_update(weight, grad, first_mom, second_mom, rate, decay):
    mom_new = BETA1 * first_mom + (1.0 - BETA1) * grad
    sec_new = BETA2 * second_mom + (1.0 - BETA2) * grad * grad
    mom_hat = mom_new / (1.0 - BETA1**STEP_COUNT)
    sec_hat = sec_new / (1.0 - BETA2**STEP_COUNT)
    weight_new = weight - rate * (mom_hat / (jnp.sqrt(sec_hat) + ADAM_EPS) + decay * weight)
    return (weight_new, mom_new, sec_new)


def per_device(
    token_ids,
    next_ids,
    seq_lengths,
    embedding,
    embedding_mom,
    embedding_sec,
    head_table,
    head_mom,
    head_sec,
    w_qkv,
    qkv_mom,
    qkv_sec,
    w_out,
    out_mom,
    out_sec,
    w_gateup,
    gateup_mom,
    gateup_sec,
    w_down,
    down_mom,
    down_sec,
    gains,
    gains_mom,
    gains_sec,
):
    planes = lax.axis_size("fsdp")
    replicas = lax.axis_size("dp")
    first = lax.axis_index("section") == 0
    first_f = first.astype(WIDE)
    me = lax.axis_index("fsdp")
    token_total = jnp.sum(seq_lengths).astype(WIDE)
    tokens = MB * ROW

    my_ids = jnp.stack([token_ids.reshape(-1), next_ids.reshape(-1)])
    rel_ids = jnp.stack([my_ids] + [shift(my_ids, "fsdp", step) for step in range(1, planes)])
    my_kind = jnp.where(first, rel_ids[:, 0], rel_ids[:, 1])
    vocab_rows = embedding.shape[0]
    vocab_start = me * vocab_rows
    local = my_kind - vocab_start
    inside = (local >= 0) & (local < vocab_rows)
    found = jnp.take(embedding, jnp.clip(local, 0, vocab_rows - 1), axis=0)
    found = jnp.where(inside[..., None], found, 0.0).astype(LOW)
    looked = found[0].astype(WIDE)
    for step in range(1, planes):
        looked = looked + shift(found[step], "fsdp", planes - step).astype(WIDE)
    next_embed = swap(looked.astype(LOW), "section", 1).astype(WIDE)

    full = gather_weights(
        planes,
        replicas,
        [w_qkv[0].astype(LOW), w_out[0].astype(LOW), w_gateup[0].astype(LOW), w_down[0].astype(LOW)],
    )
    gains_full = lax.all_gather(gains[0].astype(LOW), "fsdp", axis=1, tiled=True).astype(WIDE)
    layer_weights = (full[0], full[1], full[2], full[3], gains_full[0], gains_full[1])
    head_gain = gains_full[2]
    head_low = head_table.astype(LOW)

    first_out, _ = layer_fwd(looked, layer_weights)
    middle = swap(first_out.astype(LOW), "section", 1).astype(WIDE)
    layer_in = jnp.where(first, looked, middle)
    layer_out, saved = layer_fwd(layer_in, layer_weights)
    final_state = norm_fwd(layer_out, head_gain)
    arrived = swap(final_state.astype(LOW), "section", 1).astype(WIDE)
    merged_in = jnp.where(first, arrived + next_embed, layer_out)
    head_in = norm_fwd(merged_in, head_gain)

    lengths = seq_lengths.reshape(replicas, planes, MB)[lax.axis_index("dp")]
    rel_planes = (me - jnp.arange(planes)) % planes
    lengths = jnp.take(lengths, rel_planes, axis=0)
    targets_main = rel_ids[:, 1].reshape(planes, MB, ROW)
    shifted = jnp.concatenate([targets_main[..., 1:], targets_main[..., :1]], axis=-1)
    targets = jnp.where(first, shifted, targets_main)
    limit = lengths - first.astype(jnp.int32)
    positions = jnp.arange(ROW, dtype=jnp.int32)
    weights_tok = (positions < limit[..., None]).astype(WIDE) * jnp.where(first, MTP_WEIGHT, 1.0)
    loss_part, grad_head, grad_in = head_pass(
        head_in.astype(LOW),
        targets.reshape(-1),
        weights_tok.reshape(-1),
        head_low,
        vocab_start,
        token_total,
    )
    head_pieces = reduce_shared(grad_head, replicas)

    merged_grad, mtp_gain = norm_back(merged_in, head_gain, grad_in)
    merged_low = merged_grad.astype(LOW)
    sent = swap(merged_low, "section", 1).astype(WIDE)
    top_grad, top_gain = norm_back(layer_out, head_gain, grad_in + sent)
    head_gain_grad = jnp.where(first, mtp_gain, top_gain)
    below, _, _ = layer_back(layer_in, layer_weights, saved, top_grad)
    upstream = jnp.where(first, swap(below.astype(LOW), "section", 1).astype(WIDE), top_grad)
    grad_inputs, right, gain_parts = layer_back(layer_in, layer_weights, saved, upstream)

    left = (saved[0], saved[6], saved[8], saved[10])
    shards = []
    for a_side, b_side in zip(left, right):
        a_all = everyone(a_side, replicas)
        b_all = quarters(b_side, replicas)
        part = contract_rows(a_all, b_all).astype(LOW)
        shards.append(other_replicas(rows_to_owner(part), replicas).astype(LOW))
    gains_grad = jnp.stack([gain_parts[0], gain_parts[1], head_gain_grad])
    gains_grad = lax.psum(
        lax.psum_scatter(gains_grad, "fsdp", scatter_dimension=1, tiled=True), "dp"
    )

    row_grads = jnp.where(first, grad_inputs.astype(LOW), sent.astype(LOW))
    rel_grads = jnp.stack([row_grads] + [shift(row_grads, "fsdp", step) for step in range(1, planes)])
    slot = jnp.where(inside, local, vocab_rows)
    grad_table = jnp.zeros((vocab_rows, D), WIDE)
    grad_table = grad_table.at[slot.reshape(-1)].add(
        rel_grads.reshape(-1, D).astype(WIDE), mode="drop"
    )
    table_pieces = reduce_shared(grad_table.astype(LOW), replicas)

    def square(item):
        wide = item.astype(WIDE)
        return jnp.sum(wide * wide)

    squares = jnp.zeros((), WIDE)
    for item in shards:
        squares = squares + square(item) * (SHARE / replicas)
    for item in head_pieces + table_pieces:
        squares = squares + square(item)
    squares = squares + square(gains_grad) / replicas
    totals = lax.psum(jnp.stack([squares, loss_part / planes]), ("section", "dp", "fsdp"))
    grad_norm = jnp.sqrt(totals[0])
    loss_total = totals[1]
    clip_scale = CLIP / jnp.maximum(grad_norm, CLIP)

    grad_table = gather_shared(table_pieces, replicas).astype(WIDE)
    grad_head = gather_shared(head_pieces, replicas).astype(WIDE)
    layer_grads = [columns_from_plane(item, replicas).astype(WIDE) for item in shards]
    params = (embedding, head_table, w_qkv[0], w_out[0], w_gateup[0], w_down[0], gains[0])
    grads_all = (grad_table, grad_head, *layer_grads, gains_grad)
    moments = (
        (embedding_mom, embedding_sec),
        (head_mom, head_sec),
        (qkv_mom[0], qkv_sec[0]),
        (out_mom[0], out_sec[0]),
        (gateup_mom[0], gateup_sec[0]),
        (down_mom[0], down_sec[0]),
        (gains_mom[0], gains_sec[0]),
    )
    rates = (0.6, 0.03, 0.03, 0.12, 0.03, 0.03, 0.6)
    decays = (0.1, 0.1, 0.1, 0.1, 0.1, 0.1, 0.0)
    outputs = [loss_total, token_total, grad_norm]
    for index in range(7):
        weight_new, mom_new, sec_new = adam_update(
            params[index],
            grads_all[index] * clip_scale,
            moments[index][0],
            moments[index][1],
            rates[index],
            decays[index],
        )
        if index >= 2:
            weight_new, mom_new, sec_new = (weight_new[None], mom_new[None], sec_new[None])
        outputs.extend([weight_new, mom_new, sec_new])
        if index < 6:
            outputs.append(weight_new.astype(LOW))
    return tuple(outputs)


def solution(mesh):
    placed = (
        P(("dp", "fsdp"), None),
        P(("dp", "fsdp"), None),
        P(),
        P("fsdp", None),
        P("fsdp", None),
        P("fsdp", None),
        P(None, "fsdp"),
        P(None, "fsdp"),
        P(None, "fsdp"),
        P("section", "fsdp", None),
        P("section", "fsdp", None),
        P("section", "fsdp", None),
        P("section", "fsdp", None),
        P("section", "fsdp", None),
        P("section", "fsdp", None),
        P("section", "fsdp", None),
        P("section", "fsdp", None),
        P("section", "fsdp", None),
        P("section", "fsdp", None),
        P("section", "fsdp", None),
        P("section", "fsdp", None),
        P("section", None, "fsdp"),
        P("section", None, "fsdp"),
        P("section", None, "fsdp"),
    )
    return jax.shard_map(
        per_device,
        mesh=mesh,
        in_specs=placed,
        out_specs=(
            P(),
            P(),
            P(),
            P("fsdp", None),
            P("fsdp", None),
            P("fsdp", None),
            P("fsdp", None),
            P(None, "fsdp"),
            P(None, "fsdp"),
            P(None, "fsdp"),
            P(None, "fsdp"),
            P("section", "fsdp", None),
            P("section", "fsdp", None),
            P("section", "fsdp", None),
            P("section", "fsdp", None),
            P("section", "fsdp", None),
            P("section", "fsdp", None),
            P("section", "fsdp", None),
            P("section", "fsdp", None),
            P("section", "fsdp", None),
            P("section", "fsdp", None),
            P("section", "fsdp", None),
            P("section", "fsdp", None),
            P("section", "fsdp", None),
            P("section", "fsdp", None),
            P("section", "fsdp", None),
            P("section", "fsdp", None),
            P("section", None, "fsdp"),
            P("section", None, "fsdp"),
            P("section", None, "fsdp"),
        ),
        check_vma=False,
    )
```

```python
import functools
import math

import jax
import jax.numpy as jnp
from jax import lax
from jax.experimental import pallas as pl
from jax.experimental.pallas import tpu as pltpu
from jax.sharding import PartitionSpec as P

D = 768
HEADS = 12
HEAD_DIM = 64
FF = 3072
ROW = 128
MB = 2
STEP_COUNT = 10
SHARE = 4


EPS = 1e-05
MTP_WEIGHT = 0.3
CLIP = 0.01
BETA1 = 0.9
BETA2 = 0.95
ADAM_EPS = 1e-08
LOW = jnp.bfloat16
WIDE = jnp.float32

MESH = pl.DeviceIdType.MESH

def weights_kernel(planes, replicas, units, rows, *refs):
    n = len(rows)
    own, full = refs[:n], refs[n:2*n]
    send, recv, local = refs[2*n:]
    z = lax.axis_index("fsdp")
    i = lax.axis_index("dp")
    half = replicas // 2
    low, top = i % 2, i // half
    q = top * 2 + low
    xn = i + 1 - 2 * low
    yn = (i + half) % replicas
    qx = top * 2 + 1 - low
    qy = (1 - top) * 2 + low
    barrier = pltpu.get_barrier_semaphore()
    for step in range(1, planes):
        pl.semaphore_signal(barrier, inc=1, device_id={"fsdp": (z + step) % planes}, device_id_type=MESH)
    pl.semaphore_signal(barrier, inc=1, device_id={"dp": xn}, device_id_type=MESH)
    pl.semaphore_signal(barrier, inc=1, device_id={"dp": yn}, device_id_type=MESH)
    pl.semaphore_wait(barrier, planes + 1)
    keep = []
    for m in range(n):
        c = pltpu.make_async_copy(own[m], full[m].at[pl.ds(pl.multiple_of(z * rows[m], 16), rows[m]), :], local.at[m])
        c.start()
        keep.append(c)
    per = 3 * (planes - 1) + (planes - 1)
    def cp(src, dst, k, dev):
        return pltpu.make_async_remote_copy(src_ref=src, dst_ref=dst, send_sem=send.at[k], recv_sem=recv.at[k], device_id=dev, device_id_type=MESH)
    def block(m, plane, quarter, cols):
        r = rows[m] // 4
        return full[m].at[pl.ds(pl.multiple_of(plane * rows[m] + quarter * r, 16), r), pl.ds(cols[0], cols[1])]
    first, second, third = [], [], []
    for u, (m, cols, order) in enumerate(units):
        r = rows[m] // 4
        group = []
        for step in range(1, planes):
            src = own[m].at[pl.ds(pl.multiple_of(q * r, 16), r), pl.ds(cols[0], cols[1])]
            c = cp(src, block(m, z, q, cols), u * per + step - 1, {"fsdp": (z + step) % planes})
            c.start()
            group.append(c)
        first.append(group)
    def phase2(u):
        m, cols, order = units[u]
        base = u * per + planes - 1
        group = []
        for step in range(1, planes):
            first[u][step - 1].wait_recv()
            b = block(m, (z + planes - step) % planes, q, cols)
            c = cp(b, b, base + step - 1, {"dp": xn if order == 0 else yn})
            c.start()
            group.append(c)
        second.append(group)
    def phase3(u):
        m, cols, order = units[u]
        base = u * per + 2 * (planes - 1)
        group = []
        for step in range(1, planes):
            second[u][step - 1].wait_recv()
            for w, quarter in enumerate((q, qx if order == 0 else qy)):
                b = block(m, (z + planes - step) % planes, quarter, cols)
                c = cp(b, b, base + 2 * (step - 1) + w, {"dp": yn if order == 0 else xn})
                c.start()
                group.append(c)
        third.append(group)
    total = len(units)
    for u in range(total):
        phase2(u)
        if u >= 1:
            phase3(u - 1)
    phase3(total - 1)
    for u in range(total):
        for c in third[u]:
            c.wait_recv()
    for u in range(total):
        for c in first[u] + second[u] + third[u]:
            c.wait_send()
    for c in keep:
        c.wait()

def gather_weights(planes, replicas, shards):
    rows = [w.shape[0] for w in shards]
    if any(r % (SHARE * 16) for r in rows):
        return [lax.all_gather(w, "fsdp", axis=0, tiled=True) for w in shards]
    units = []
    for m, w in enumerate(shards):
        width = w.shape[1]
        parts = 4 if width > 4096 else 2
        step = width // parts
        for p in range(parts):
            units.append((m, (p * step, step), p % 2))
    copies = len(units) * 4 * (planes - 1)
    return pl.pallas_call(
        functools.partial(weights_kernel, planes, replicas, units, rows),
        out_shape=[jax.ShapeDtypeStruct((planes * w.shape[0], w.shape[1]), w.dtype) for w in shards],
        in_specs=[pl.BlockSpec(memory_space=pl.ANY)] * len(shards),
        out_specs=[pl.BlockSpec(memory_space=pl.ANY)] * len(shards),
        scratch_shapes=[pltpu.SemaphoreType.DMA((copies,)), pltpu.SemaphoreType.DMA((copies,)), pltpu.SemaphoreType.DMA((len(shards),))],
        compiler_params=pltpu.CompilerParams(collective_id=1, has_side_effects=True),
        name="gather_weights",
    )(*shards)


def norm_fwd(values, scale_gain):
    inverse = lax.rsqrt(jnp.mean(values * values, axis=-1, keepdims=True) + EPS)
    return values * inverse * scale_gain


def norm_back(values, scale_gain, upstream):
    _, pullback = jax.vjp(norm_fwd, values, scale_gain)
    return pullback(upstream)


def rope_tables(row_count, head_width):
    half_width = head_width // 2
    position = jnp.arange(row_count, dtype=jnp.float32)[:, None]
    frequency = 10000.0 ** (-jnp.arange(half_width, dtype=jnp.float32) / half_width)
    angles = position * frequency[None, :]
    return (jnp.cos(angles), jnp.sin(angles))


def rotate(values, cosine, sine_table):
    half_width = values.shape[-1] // 2
    first, second = (values[..., :half_width], values[..., half_width:])
    return jnp.concatenate(
        [first * cosine - second * sine_table, second * cosine + first * sine_table], axis=-1
    )


def contract_rows(left, right):
    return lax.dot_general(
        left, right, (((0,), (0,)), ((), ())), preferred_element_type=jnp.float32
    )


def contract_cols(left, right):
    return lax.dot_general(
        left, right, (((1,), (1,)), ((), ())), preferred_element_type=jnp.float32
    )


def swiglu(gate_up):
    return jax.nn.silu(gate_up[:, :FF]) * gate_up[:, FF:]


def shift(block, axis, distance):
    count = lax.axis_size(axis)
    return lax.ppermute(block, axis, [(i, (i + distance) % count) for i in range(count)])


def swap(block, axis, mask):
    count = lax.axis_size(axis)
    return lax.ppermute(block, axis, [(i, i ^ mask) for i in range(count)])


def pick(array, index, axis=0):
    return lax.dynamic_index_in_dim(array, index, axis, keepdims=False)


def layer_fwd(inputs, weights):
    w_qkv, w_out, w_gateup, w_down, attn_gain, ffn_gain = weights
    normed = norm_fwd(inputs, attn_gain).astype(LOW)
    packed = jnp.dot(normed, w_qkv, preferred_element_type=WIDE)
    split = packed.reshape(MB, ROW, 3, HEADS, HEAD_DIM).transpose(2, 0, 3, 1, 4)
    split = split.reshape(3, MB * HEADS, ROW, HEAD_DIM)
    cosine, sine_table = rope_tables(ROW, HEAD_DIM)
    queries = rotate(split[0], cosine, sine_table).astype(LOW)
    keys_rot = rotate(split[1], cosine, sine_table).astype(LOW)
    values_low = split[2].astype(LOW)
    scores = jnp.einsum(
        "hqd,hkd->hqk", queries, keys_rot, preferred_element_type=WIDE
    ) * HEAD_DIM ** (-0.5)
    position = jnp.arange(ROW)
    causal = position[:, None] >= position[None, :]
    scores = jnp.where(causal[None], scores, -1e30)
    shifted = jnp.exp(scores - jnp.max(scores, axis=-1, keepdims=True))
    probs = shifted / jnp.sum(shifted, axis=-1, keepdims=True)
    probs_low = probs.astype(LOW)
    mixed = jnp.einsum("hqk,hkd->hqd", probs_low, values_low, preferred_element_type=WIDE)
    mixed = mixed.reshape(MB, HEADS, ROW, HEAD_DIM).transpose(0, 2, 1, 3)
    mixed_low = mixed.reshape(MB * ROW, D).astype(LOW)
    after_attn = inputs + jnp.dot(mixed_low, w_out, preferred_element_type=WIDE)
    normed_ffn = norm_fwd(after_attn, ffn_gain).astype(LOW)
    gate_up = jnp.dot(normed_ffn, w_gateup, preferred_element_type=WIDE)
    hidden = swiglu(gate_up).astype(LOW)
    output = after_attn + jnp.dot(hidden, w_down, preferred_element_type=WIDE)
    saved = (
        normed,
        queries,
        keys_rot,
        values_low,
        probs,
        probs_low,
        mixed_low,
        after_attn,
        normed_ffn,
        gate_up,
        hidden,
    )
    return (output, saved)


def layer_back(inputs, weights, saved, upstream):
    w_qkv, w_out, w_gateup, w_down, attn_gain, ffn_gain = weights
    (
        normed,
        queries,
        keys_rot,
        values_low,
        probs,
        probs_low,
        mixed_low,
        after_attn,
        normed_ffn,
        gate_up,
        hidden,
    ) = saved
    upstream_low = upstream.astype(LOW)
    grad_hidden = contract_cols(upstream_low, w_down)
    _, pullback = jax.vjp(swiglu, gate_up)
    grad_gu = pullback(grad_hidden)[0].astype(LOW)
    grad_nffn = contract_cols(grad_gu, w_gateup)
    back_ffn, grad_ffn_gain = norm_back(after_attn, ffn_gain, grad_nffn)
    grad_after = upstream + back_ffn
    after_low = grad_after.astype(LOW)
    grad_mixed = contract_cols(after_low, w_out).astype(LOW)
    grad_mixed = grad_mixed.reshape(MB, ROW, HEADS, HEAD_DIM).transpose(0, 2, 1, 3)
    grad_mixed = grad_mixed.reshape(MB * HEADS, ROW, HEAD_DIM)
    grad_probs = jnp.einsum("hqd,hkd->hqk", grad_mixed, values_low, preferred_element_type=WIDE)
    grad_values = jnp.einsum("hqk,hqd->hkd", probs_low, grad_mixed, preferred_element_type=WIDE)
    grad_scores = probs * (grad_probs - jnp.sum(probs * grad_probs, axis=-1, keepdims=True))
    grad_scores = grad_scores.astype(LOW)
    scale_attn = HEAD_DIM ** (-0.5)
    grad_query = (
        jnp.einsum("hqk,hkd->hqd", grad_scores, keys_rot, preferred_element_type=WIDE)
        * scale_attn
    )
    grad_key = (
        jnp.einsum("hqk,hqd->hkd", grad_scores, queries, preferred_element_type=WIDE)
        * scale_attn
    )
    cosine, sine_table = rope_tables(ROW, HEAD_DIM)
    grad_query = rotate(grad_query, cosine, -sine_table)
    grad_key = rotate(grad_key, cosine, -sine_table)
    grad_packed = jnp.stack([grad_query, grad_key, grad_values]).astype(LOW)
    grad_packed = grad_packed.reshape(3, MB, HEADS, ROW, HEAD_DIM).transpose(1, 3, 0, 2, 4)
    grad_packed = grad_packed.reshape(MB * ROW, 3 * D)
    grad_normed = contract_cols(grad_packed, w_qkv)
    back_attn, grad_attn_gain = norm_back(inputs, attn_gain, grad_normed)
    grad_inputs = grad_after + back_attn
    return (
        grad_inputs,
        (grad_packed, after_low, grad_gu, upstream_low),
        (grad_attn_gain, grad_ffn_gain),
    )


def plane_rank():
    return lax.axis_index("dp")


def quarter(block, index):
    width = block.shape[1] // SHARE
    return lax.dynamic_slice_in_dim(block, index * width, width, 1)


def sub_quarter(block, planes, index):
    rows, width = block.shape
    split = block.reshape(rows, planes, SHARE, width // planes // SHARE)
    return lax.dynamic_index_in_dim(split, index, 2, keepdims=False).reshape(rows, -1)


def spread(make):
    rank = plane_rank()
    own = make(rank)
    rows = own.shape[0]
    full = lax.dynamic_update_slice(jnp.zeros((SHARE * rows, own.shape[1]), LOW), own, (0, 0))
    for mask in range(1, SHARE):
        piece = swap(make(rank ^ mask), "dp", mask)
        full = lax.dynamic_update_slice(full, piece, (mask * rows, 0))
    return full


def in_order(pieces, rank, axis):
    low = rank % 2 == 0
    top = rank // 2 == 0
    pairs = []
    for k in (0, 2):
        pairs.append(
            (jnp.where(low, pieces[k], pieces[k + 1]), jnp.where(low, pieces[k + 1], pieces[k]))
        )
    lower = [jnp.where(top, pairs[0][j], pairs[1][j]) for j in range(2)]
    upper = [jnp.where(top, pairs[1][j], pairs[0][j]) for j in range(2)]
    return jnp.concatenate(lower + upper, axis=axis)


def relative_blocks():
    s = lax.axis_index("section")
    i = lax.axis_index("dp")
    x, y = i % 2, i // 2
    blocks = []
    for es in (0, 1):
        for kind in (0, 1):
            for e1 in (0, 1):
                for e2 in (0, 1):
                    a, b = (x, y) if kind == 0 else (y, x)
                    within = ((a + e1) % 2) * 2 + (b + e2) % 2
                    blocks.append(((s + es) % 2) * 8 + kind * 4 + within)
    return jnp.stack(blocks).astype(jnp.int32)


TOKENS = 256


def head_piece(vocab):
    return -(-vocab // 256) * 16


def table_block(vocab, base, h_ref):
    inside = lax.broadcasted_iota(jnp.int32, h_ref.shape, 0) + base < vocab
    return jnp.where(inside, h_ref[...], 0.0).astype(LOW)


def head_scores(vocab, base, table, rows):
    logits = contract_cols(table, rows)
    index = lax.broadcasted_iota(jnp.int32, logits.shape, 0) + base
    return jnp.where(index < vocab, logits, -1e30), index


def head_stats_kernel(vocab, h_ref, rows_ref, target_ref, out):
    step = pl.program_id(0)
    base = step * h_ref.shape[0]
    table = table_block(vocab, base, h_ref)

    @pl.when(step == 0)
    def _():
        out[0:1, :] = jnp.full((1, out.shape[1]), -1e30, WIDE)
        out[1:3, :] = jnp.zeros((2, out.shape[1]), WIDE)

    for c in range(rows_ref.shape[0] // TOKENS):
        span = slice(c * TOKENS, (c + 1) * TOKENS)
        logits, index = head_scores(vocab, base, table, rows_ref[span, :])
        before = out[0:1, span]
        peak = jnp.maximum(before, jnp.max(logits, axis=0, keepdims=True))
        summed = jnp.sum(jnp.exp(logits - peak), axis=0, keepdims=True)
        picked = jnp.sum(jnp.where(index == target_ref[:, span], logits, 0.0), axis=0, keepdims=True)
        out[0:1, span] = peak
        out[1:2, span] = out[1:2, span] * jnp.exp(before - peak) + summed
        out[2:3, span] += picked


def once(shape):
    return pl.BlockSpec(shape, lambda g, *_: (0,) * len(shape), pipeline_mode=pl.Buffered(1))


def head_stats(head, rows, targets):
    vocab, count = head.shape[0], rows.shape[0]
    piece = head_piece(vocab)
    return pl.pallas_call(
        functools.partial(head_stats_kernel, vocab),
        grid=(-(-vocab // piece),),
        in_specs=[pl.BlockSpec((piece, D), lambda g: (g, 0)), once((count, D)), once((1, count))],
        out_specs=pl.BlockSpec((8, count), lambda g: (0, 0)),
        out_shape=jax.ShapeDtypeStruct((8, count), WIDE),
        compiler_params=pltpu.CompilerParams(vmem_limit_bytes=50 << 20),
        cost_estimate=pl.CostEstimate(
            flops=2 * vocab * count * D, bytes_accessed=vocab * D * 4, transcendentals=vocab * count
        ),
        name="head_stats",
    )(head, rows, targets)


def head_grads_kernel(vocab, order, h_ref, rows_ref, target_ref, lse_ref, factor_ref, g_ref, c_ref, flipped, delta):
    step = pl.program_id(0)
    base = order[step] * h_ref.shape[0]
    table = table_block(vocab, base, h_ref)
    flipped[...] = table.astype(WIDE).T.astype(LOW)

    @pl.when(step == 0)
    def _():
        c_ref[...] = jnp.zeros(c_ref.shape, WIDE)

    for c in range(rows_ref.shape[0] // TOKENS):
        span = slice(c * TOKENS, (c + 1) * TOKENS)
        logits, index = head_scores(vocab, base, table, rows_ref[span, :])
        onehot = (index == target_ref[:, span]).astype(WIDE)
        delta[:, span] = (
            (jnp.exp(logits - lse_ref[:, span]) - onehot) * factor_ref[:, span]
        ).astype(LOW)
    g_ref[...] = jnp.dot(delta[...], rows_ref[...], preferred_element_type=WIDE).astype(LOW)
    for c in range(rows_ref.shape[0] // TOKENS):
        span = slice(c * TOKENS, (c + 1) * TOKENS)
        c_ref[:, span] += jnp.dot(flipped[...], delta[:, span], preferred_element_type=WIDE)


def head_grads(head, rows, targets, lse, factor):
    vocab, count = head.shape[0], rows.shape[0]
    piece = head_piece(vocab)
    return pl.pallas_call(
        functools.partial(head_grads_kernel, vocab),
        grid_spec=pltpu.PrefetchScalarGridSpec(
            num_scalar_prefetch=1,
            grid=(16,),
            in_specs=[
                pl.BlockSpec((piece, D), lambda g, order: (order[g], 0)),
                once((count, D)),
                once((1, count)),
                once((1, count)),
                once((1, count)),
            ],
            out_specs=[
                pl.BlockSpec((piece, D), lambda g, order: (g, 0)),
                pl.BlockSpec((D, count), lambda g, order: (0, 0)),
            ],
            scratch_shapes=[pltpu.VMEM((D, piece), LOW), pltpu.VMEM((piece, count), LOW)],
        ),
        out_shape=[
            jax.ShapeDtypeStruct((16 * piece, D), LOW),
            jax.ShapeDtypeStruct((D, count), WIDE),
        ],
        compiler_params=pltpu.CompilerParams(vmem_limit_bytes=56 << 20),
        cost_estimate=pl.CostEstimate(
            flops=6 * vocab * count * D, bytes_accessed=vocab * D * 8, transcendentals=vocab * count
        ),
        name="head_grads",
    )(relative_blocks(), head, rows, targets, lse, factor)


def head_pass(rows_low, targets, weights_tok, head, vocab_start, token_total):
    planes = lax.axis_size("fsdp")
    gathered = jnp.concatenate(
        [rows_low] + [shift(rows_low, "fsdp", step) for step in range(1, planes)], axis=0
    )
    local = targets - vocab_start
    local = jnp.where((local >= 0) & (local < head.shape[0]), local, -1)[None, :]
    stats = head_stats(head, gathered, local)[:3].reshape(3, planes, -1)
    parts = [stats] + [
        jnp.roll(shift(stats, "fsdp", step), step, axis=1) for step in range(1, planes)
    ]
    parts = jnp.stack(parts)
    peak = jnp.max(parts[:, 0], axis=0)
    total = jnp.sum(parts[:, 1] * jnp.exp(parts[:, 0] - peak[None]), axis=0)
    lse = (peak + jnp.log(total)).reshape(-1)
    loss_part = jnp.sum((lse - jnp.sum(parts[:, 2], axis=0).reshape(-1)) * weights_tok)
    factor = weights_tok / token_total
    grad_head, partial = head_grads(head, gathered, local, lse[None, :], factor[None, :])
    partial = partial.T.reshape(planes, -1, D)
    grad_rows = partial[0]
    for step in range(1, planes):
        grad_rows = grad_rows + shift(partial[step].astype(LOW), "fsdp", planes - step).astype(WIDE)
    middle = grad_head.shape[0] // 2
    return (loss_part, grad_head[:middle], grad_head[middle:], grad_rows)


def add_low(one, other):
    return (one.astype(WIDE) + other.astype(WIDE)).astype(LOW)


def keep_half(block, mask):
    half = block.shape[0] // 2
    return add_low(block[:half], swap(block[half:], "dp", mask))


def adam_update(weight, grad, first_mom, second_mom, rate, decay):
    mom_new = BETA1 * first_mom + (1.0 - BETA1) * grad
    sec_new = BETA2 * second_mom + (1.0 - BETA2) * grad * grad
    mom_hat = mom_new / (1.0 - BETA1**STEP_COUNT)
    sec_hat = sec_new / (1.0 - BETA2**STEP_COUNT)
    weight_new = weight - rate * (mom_hat / (jnp.sqrt(sec_hat) + ADAM_EPS) + decay * weight)
    return (weight_new, mom_new, sec_new)


def exchange_kernel(planes, rows_ref, pa, pb, *refs):
    n = (len(refs) - 7) // 2
    parts, rows_all, head, slots = refs[:n], refs[n], refs[n + 1], refs[n + 2 : 2 * n + 2]
    send, recv, core_send, core_recv, local = refs[2 * n + 2 :]
    s = lax.axis_index("section")
    i = lax.axis_index("dp")
    z = lax.axis_index("fsdp")
    x, y = i % 2, i // 2
    xn, yn, diag = i + 1 - 2 * x, (i + 2) % 4, 3 - i
    to_x, to_y, to_core = {"dp": xn}, {"dp": yn}, {"section": 1 - s}
    barrier = pltpu.get_barrier_semaphore()
    for device in [to_x, to_y, to_core] + [{"fsdp": (z + k) % planes} for k in range(1, planes)]:
        pl.semaphore_signal(barrier, inc=1, device_id=device, device_id_type=MESH)
    pl.semaphore_wait(barrier, planes + 2)
    counts = [0, 0]
    sent = []

    def put(src, dst, device):
        over = device is to_core
        k = counts[over]
        counts[over] += 1
        copy = pltpu.make_async_remote_copy(
            src_ref=src,
            dst_ref=dst,
            send_sem=(core_send if over else send).at[k],
            recv_sem=(core_recv if over else recv).at[k],
            device_id=device,
            device_id_type=MESH,
        )
        copy.start()
        sent.append(copy)
        return copy

    def take(*copies):
        for copy in copies:
            copy.wait_recv()

    piece = pa.shape[0]
    side = 4 * piece

    def head_a(xx, yy, count):
        return head.at[pl.ds(pl.multiple_of(s * 2 * side + xx * 2 * piece + yy * piece, 16), count)]

    def head_b(xx, yy, count):
        return head.at[
            pl.ds(pl.multiple_of(s * 2 * side + side + yy * 2 * piece + xx * piece, 16), count)
        ]

    own = []
    for k, (src, dst) in enumerate(
        [(rows_ref, rows_all.at[s, i, z]), (pa, head_a(x, y, piece)), (pb, head_b(x, y, piece))]
    ):
        copy = pltpu.make_async_copy(src, dst, local.at[k])
        copy.start()
        own.append(copy)
    near = [put(rows_ref, rows_all.at[s, i, z], {"fsdp": (z + k) % planes}) for k in range(1, planes)]
    head1 = [put(pa, head_a(x, y, piece), to_y), put(pb, head_b(x, y, piece), to_x)]
    reduce = []
    for m in range(n):
        height = slots[m].shape[1]
        for k in range(1, planes):
            target = (z + k) % planes
            block = parts[m].at[pl.ds(pl.multiple_of(target * height, 16), height)]
            reduce.append(put(block, slots[m].at[k - 1], {"fsdp": target}))
    for copy in own:
        copy.wait()
    take(*near)
    mid = planes // 2
    early, late = pl.ds(0, mid), pl.ds(mid, planes - mid)
    a1 = put(rows_all.at[s, i, early], rows_all.at[s, i, early], to_x)
    b1 = put(rows_all.at[s, i, late], rows_all.at[s, i, late], to_y)
    core = [put(rows_all.at[s, i], rows_all.at[s, i], to_core)]
    take(*head1)
    block = head_a(x, 0, 2 * piece)
    ha = put(block, block, to_x)
    block = head_b(0, y, 2 * piece)
    hb = put(block, block, to_y)
    take(a1, b1)
    second = []
    for who, span, device in ((i, early, to_y), (xn, early, to_y), (i, late, to_x), (yn, late, to_x)):
        block = rows_all.at[s, who, span]
        second.append(put(block, block, device))
    for who, span in ((xn, early), (yn, late)):
        block = rows_all.at[s, who, span]
        core.append(put(block, block, to_core))
    take(ha, hb)
    block = head.at[pl.ds(pl.multiple_of(s * 2 * side, 16), 2 * side)]
    core.append(put(block, block, to_core))
    take(*second)
    for who, span in ((yn, early), (diag, early), (xn, late), (diag, late)):
        block = rows_all.at[s, who, span]
        core.append(put(block, block, to_core))
    take(*reduce)
    take(*core)
    for copy in sent:
        copy.wait_send()


def exchange(planes, row_grads, pieces, parts):
    piece, vocab = pieces[0].shape
    shape = jax.ShapeDtypeStruct
    outs = [shape((2, 4, planes) + row_grads.shape, LOW), shape((16 * piece, vocab), LOW)]
    outs += [shape((planes - 1, p.shape[0] // planes, p.shape[1]), LOW) for p in parts]
    copies = (planes - 1) * (1 + len(parts)) + 2 + 2 + 2 + 4
    anywhere = pl.BlockSpec(memory_space=pl.ANY)
    result = pl.pallas_call(
        functools.partial(exchange_kernel, planes),
        out_shape=outs,
        in_specs=[anywhere] * (3 + len(parts)),
        out_specs=[anywhere] * len(outs),
        scratch_shapes=[pltpu.SemaphoreType.DMA((copies,))] * 2
        + [pltpu.SemaphoreType.DMA((8,))] * 2
        + [pltpu.SemaphoreType.DMA((3,))],
        compiler_params=pltpu.CompilerParams(collective_id=2, has_side_effects=True),
        name="exchange",
    )(row_grads, *pieces, *parts)
    return result[0], result[1], result[2:]


VOCAB_BLOCK = 400


def chunk_of(lists):
    return 32 if lists <= 64 else 16


def start_chunks(lists, length, step, steps, starts, rows_hbm, buffer, sem):
    chunk = chunk_of(lists)

    def one(k, carry):
        at = jnp.minimum(starts[k * steps + step] // 16 * 16, length - chunk)
        src = rows_hbm.at[pl.ds(pl.multiple_of(k * length + at, 16), chunk)]
        pltpu.make_async_copy(src, buffer.at[pl.ds(pl.multiple_of(k * chunk, 16), chunk)], sem).start()
        return carry

    lax.fori_loop(0, lists, one, 0)


def block_grad(
    lists, length, steps, step, starts, passes, bases, rows_hbm, ids_ref, near_ref, buffers, hot, wide_hot, grad, sems
):
    chunk = chunk_of(lists)
    slot = step % 2
    spare = buffers.at[2]

    @pl.when(step == 0)
    def _():
        start_chunks(lists, length, 0, steps, starts, rows_hbm, buffers.at[0], sems.at[0])

    @pl.when(step + 1 < steps)
    def _():
        start_chunks(lists, length, step + 1, steps, starts, rows_hbm, buffers.at[1 - slot], sems.at[1 - slot])

    pltpu.make_async_copy(buffers.at[slot], buffers.at[slot], sems.at[slot]).wait()
    lanes = lax.broadcasted_iota(jnp.int32, (chunk, VOCAB_BLOCK), 1) + bases[step]
    within = lax.broadcasted_iota(jnp.int32, (chunk, VOCAB_BLOCK), 0)

    def mark(shifted):
        def one(k, carry):
            begin = starts[k * steps + step] // 16 * 16 + shifted
            at = jnp.minimum(begin, length - chunk)
            ids = ids_ref[pl.ds(pl.multiple_of(k * length + at, 16), chunk), :]
            same = (ids == lanes) & (within >= begin - at)
            hot[pl.ds(pl.multiple_of(k * chunk, 16), chunk), :] = same.astype(WIDE).astype(LOW)
            return carry

        lax.fori_loop(0, lists, one, 0)

    down = lax.broadcasted_iota(jnp.int32, (VOCAB_BLOCK, lists * chunk), 0) + bases[step]
    wide_hot[...] = (down == near_ref[0]).astype(WIDE).astype(LOW)
    grad[...] = jnp.dot(wide_hot[...], buffers[slot], preferred_element_type=WIDE)

    def more(p, carry):
        mark(p * chunk)

        def one(k, inner):
            begin = starts[k * steps + step] // 16 * 16 + p * chunk
            at = jnp.minimum(begin, length - chunk)
            src = rows_hbm.at[pl.ds(pl.multiple_of(k * length + at, 16), chunk)]
            pltpu.make_async_copy(
                src, spare.at[pl.ds(pl.multiple_of(k * chunk, 16), chunk)], sems.at[2]
            ).start()
            return inner

        lax.fori_loop(0, lists, one, 0)
        pltpu.make_async_copy(spare, spare, sems.at[2]).wait()
        grad[...] += contract_rows(hot[...], spare[...])
        return carry

    lax.fori_loop(1, passes[step], more, 0)


def table_square_kernel(lists, length, steps, starts, passes, bases, rows_hbm, ids_ref, near_ref, out, buffers, hot, wide_hot, grad, sems):
    step = pl.program_id(0)
    block_grad(lists, length, steps, step, starts, passes, bases, rows_hbm, ids_ref, near_ref, buffers, hot, wide_hot, grad, sems)
    part = jnp.sum((grad[...] * grad[...]).reshape(-1, 8, D), axis=0)
    part = jnp.where(passes[step] > 0, part, 0.0)

    @pl.when(step == 0)
    def _():
        out[...] = part

    @pl.when(step > 0)
    def _():
        out[...] += part


def table_adam_kernel(
    lists, length, steps, rate, decay, starts, passes, bases, clip, rows_hbm, ids_ref, near_ref, w, m, v, w_new, m_new, v_new, low, buffers, hot, wide_hot, grad, sems
):
    step = pl.program_id(0)
    block_grad(lists, length, steps, step, starts, passes, bases, rows_hbm, ids_ref, near_ref, buffers, hot, wide_hot, grad, sems)
    weight, mom, sec = adam_update(w[...], grad[...] * clip[0], m[...], v[...], rate, decay)
    w_new[...] = weight
    m_new[...] = mom
    v_new[...] = sec
    low[...] = weight.astype(LOW)


def table_scratch(lists):
    chunk = chunk_of(lists)
    return [
        pltpu.VMEM((3, lists * chunk, D), LOW),
        pltpu.VMEM((lists * chunk, VOCAB_BLOCK), LOW),
        pltpu.VMEM((VOCAB_BLOCK, lists * chunk), LOW),
        pltpu.VMEM((VOCAB_BLOCK, D), WIDE),
        pltpu.SemaphoreType.DMA((3,)),
    ]


def chunk_scalars(ids_sorted, bases):
    chunk = chunk_of(ids_sorted.shape[0])
    edges = bases[None, :, None]
    starts = jnp.sum((ids_sorted[:, None, :] < edges).astype(jnp.int32), axis=-1)
    ends = jnp.sum((ids_sorted[:, None, :] < edges + VOCAB_BLOCK).astype(jnp.int32), axis=-1)
    passes = jnp.max((ends - starts // 16 * 16 + chunk - 1) // chunk, axis=0)
    length = ids_sorted.shape[1]
    begin = (starts // 16 * 16).T[:, :, None]
    at = jnp.minimum(begin, length - chunk) + jnp.arange(chunk)[None, None, :]
    near = jnp.sum(
        jnp.where(
            at[..., None] == jnp.arange(length)[None, None, None, :], ids_sorted[None, :, None, :], 0
        ),
        axis=-1,
    )
    near = jnp.where(at >= begin, near, -(1 << 30)).reshape(near.shape[0], 1, -1)
    return starts.reshape(-1), jnp.maximum(passes, 1), near


def table_square(ids_sorted, ids_column, rows_flat, rank, ranks, vocab_rows):
    lists, length = ids_sorted.shape
    total = vocab_rows // VOCAB_BLOCK
    steps = -(-total // ranks)
    blocks = rank + ranks * jnp.arange(steps, dtype=jnp.int32)
    bases = blocks * VOCAB_BLOCK
    starts, passes, near = chunk_scalars(ids_sorted, bases)
    passes = jnp.where(blocks < total, passes, 0)
    out = pl.pallas_call(
        functools.partial(table_square_kernel, lists, length, steps),
        grid_spec=pltpu.PrefetchScalarGridSpec(
            num_scalar_prefetch=3,
            grid=(steps,),
            in_specs=[
                pl.BlockSpec(memory_space=pl.ANY),
                pl.BlockSpec(
                    (lists * length, 1), lambda g, *_: (0, 0), pipeline_mode=pl.Buffered(1)
                ),
                pl.BlockSpec((1, 1, near.shape[2]), lambda g, *_: (g, 0, 0)),
            ],
            out_specs=pl.BlockSpec((8, D), lambda g, *_: (0, 0)),
            scratch_shapes=table_scratch(lists),
        ),
        out_shape=jax.ShapeDtypeStruct((8, D), WIDE),
        compiler_params=pltpu.CompilerParams(vmem_limit_bytes=56 << 20),
        name="table_square",
    )(starts, passes, bases, rows_flat, ids_column, near)
    return jnp.sum(out)


def table_adam(ids_sorted, ids_column, rows_flat, clip_scale, table, mom, sec, rate, decay):
    lists, length = ids_sorted.shape
    vocab_rows = table.shape[0]
    steps = vocab_rows // VOCAB_BLOCK
    bases = jnp.arange(steps, dtype=jnp.int32) * VOCAB_BLOCK
    starts, passes, near = chunk_scalars(ids_sorted, bases)
    block = pl.BlockSpec((VOCAB_BLOCK, D), lambda g, *_: (g, 0))
    wide = jax.ShapeDtypeStruct(table.shape, WIDE)
    return pl.pallas_call(
        functools.partial(table_adam_kernel, lists, length, steps, rate, decay),
        grid_spec=pltpu.PrefetchScalarGridSpec(
            num_scalar_prefetch=4,
            grid=(steps,),
            in_specs=[
                pl.BlockSpec(memory_space=pl.ANY),
                pl.BlockSpec(
                    (lists * length, 1), lambda g, *_: (0, 0), pipeline_mode=pl.Buffered(1)
                ),
                pl.BlockSpec((1, 1, near.shape[2]), lambda g, *_: (g, 0, 0)),
                block,
                block,
                block,
            ],
            out_specs=[block] * 4,
            scratch_shapes=table_scratch(lists),
        ),
        out_shape=[wide, wide, wide, jax.ShapeDtypeStruct(table.shape, LOW)],
        compiler_params=pltpu.CompilerParams(vmem_limit_bytes=60 << 20),
        cost_estimate=pl.CostEstimate(
            flops=steps * 2 * VOCAB_BLOCK * lists * chunk_of(lists) * D,
            bytes_accessed=table.size * 26,
            transcendentals=table.size,
        ),
        name="table_adam",
    )(starts, passes, bases, clip_scale.reshape(1), rows_flat, ids_column, near, table, mom, sec)


HEAD_BLOCK = 512


def head_adam_kernel(rate, decay, clip, grad, w, m, v, w_new, m_new, v_new, low):
    scaled = grad[...].astype(WIDE) * clip[0]
    weight, mom, sec = adam_update(w[...], scaled, m[...], v[...], rate, decay)
    w_new[...] = weight
    m_new[...] = mom
    v_new[...] = sec
    low[...] = weight.astype(LOW)


def head_adam(grad, clip_scale, head, mom, sec, rate, decay):
    vocab = head.shape[1]
    block = pl.BlockSpec((HEAD_BLOCK, D), lambda g, *_: (g, 0))
    wide = jax.ShapeDtypeStruct((vocab, D), WIDE)
    results = pl.pallas_call(
        functools.partial(head_adam_kernel, rate, decay),
        grid_spec=pltpu.PrefetchScalarGridSpec(
            num_scalar_prefetch=1,
            grid=(-(-vocab // HEAD_BLOCK),),
            in_specs=[block] * 4,
            out_specs=[block] * 4,
        ),
        out_shape=[wide, wide, wide, jax.ShapeDtypeStruct((vocab, D), LOW)],
        compiler_params=pltpu.CompilerParams(vmem_limit_bytes=56 << 20),
        cost_estimate=pl.CostEstimate(
            flops=head.size * 20, bytes_accessed=head.size * 28, transcendentals=head.size
        ),
        name="head_adam",
    )(clip_scale.reshape(1), grad, head.T, mom.T, sec.T)
    return [item.T for item in results]


def small_gather_kernel(axes, sizes, *refs):
    n = (len(refs) - 2) // 2
    blocks, outs, send, recv = refs[:n], refs[n : 2 * n], refs[2 * n], refs[2 * n + 1]
    mine = [lax.axis_index(axis) for axis in axes]
    slot = 0
    for index, size in zip(mine, sizes):
        slot = slot * size + index
    offsets = [()]
    for size in sizes:
        offsets = [o + (k,) for o in offsets for k in range(size)]
    peers = [
        {axis: (index + k) % size for axis, index, size, k in zip(axes, mine, sizes, offset)}
        for offset in offsets[1:]
    ]
    barrier = pltpu.get_barrier_semaphore()
    for peer in peers:
        pl.semaphore_signal(barrier, inc=1, device_id=peer, device_id_type=MESH)
    pl.semaphore_wait(barrier, len(peers))
    copies = []
    for m in range(n):
        for k, peer in enumerate(peers):
            copy = pltpu.make_async_remote_copy(
                src_ref=blocks[m],
                dst_ref=outs[m].at[slot],
                send_sem=send.at[m * len(peers) + k],
                recv_sem=recv.at[m * len(peers) + k],
                device_id=peer,
                device_id_type=MESH,
            )
            copy.start()
            copies.append(copy)
        outs[m][slot] = blocks[m][...]
    for copy in copies:
        copy.wait()


def small_gather(blocks, axes, identity):
    sizes = [lax.axis_size(axis) for axis in axes]
    count = math.prod(sizes)
    copies = (count - 1) * len(blocks)
    whole = pl.BlockSpec(memory_space=pltpu.VMEM)
    return pl.pallas_call(
        functools.partial(small_gather_kernel, axes, sizes),
        out_shape=[jax.ShapeDtypeStruct((count,) + b.shape, b.dtype) for b in blocks],
        in_specs=[whole] * len(blocks),
        out_specs=[whole] * len(blocks),
        scratch_shapes=[pltpu.SemaphoreType.DMA((copies,))] * 2,
        compiler_params=pltpu.CompilerParams(collective_id=identity, has_side_effects=True),
        name=f"small_gather_{identity}",
    )(*blocks)


def per_device(
    token_ids,
    next_ids,
    seq_lengths,
    embedding,
    embedding_mom,
    embedding_sec,
    head_table,
    head_mom,
    head_sec,
    w_qkv,
    qkv_mom,
    qkv_sec,
    w_out,
    out_mom,
    out_sec,
    w_gateup,
    gateup_mom,
    gateup_sec,
    w_down,
    down_mom,
    down_sec,
    gains,
    gains_mom,
    gains_sec,
):
    planes = lax.axis_size("fsdp")
    replicas = lax.axis_size("dp")
    first = lax.axis_index("section") == 0
    first_f = first.astype(WIDE)
    me = lax.axis_index("fsdp")
    token_total = jnp.sum(seq_lengths).astype(WIDE)
    tokens = MB * ROW

    my_ids = jnp.stack([token_ids.reshape(-1), next_ids.reshape(-1)])
    ids_all, gains_all = small_gather([my_ids, gains[0]], ("dp", "fsdp"), 3)
    ids_all = ids_all.reshape(replicas, planes, 2, tokens)
    gains_full = gains_all[:planes].transpose(1, 0, 2).reshape(3, D)
    gains_full = lax.optimization_barrier(gains_full.astype(LOW)).astype(WIDE)
    group_ids = pick(ids_all, lax.axis_index("dp"))
    rel_ids = jnp.stack([pick(group_ids, (me - step) % planes) for step in range(planes)])
    my_kind = jnp.where(first, rel_ids[:, 0], rel_ids[:, 1])
    vocab_rows = embedding.shape[0]
    vocab_start = me * vocab_rows
    local = my_kind - vocab_start
    inside = (local >= 0) & (local < vocab_rows)
    found = jnp.take(embedding, jnp.clip(local, 0, vocab_rows - 1), axis=0)
    found = lax.optimization_barrier(jnp.where(inside[..., None], found, 0.0).astype(LOW))
    looked = found[0].astype(WIDE)
    for step in range(1, planes):
        looked = looked + shift(found[step], "fsdp", planes - step).astype(WIDE)
    next_embed = swap(looked.astype(LOW), "section", 1).astype(WIDE)

    lists = ids_all.transpose(2, 0, 1, 3).reshape(-1, tokens) - vocab_start
    place = jnp.arange(tokens)
    before = (lists[:, None, :] < lists[:, :, None]) | (
        (lists[:, None, :] == lists[:, :, None]) & (place[None, None, :] < place[None, :, None])
    )
    ranks = jnp.sum(before.astype(jnp.int32), axis=-1)
    sorted_ids = jnp.sum(
        jnp.where(ranks[:, None, :] == place[None, :, None], lists[:, None, :], 0), axis=-1
    )
    own_list = (
        lax.axis_index("section") * replicas + lax.axis_index("dp")
    ) * planes + me
    arrange = (pick(ranks, own_list)[None, :] == place[:, None]).astype(LOW)

    full = gather_weights(
        planes,
        replicas,
        [w_qkv[0].astype(LOW), w_out[0].astype(LOW), w_gateup[0].astype(LOW), w_down[0].astype(LOW)],
    )
    layer_weights = (full[0], full[1], full[2], full[3], gains_full[0], gains_full[1])
    head_gain = gains_full[2]

    first_out, _ = layer_fwd(looked, layer_weights)
    middle = swap(first_out.astype(LOW), "section", 1).astype(WIDE)
    layer_in = jnp.where(first, looked, middle)
    layer_out, saved = layer_fwd(layer_in, layer_weights)
    final_state = norm_fwd(layer_out, head_gain)
    arrived = swap(final_state.astype(LOW), "section", 1).astype(WIDE)
    merged_in = jnp.where(first, arrived + next_embed, layer_out)
    head_in = norm_fwd(merged_in, head_gain)

    lengths = seq_lengths.reshape(replicas, planes, MB)[lax.axis_index("dp")]
    lengths = jnp.stack([pick(lengths, (me - step) % planes) for step in range(planes)])
    targets_main = rel_ids[:, 1].reshape(planes, MB, ROW)
    shifted = jnp.concatenate([targets_main[..., 1:], targets_main[..., :1]], axis=-1)
    targets = jnp.where(first, shifted, targets_main)
    limit = lengths - first.astype(jnp.int32)
    positions = jnp.arange(ROW, dtype=jnp.int32)
    weights_tok = (positions < limit[..., None]).astype(WIDE) * jnp.where(first, MTP_WEIGHT, 1.0)
    left = [saved[0], saved[6], saved[8]]
    left_all = spread(
        lambda index: jnp.concatenate(left + [sub_quarter(saved[10], planes, index)], axis=1)
    )
    loss_part, mine, theirs, grad_in = head_pass(
        head_in.astype(LOW),
        targets.reshape(-1),
        weights_tok.reshape(-1),
        head_table.T,
        vocab_start,
        token_total,
    )
    sorted_ids, loss_part = lax.optimization_barrier((sorted_ids, loss_part))
    merged_grad, mtp_gain = norm_back(merged_in, head_gain, grad_in)
    merged_low = merged_grad.astype(LOW)
    sent = swap(merged_low, "section", 1).astype(WIDE)
    top_grad, top_gain = norm_back(layer_out, head_gain, grad_in + sent)
    head_gain_grad = jnp.where(first, mtp_gain, top_gain)
    half = add_low(mine, swap(theirs, "section", 1))
    top_grad, left_all = lax.optimization_barrier((top_grad, left_all))
    below, _, _ = layer_back(layer_in, layer_weights, saved, top_grad)
    below, half = lax.optimization_barrier((below.astype(LOW), half))
    side = half.shape[0] // 2
    piece_a, piece_b = keep_half(half[:side], 1), keep_half(half[side:], 2)
    upstream = jnp.where(first, swap(below, "section", 1).astype(WIDE), top_grad)
    grad_inputs, right, gain_parts = layer_back(layer_in, layer_weights, saved, upstream)
    grad_inputs, piece_a, piece_b = lax.optimization_barrier((grad_inputs, piece_a, piece_b))
    piece_a, piece_b = keep_half(piece_a, 2), keep_half(piece_b, 1)

    grad_packed, after_low, grad_gu, upstream_low = right
    tops = spread(lambda index: upstream_low)
    early = spread(lambda index: quarter(grad_gu, index))
    late = spread(
        lambda index: jnp.concatenate([quarter(after_low, index), quarter(grad_packed, index)], axis=1)
    )
    cut = D // SHARE
    parts = [
        contract_rows(left_all[:, 2 * D : 3 * D], early),
        contract_rows(left_all[:, 3 * D :], tops),
        contract_rows(left_all[:, :D], late[:, cut:]),
        contract_rows(left_all[:, D : 2 * D], late[:, :cut]),
    ]
    parts = [part.astype(LOW) for part in parts]
    gains_grad = jnp.stack([gain_parts[0], gain_parts[1], head_gain_grad])
    gains_grad = jnp.sum(small_gather([gains_grad], ("dp", "fsdp"), 4)[0], axis=0)
    gains_grad = lax.dynamic_slice_in_dim(gains_grad, me * (D // planes), D // planes, 1)

    row_grads = jnp.where(first, grad_inputs.astype(LOW), sent.astype(LOW))
    row_grads = jnp.dot(arrange, row_grads, preferred_element_type=WIDE).astype(LOW)
    rows_all, grad_head, slots = exchange(planes, row_grads, (piece_a, piece_b), parts)
    rows_flat = rows_all.reshape(-1, D)
    ids_column = sorted_ids.reshape(-1, 1)

    def square(item):
        wide = item.astype(WIDE)
        return jnp.sum(wide * wide)

    shards = []
    for part, slot in zip(parts, slots):
        mine = pick(part.reshape((planes,) + slot.shape[1:]), me).astype(WIDE)
        shards.append((mine + jnp.sum(slot.astype(WIDE), axis=0)).astype(LOW))
    group = lax.axis_index("section") * replicas + lax.axis_index("dp")
    squares = table_square(sorted_ids, ids_column, rows_flat, group, 2 * replicas, vocab_rows)
    for item in shards + [piece_a, piece_b]:
        squares = squares + square(item)
    squares = squares + square(gains_grad) / replicas
    totals = jnp.stack([squares, loss_part / planes])[:, None] * jnp.ones((1, 128), WIDE)
    totals = jnp.sum(small_gather([totals], ("section", "dp", "fsdp"), 5)[0], axis=0)[:, 0]
    grad_norm = jnp.sqrt(totals[0])
    loss_total = totals[1]
    clip_scale = CLIP / jnp.maximum(grad_norm, CLIP)

    shards, clip_scale = lax.optimization_barrier((shards, clip_scale))
    widths = [0, 2 * D, 3 * D, 3 * D + 3 * cut, 4 * D]
    packed = jnp.concatenate(shards, axis=1)
    rank = plane_rank()
    others = [packed] + [swap(packed, "dp", mask) for mask in range(1, SHARE)]
    layer_grads = [
        in_order([other[:, lo:hi] for other in others], rank, 0 if index == 1 else 1).astype(WIDE)
        for index, (lo, hi) in enumerate(zip(widths[:-1], widths[1:]))
    ]
    params = (w_qkv[0], w_out[0], w_gateup[0], w_down[0], gains[0])
    grads_all = (
        layer_grads[2],
        layer_grads[3],
        layer_grads[0],
        layer_grads[1],
        gains_grad,
    )
    moments = (
        (qkv_mom[0], qkv_sec[0]),
        (out_mom[0], out_sec[0]),
        (gateup_mom[0], gateup_sec[0]),
        (down_mom[0], down_sec[0]),
        (gains_mom[0], gains_sec[0]),
    )
    rates = (0.03, 0.12, 0.03, 0.03, 0.6)
    decays = (0.1, 0.1, 0.1, 0.1, 0.0)
    outputs = [loss_total, token_total, grad_norm]
    outputs += table_adam(
        sorted_ids,
        ids_column,
        rows_flat,
        clip_scale,
        embedding,
        embedding_mom,
        embedding_sec,
        0.6,
        0.1,
    )
    outputs += head_adam(grad_head, clip_scale, head_table, head_mom, head_sec, 0.03, 0.1)
    for index in range(5):
        weight_new, mom_new, sec_new = adam_update(
            params[index],
            grads_all[index] * clip_scale,
            moments[index][0],
            moments[index][1],
            rates[index],
            decays[index],
        )
        outputs.extend([weight_new[None], mom_new[None], sec_new[None]])
        if index < 4:
            outputs.append(weight_new.astype(LOW)[None])
    return tuple(outputs)


def solution(mesh):
    placed = (
        P(("dp", "fsdp"), None),
        P(("dp", "fsdp"), None),
        P(),
        P("fsdp", None),
        P("fsdp", None),
        P("fsdp", None),
        P(None, "fsdp"),
        P(None, "fsdp"),
        P(None, "fsdp"),
        P("section", "fsdp", None),
        P("section", "fsdp", None),
        P("section", "fsdp", None),
        P("section", "fsdp", None),
        P("section", "fsdp", None),
        P("section", "fsdp", None),
        P("section", "fsdp", None),
        P("section", "fsdp", None),
        P("section", "fsdp", None),
        P("section", "fsdp", None),
        P("section", "fsdp", None),
        P("section", "fsdp", None),
        P("section", None, "fsdp"),
        P("section", None, "fsdp"),
        P("section", None, "fsdp"),
    )
    return jax.shard_map(
        per_device,
        mesh=mesh,
        in_specs=placed,
        out_specs=(
            P(),
            P(),
            P(),
            P("fsdp", None),
            P("fsdp", None),
            P("fsdp", None),
            P("fsdp", None),
            P(None, "fsdp"),
            P(None, "fsdp"),
            P(None, "fsdp"),
            P(None, "fsdp"),
            P("section", "fsdp", None),
            P("section", "fsdp", None),
            P("section", "fsdp", None),
            P("section", "fsdp", None),
            P("section", "fsdp", None),
            P("section", "fsdp", None),
            P("section", "fsdp", None),
            P("section", "fsdp", None),
            P("section", "fsdp", None),
            P("section", "fsdp", None),
            P("section", "fsdp", None),
            P("section", "fsdp", None),
            P("section", "fsdp", None),
            P("section", "fsdp", None),
            P("section", "fsdp", None),
            P("section", "fsdp", None),
            P("section", None, "fsdp"),
            P("section", None, "fsdp"),
            P("section", None, "fsdp"),
        ),
        check_vma=False,
    )
```

```python
import functools
import math

import jax
import jax.numpy as jnp
from jax import lax
from jax.experimental import pallas as pl
from jax.experimental.pallas import tpu as pltpu
from jax.sharding import PartitionSpec as P

D = 768
HEADS = 12
HEAD_DIM = 64
FF = 3072
ROW = 128
MB = 2
STEP_COUNT = 10
SHARE = 4


EPS = 1e-05
MTP_WEIGHT = 0.3
CLIP = 0.01
BETA1 = 0.9
BETA2 = 0.95
ADAM_EPS = 1e-08
LOW = jnp.bfloat16
WIDE = jnp.float32

AHEAD = 2
MESH = pl.DeviceIdType.MESH

def weights_kernel(planes, units, rows, *refs):
    n = len(rows)
    own, full = refs[:n], refs[n : 2 * n]
    send, recv, local = refs[2 * n :]
    z = lax.axis_index("fsdp")
    i = lax.axis_index("dp")
    x, y = i % 2, i // 2
    q = i
    xn, yn = i + 1 - 2 * x, (i + 2) % 4
    near, far = z + 1 - 2 * (z % 2), planes - 1 - z
    beyond = planes - 1 - near
    to_x, to_y, to_near, to_far = {"dp": xn}, {"dp": yn}, {"fsdp": near}, {"fsdp": far}
    barrier = pltpu.get_barrier_semaphore()
    for device in (to_x, to_y, to_near, to_far):
        pl.semaphore_signal(barrier, inc=1, device_id=device, device_id_type=MESH)
    pl.semaphore_wait(barrier, 4)
    keep = []
    for m in range(n):
        c = pltpu.make_async_copy(
            own[m], full[m].at[pl.ds(pl.multiple_of(z * rows[m], 16), rows[m]), :], local.at[m]
        )
        c.start()
        keep.append(c)
    started = []

    def put(src, dst, k, device):
        copy = pltpu.make_async_remote_copy(
            src_ref=src,
            dst_ref=dst,
            send_sem=send.at[k],
            recv_sem=recv.at[k],
            device_id=device,
            device_id_type=MESH,
        )
        copy.start()
        started.append(copy)
        return copy

    def block(u, plane, part):
        m, cols, _ = units[u]
        r = rows[m] // 4
        return full[m].at[pl.ds(pl.multiple_of(plane * rows[m] + part * r, 16), r), pl.ds(*cols)]

    sources = (near, far, beyond)
    zs, seconds, thirds = {}, {}, []
    total = len(units)

    def first(u):
        m, cols, _ = units[u]
        r = rows[m] // 4
        src = own[m].at[pl.ds(pl.multiple_of(q * r, 16), r), pl.ds(*cols)]
        zs[u, 0] = put(src, block(u, z, q), 12 * u, to_near)
        zs[u, 1] = put(src, block(u, z, q), 12 * u + 1, to_far)

    def onward(u):
        zs[u, 1].wait_recv()
        zs[u, 2] = put(block(u, far, q), block(u, far, q), 12 * u + 2, to_near)

    def second(u, j):
        if j != 1:
            zs[u, j].wait_recv()
        b = block(u, sources[j], q)
        seconds[u, j] = put(b, b, 12 * u + 3 + j, to_y if units[u][2] else to_x)

    def third(u, j):
        seconds[u, j].wait_recv()
        order = units[u][2]
        for w, part in enumerate((q, yn if order else xn)):
            b = block(u, sources[j], part)
            thirds.append(put(b, b, 12 * u + 6 + 2 * j + w, to_x if order else to_y))

    pairs = [(u, u + 1) for u in range(0, total, 2)]
    for ahead in range(AHEAD):
        for u in pairs[ahead]:
            first(u)
    for t in range(len(pairs) + 2):
        if t < len(pairs):
            for u in pairs[t]:
                onward(u)
            if t + AHEAD < len(pairs):
                for u in pairs[t + AHEAD]:
                    first(u)
            for j in (0, 1):
                for u in pairs[t]:
                    second(u, j)
        if 1 <= t <= len(pairs):
            for u in pairs[t - 1]:
                second(u, 2)
            for j in (0, 1):
                for u in pairs[t - 1]:
                    third(u, j)
        if t >= 2:
            for u in pairs[t - 2]:
                third(u, 2)
    for c in thirds:
        c.wait_recv()
    for c in started:
        c.wait_send()
    for c in keep:
        c.wait()


def gather_weights(planes, replicas, shards):
    rows = [w.shape[0] for w in shards]
    if planes != 4 or replicas != 4 or any(r % (SHARE * 16) for r in rows):
        return [lax.all_gather(w, "fsdp", axis=0, tiled=True) for w in shards]
    units = []
    for m, w in enumerate(shards):
        width = w.shape[1]
        parts = 4 if width > 4096 else 2
        step = width // parts
        for p in range(parts):
            units.append((m, (p * step, step), p % 2))
    copies = len(units) * 12
    return pl.pallas_call(
        functools.partial(weights_kernel, planes, units, rows),
        out_shape=[jax.ShapeDtypeStruct((planes * w.shape[0], w.shape[1]), w.dtype) for w in shards],
        in_specs=[pl.BlockSpec(memory_space=pltpu.VMEM)] * len(shards),
        out_specs=[pl.BlockSpec(memory_space=pl.ANY)] * len(shards),
        scratch_shapes=[pltpu.SemaphoreType.DMA((copies,)), pltpu.SemaphoreType.DMA((copies,)), pltpu.SemaphoreType.DMA((len(shards),))],
        compiler_params=pltpu.CompilerParams(collective_id=1, has_side_effects=True),
        name="gather_weights",
    )(*shards)


def norm_fwd(values, scale_gain):
    inverse = lax.rsqrt(jnp.mean(values * values, axis=-1, keepdims=True) + EPS)
    return values * inverse * scale_gain


def norm_back(values, scale_gain, upstream):
    _, pullback = jax.vjp(norm_fwd, values, scale_gain)
    return pullback(upstream)


def rope_tables(row_count, head_width):
    half_width = head_width // 2
    position = jnp.arange(row_count, dtype=jnp.float32)[:, None]
    frequency = 10000.0 ** (-jnp.arange(half_width, dtype=jnp.float32) / half_width)
    angles = position * frequency[None, :]
    return (jnp.cos(angles), jnp.sin(angles))


def rotate(values, cosine, sine_table):
    half_width = values.shape[-1] // 2
    first, second = (values[..., :half_width], values[..., half_width:])
    return jnp.concatenate(
        [first * cosine - second * sine_table, second * cosine + first * sine_table], axis=-1
    )


def contract_rows(left, right):
    return lax.dot_general(
        left, right, (((0,), (0,)), ((), ())), preferred_element_type=jnp.float32
    )


def contract_cols(left, right):
    return lax.dot_general(
        left, right, (((1,), (1,)), ((), ())), preferred_element_type=jnp.float32
    )


def swiglu(gate_up):
    return jax.nn.silu(gate_up[:, :FF]) * gate_up[:, FF:]


def shift(block, axis, distance):
    count = lax.axis_size(axis)
    return lax.ppermute(block, axis, [(i, (i + distance) % count) for i in range(count)])


def swap(block, axis, mask):
    count = lax.axis_size(axis)
    return lax.ppermute(block, axis, [(i, i ^ mask) for i in range(count)])


def pick(array, index, axis=0):
    return lax.dynamic_index_in_dim(array, index, axis, keepdims=False)


def layer_fwd(inputs, weights):
    w_qkv, w_out, w_gateup, w_down, attn_gain, ffn_gain = weights
    normed = norm_fwd(inputs, attn_gain).astype(LOW)
    packed = jnp.dot(normed, w_qkv, preferred_element_type=WIDE)
    split = packed.reshape(MB, ROW, 3, HEADS, HEAD_DIM).transpose(2, 0, 3, 1, 4)
    split = split.reshape(3, MB * HEADS, ROW, HEAD_DIM)
    cosine, sine_table = rope_tables(ROW, HEAD_DIM)
    queries = rotate(split[0], cosine, sine_table).astype(LOW)
    keys_rot = rotate(split[1], cosine, sine_table).astype(LOW)
    values_low = split[2].astype(LOW)
    scores = jnp.einsum(
        "hqd,hkd->hqk", queries, keys_rot, preferred_element_type=WIDE
    ) * HEAD_DIM ** (-0.5)
    position = jnp.arange(ROW)
    causal = position[:, None] >= position[None, :]
    scores = jnp.where(causal[None], scores, -1e30)
    shifted = jnp.exp(scores - jnp.max(scores, axis=-1, keepdims=True))
    probs = shifted / jnp.sum(shifted, axis=-1, keepdims=True)
    probs_low = probs.astype(LOW)
    mixed = jnp.einsum("hqk,hkd->hqd", probs_low, values_low, preferred_element_type=WIDE)
    mixed = mixed.reshape(MB, HEADS, ROW, HEAD_DIM).transpose(0, 2, 1, 3)
    mixed_low = mixed.reshape(MB * ROW, D).astype(LOW)
    after_attn = inputs + jnp.dot(mixed_low, w_out, preferred_element_type=WIDE)
    normed_ffn = norm_fwd(after_attn, ffn_gain).astype(LOW)
    gate_up = jnp.dot(normed_ffn, w_gateup, preferred_element_type=WIDE)
    hidden = swiglu(gate_up).astype(LOW)
    output = after_attn + jnp.dot(hidden, w_down, preferred_element_type=WIDE)
    saved = (
        normed,
        queries,
        keys_rot,
        values_low,
        probs,
        probs_low,
        mixed_low,
        after_attn,
        normed_ffn,
        gate_up,
        hidden,
    )
    return (output, saved)


def layer_back(inputs, weights, saved, upstream):
    w_qkv, w_out, w_gateup, w_down, attn_gain, ffn_gain = weights
    (
        normed,
        queries,
        keys_rot,
        values_low,
        probs,
        probs_low,
        mixed_low,
        after_attn,
        normed_ffn,
        gate_up,
        hidden,
    ) = saved
    upstream_low = upstream.astype(LOW)
    grad_hidden = contract_cols(upstream_low, w_down)
    _, pullback = jax.vjp(swiglu, gate_up)
    grad_gu = pullback(grad_hidden)[0].astype(LOW)
    grad_nffn = contract_cols(grad_gu, w_gateup)
    back_ffn, grad_ffn_gain = norm_back(after_attn, ffn_gain, grad_nffn)
    grad_after = upstream + back_ffn
    after_low = grad_after.astype(LOW)
    grad_mixed = contract_cols(after_low, w_out).astype(LOW)
    grad_mixed = grad_mixed.reshape(MB, ROW, HEADS, HEAD_DIM).transpose(0, 2, 1, 3)
    grad_mixed = grad_mixed.reshape(MB * HEADS, ROW, HEAD_DIM)
    grad_probs = jnp.einsum("hqd,hkd->hqk", grad_mixed, values_low, preferred_element_type=WIDE)
    grad_values = jnp.einsum("hqk,hqd->hkd", probs_low, grad_mixed, preferred_element_type=WIDE)
    grad_scores = probs * (grad_probs - jnp.sum(probs * grad_probs, axis=-1, keepdims=True))
    grad_scores = grad_scores.astype(LOW)
    scale_attn = HEAD_DIM ** (-0.5)
    grad_query = (
        jnp.einsum("hqk,hkd->hqd", grad_scores, keys_rot, preferred_element_type=WIDE)
        * scale_attn
    )
    grad_key = (
        jnp.einsum("hqk,hqd->hkd", grad_scores, queries, preferred_element_type=WIDE)
        * scale_attn
    )
    cosine, sine_table = rope_tables(ROW, HEAD_DIM)
    grad_query = rotate(grad_query, cosine, -sine_table)
    grad_key = rotate(grad_key, cosine, -sine_table)
    grad_packed = jnp.stack([grad_query, grad_key, grad_values]).astype(LOW)
    grad_packed = grad_packed.reshape(3, MB, HEADS, ROW, HEAD_DIM).transpose(1, 3, 0, 2, 4)
    grad_packed = grad_packed.reshape(MB * ROW, 3 * D)
    grad_normed = contract_cols(grad_packed, w_qkv)
    back_attn, grad_attn_gain = norm_back(inputs, attn_gain, grad_normed)
    grad_inputs = grad_after + back_attn
    return (
        grad_inputs,
        (grad_packed, after_low, grad_gu, upstream_low),
        (grad_attn_gain, grad_ffn_gain),
    )


def plane_rank():
    return lax.axis_index("dp")


def quarter(block, index):
    width = block.shape[1] // SHARE
    return lax.dynamic_slice_in_dim(block, index * width, width, 1)


def sub_quarter(block, planes, index):
    rows, width = block.shape
    split = block.reshape(rows, planes, SHARE, width // planes // SHARE)
    return lax.dynamic_index_in_dim(split, index, 2, keepdims=False).reshape(rows, -1)


def spread(make):
    rank = plane_rank()
    own = make(rank)
    rows = own.shape[0]
    full = lax.dynamic_update_slice(jnp.zeros((SHARE * rows, own.shape[1]), LOW), own, (0, 0))
    for mask in range(1, SHARE):
        piece = swap(make(rank ^ mask), "dp", mask)
        full = lax.dynamic_update_slice(full, piece, (mask * rows, 0))
    return full


def in_order(pieces, rank, axis):
    low = rank % 2 == 0
    top = rank // 2 == 0
    pairs = []
    for k in (0, 2):
        pairs.append(
            (jnp.where(low, pieces[k], pieces[k + 1]), jnp.where(low, pieces[k + 1], pieces[k]))
        )
    lower = [jnp.where(top, pairs[0][j], pairs[1][j]) for j in range(2)]
    upper = [jnp.where(top, pairs[1][j], pairs[0][j]) for j in range(2)]
    return jnp.concatenate(lower + upper, axis=axis)


def relative_blocks():
    s = lax.axis_index("section")
    i = lax.axis_index("dp")
    x, y = i % 2, i // 2
    blocks = []
    for es in (0, 1):
        for kind in (0, 1):
            for e1 in (0, 1):
                for e2 in (0, 1):
                    a, b = (x, y) if kind == 0 else (y, x)
                    within = ((a + e1) % 2) * 2 + (b + e2) % 2
                    blocks.append(((s + es) % 2) * 8 + kind * 4 + within)
    return jnp.stack(blocks).astype(jnp.int32)


TOKENS = 256


def head_piece(vocab):
    return -(-vocab // 256) * 16


def table_block(vocab, base, h_ref):
    inside = lax.broadcasted_iota(jnp.int32, h_ref.shape, 0) + base < vocab
    return jnp.where(inside, h_ref[...], 0.0).astype(LOW)


def head_scores(vocab, base, table, rows):
    logits = contract_cols(table, rows)
    index = lax.broadcasted_iota(jnp.int32, logits.shape, 0) + base
    return jnp.where(index < vocab, logits, -1e30), index


def head_stats_kernel(vocab, h_ref, rows_ref, target_ref, out):
    step = pl.program_id(0)
    base = step * h_ref.shape[0]
    table = table_block(vocab, base, h_ref)

    @pl.when(step == 0)
    def _():
        out[0:1, :] = jnp.full((1, out.shape[1]), -1e30, WIDE)
        out[1:3, :] = jnp.zeros((2, out.shape[1]), WIDE)

    for c in range(rows_ref.shape[0] // TOKENS):
        span = slice(c * TOKENS, (c + 1) * TOKENS)
        logits, index = head_scores(vocab, base, table, rows_ref[span, :])
        before = out[0:1, span]
        peak = jnp.maximum(before, jnp.max(logits, axis=0, keepdims=True))
        summed = jnp.sum(jnp.exp(logits - peak), axis=0, keepdims=True)
        picked = jnp.sum(jnp.where(index == target_ref[:, span], logits, 0.0), axis=0, keepdims=True)
        out[0:1, span] = peak
        out[1:2, span] = out[1:2, span] * jnp.exp(before - peak) + summed
        out[2:3, span] += picked


def once(shape):
    return pl.BlockSpec(shape, lambda g, *_: (0,) * len(shape), pipeline_mode=pl.Buffered(1))


def head_stats(head, rows, targets):
    vocab, count = head.shape[0], rows.shape[0]
    piece = head_piece(vocab)
    return pl.pallas_call(
        functools.partial(head_stats_kernel, vocab),
        grid=(-(-vocab // piece),),
        in_specs=[pl.BlockSpec((piece, D), lambda g: (g, 0)), once((count, D)), once((1, count))],
        out_specs=pl.BlockSpec((8, count), lambda g: (0, 0)),
        out_shape=jax.ShapeDtypeStruct((8, count), WIDE),
        compiler_params=pltpu.CompilerParams(vmem_limit_bytes=50 << 20),
        cost_estimate=pl.CostEstimate(
            flops=2 * vocab * count * D, bytes_accessed=vocab * D * 4, transcendentals=vocab * count
        ),
        name="head_stats",
    )(head, rows, targets)


def head_grads_kernel(vocab, order, h_ref, rows_ref, target_ref, lse_ref, factor_ref, g_ref, c_ref, flipped, delta):
    step = pl.program_id(0)
    base = order[step] * h_ref.shape[0]
    table = table_block(vocab, base, h_ref)
    flipped[...] = table.astype(WIDE).T.astype(LOW)

    @pl.when(step == 0)
    def _():
        c_ref[...] = jnp.zeros(c_ref.shape, WIDE)

    for c in range(rows_ref.shape[0] // TOKENS):
        span = slice(c * TOKENS, (c + 1) * TOKENS)
        logits, index = head_scores(vocab, base, table, rows_ref[span, :])
        onehot = (index == target_ref[:, span]).astype(WIDE)
        delta[:, span] = (
            (jnp.exp(logits - lse_ref[:, span]) - onehot) * factor_ref[:, span]
        ).astype(LOW)
    g_ref[...] = jnp.dot(delta[...], rows_ref[...], preferred_element_type=WIDE).astype(LOW)
    for c in range(rows_ref.shape[0] // TOKENS):
        span = slice(c * TOKENS, (c + 1) * TOKENS)
        c_ref[:, span] += jnp.dot(flipped[...], delta[:, span], preferred_element_type=WIDE)


def head_grads(head, rows, targets, lse, factor):
    vocab, count = head.shape[0], rows.shape[0]
    piece = head_piece(vocab)
    return pl.pallas_call(
        functools.partial(head_grads_kernel, vocab),
        grid_spec=pltpu.PrefetchScalarGridSpec(
            num_scalar_prefetch=1,
            grid=(16,),
            in_specs=[
                pl.BlockSpec((piece, D), lambda g, order: (order[g], 0)),
                once((count, D)),
                once((1, count)),
                once((1, count)),
                once((1, count)),
            ],
            out_specs=[
                pl.BlockSpec((piece, D), lambda g, order: (g, 0)),
                pl.BlockSpec((D, count), lambda g, order: (0, 0)),
            ],
            scratch_shapes=[pltpu.VMEM((D, piece), LOW), pltpu.VMEM((piece, count), LOW)],
        ),
        out_shape=[
            jax.ShapeDtypeStruct((16 * piece, D), LOW),
            jax.ShapeDtypeStruct((D, count), WIDE),
        ],
        compiler_params=pltpu.CompilerParams(vmem_limit_bytes=56 << 20),
        cost_estimate=pl.CostEstimate(
            flops=6 * vocab * count * D, bytes_accessed=vocab * D * 8, transcendentals=vocab * count
        ),
        name="head_grads",
    )(relative_blocks(), head, rows, targets, lse, factor)


def head_pass(rows_low, targets, weights_tok, head, vocab_start, token_total):
    planes = lax.axis_size("fsdp")
    gathered = jnp.concatenate(
        [rows_low] + [shift(rows_low, "fsdp", step) for step in range(1, planes)], axis=0
    )
    local = targets - vocab_start
    local = jnp.where((local >= 0) & (local < head.shape[0]), local, -1)[None, :]
    stats = head_stats(head, gathered, local)[:3].reshape(3, planes, -1)
    parts = [stats] + [
        jnp.roll(shift(stats, "fsdp", step), step, axis=1) for step in range(1, planes)
    ]
    parts = jnp.stack(parts)
    peak = jnp.max(parts[:, 0], axis=0)
    total = jnp.sum(parts[:, 1] * jnp.exp(parts[:, 0] - peak[None]), axis=0)
    lse = (peak + jnp.log(total)).reshape(-1)
    loss_part = jnp.sum((lse - jnp.sum(parts[:, 2], axis=0).reshape(-1)) * weights_tok)
    factor = weights_tok / token_total
    grad_head, partial = head_grads(head, gathered, local, lse[None, :], factor[None, :])
    partial = partial.T.reshape(planes, -1, D)
    grad_rows = partial[0]
    for step in range(1, planes):
        grad_rows = grad_rows + shift(partial[step].astype(LOW), "fsdp", planes - step).astype(WIDE)
    middle = grad_head.shape[0] // 2
    return (loss_part, grad_head[:middle], grad_head[middle:], grad_rows)


def add_low(one, other):
    return (one.astype(WIDE) + other.astype(WIDE)).astype(LOW)


def keep_half(block, mask):
    half = block.shape[0] // 2
    return add_low(block[:half], swap(block[half:], "dp", mask))


def adam_update(weight, grad, first_mom, second_mom, rate, decay):
    mom_new = BETA1 * first_mom + (1.0 - BETA1) * grad
    sec_new = BETA2 * second_mom + (1.0 - BETA2) * grad * grad
    mom_hat = mom_new / (1.0 - BETA1**STEP_COUNT)
    sec_hat = sec_new / (1.0 - BETA2**STEP_COUNT)
    weight_new = weight - rate * (mom_hat / (jnp.sqrt(sec_hat) + ADAM_EPS) + decay * weight)
    return (weight_new, mom_new, sec_new)


def exchange_kernel(planes, rows_ref, pa, pb, *refs):
    paired = planes == 4
    n = (len(refs) - 7) // (4 if paired else 2)
    parts, rows_all, head, slots = refs[:n], refs[n], refs[n + 1], refs[n + 2 : 2 * n + 2]
    send, recv, core_send, core_recv, local = refs[2 * n + 2 : 2 * n + 7]
    totals, extras = refs[2 * n + 7 : 3 * n + 7], refs[3 * n + 7 :]
    s = lax.axis_index("section")
    i = lax.axis_index("dp")
    z = lax.axis_index("fsdp")
    x, y = i % 2, i // 2
    xn, yn, diag = i + 1 - 2 * x, (i + 2) % 4, 3 - i
    partner = z + 1 - 2 * (z % 2)
    to_x, to_y, to_core = {"dp": xn}, {"dp": yn}, {"section": 1 - s}
    barrier = pltpu.get_barrier_semaphore()
    for device in [to_x, to_y, to_core] + [{"fsdp": (z + k) % planes} for k in range(1, planes)]:
        pl.semaphore_signal(barrier, inc=1, device_id=device, device_id_type=MESH)
    pl.semaphore_wait(barrier, planes + 2)
    counts = [0, 0]
    sent = []

    def put(src, dst, device):
        over = device is to_core
        k = counts[over]
        counts[over] += 1
        copy = pltpu.make_async_remote_copy(
            src_ref=src,
            dst_ref=dst,
            send_sem=(core_send if over else send).at[k],
            recv_sem=(core_recv if over else recv).at[k],
            device_id=device,
            device_id_type=MESH,
        )
        copy.start()
        sent.append(copy)
        return copy

    def take(*copies):
        for copy in copies:
            copy.wait_recv()

    piece = pa.shape[0]
    side = 4 * piece

    def head_a(xx, yy, count):
        return head.at[pl.ds(pl.multiple_of(s * 2 * side + xx * 2 * piece + yy * piece, 16), count)]

    def head_b(xx, yy, count):
        return head.at[
            pl.ds(pl.multiple_of(s * 2 * side + side + yy * 2 * piece + xx * piece, 16), count)
        ]

    own = []
    for k, (src, dst) in enumerate(
        [(rows_ref, rows_all.at[s, i, z]), (pa, head_a(x, y, piece)), (pb, head_b(x, y, piece))]
    ):
        copy = pltpu.make_async_copy(src, dst, local.at[k])
        copy.start()
        own.append(copy)
    reduce = []

    def part_of(m, plane):
        height = slots[m].shape[1]
        return parts[m].at[pl.ds(pl.multiple_of(plane * height, 16), height)]

    fetched, passed = [], []
    if paired:
        for m in range(n):
            copy = pltpu.make_async_copy(part_of(m, planes - 1 - z), totals[m], local.at[3 + m])
            copy.start()
            fetched.append(copy)
    near = [put(rows_ref, rows_all.at[s, i, z], {"fsdp": (z + k) % planes}) for k in range(1, planes)]
    head1 = [put(pa, head_a(x, y, piece), to_y), put(pb, head_b(x, y, piece), to_x)]
    if not paired:
        for m in range(n):
            for k in range(1, planes):
                target = (z + k) % planes
                reduce.append(put(part_of(m, target), slots[m].at[k - 1], {"fsdp": target}))
    for copy in own:
        copy.wait()
    take(*near)
    if paired:
        for m in range(n):
            passed.append(put(part_of(m, planes - 1 - partner), extras[m], {"fsdp": partner}))
    mid = planes // 2
    early, late = pl.ds(0, mid), pl.ds(mid, planes - mid)
    a1 = put(rows_all.at[s, i, early], rows_all.at[s, i, early], to_x)
    b1 = put(rows_all.at[s, i, late], rows_all.at[s, i, late], to_y)
    core = [put(rows_all.at[s, i], rows_all.at[s, i], to_core)]
    if paired:
        for copy in fetched:
            copy.wait()
        for m in range(n):
            passed[m].wait_recv()
            held = totals[m][...].astype(WIDE) + extras[m][...].astype(WIDE)
            totals[m][...] = held.astype(LOW)
            reduce.append(put(totals[m], slots[m].at[1], {"fsdp": planes - 1 - z}))
            reduce.append(put(part_of(m, partner), slots[m].at[0], {"fsdp": partner}))
    take(*head1)
    block = head_a(x, 0, 2 * piece)
    ha = put(block, block, to_x)
    block = head_b(0, y, 2 * piece)
    hb = put(block, block, to_y)
    take(a1, b1)
    second = []
    for who, span, device in ((i, early, to_y), (xn, early, to_y), (i, late, to_x), (yn, late, to_x)):
        block = rows_all.at[s, who, span]
        second.append(put(block, block, device))
    for who, span in ((xn, early), (yn, late)):
        block = rows_all.at[s, who, span]
        core.append(put(block, block, to_core))
    take(ha, hb)
    block = head.at[pl.ds(pl.multiple_of(s * 2 * side, 16), 2 * side)]
    core.append(put(block, block, to_core))
    take(*second)
    for who, span in ((yn, early), (diag, early), (xn, late), (diag, late)):
        block = rows_all.at[s, who, span]
        core.append(put(block, block, to_core))
    take(*reduce)
    take(*core)
    for copy in sent:
        copy.wait_send()


def exchange(planes, row_grads, pieces, parts):
    piece, vocab = pieces[0].shape
    shape = jax.ShapeDtypeStruct
    outs = [shape((2, 4, planes) + row_grads.shape, LOW), shape((16 * piece, vocab), LOW)]
    blocks = [(p.shape[0] // planes, p.shape[1]) for p in parts]
    paired = planes == 4
    outs += [shape((2 if paired else planes - 1,) + b, LOW) for b in blocks]
    copies = (planes - 1) * (1 + len(parts)) + 2 + 2 + 2 + 4
    anywhere = pl.BlockSpec(memory_space=pl.ANY)
    result = pl.pallas_call(
        functools.partial(exchange_kernel, planes),
        out_shape=outs,
        in_specs=[pl.BlockSpec(memory_space=pltpu.VMEM)] * 3 + [anywhere] * len(parts),
        out_specs=[anywhere] * len(outs),
        scratch_shapes=[pltpu.SemaphoreType.DMA((copies,))] * 2
        + [pltpu.SemaphoreType.DMA((8,))] * 2
        + [pltpu.SemaphoreType.DMA((3 + len(parts),))]
        + ([pltpu.VMEM(b, LOW) for b in blocks] * 2 if paired else []),
        compiler_params=pltpu.CompilerParams(
            collective_id=2, has_side_effects=True, vmem_limit_bytes=16 << 20
        ),
        name="exchange",
    )(row_grads, *pieces, *parts)
    return result[0], result[1], result[2:]


VOCAB_BLOCK = 400


def chunk_of(lists):
    return 32 if lists <= 64 else 16


def start_chunks(lists, length, step, steps, starts, rows_hbm, buffer, sem):
    chunk = chunk_of(lists)

    def one(k, carry):
        at = jnp.minimum(starts[k * steps + step] // 16 * 16, length - chunk)
        src = rows_hbm.at[pl.ds(pl.multiple_of(k * length + at, 16), chunk)]
        pltpu.make_async_copy(src, buffer.at[pl.ds(pl.multiple_of(k * chunk, 16), chunk)], sem).start()
        return carry

    lax.fori_loop(0, lists, one, 0)


def block_grad(
    lists, length, steps, step, starts, passes, bases, rows_hbm, ids_ref, near_ref, buffers, hot, wide_hot, grad, sems
):
    chunk = chunk_of(lists)
    slot = step % 2
    spare = buffers.at[2]

    @pl.when(step == 0)
    def _():
        start_chunks(lists, length, 0, steps, starts, rows_hbm, buffers.at[0], sems.at[0])

    @pl.when(step + 1 < steps)
    def _():
        start_chunks(lists, length, step + 1, steps, starts, rows_hbm, buffers.at[1 - slot], sems.at[1 - slot])

    pltpu.make_async_copy(buffers.at[slot], buffers.at[slot], sems.at[slot]).wait()
    lanes = lax.broadcasted_iota(jnp.int32, (chunk, VOCAB_BLOCK), 1) + bases[step]
    within = lax.broadcasted_iota(jnp.int32, (chunk, VOCAB_BLOCK), 0)

    def mark(shifted):
        def one(k, carry):
            begin = starts[k * steps + step] // 16 * 16 + shifted
            at = jnp.minimum(begin, length - chunk)
            ids = ids_ref[pl.ds(pl.multiple_of(k * length + at, 16), chunk), :]
            same = (ids == lanes) & (within >= begin - at)
            hot[pl.ds(pl.multiple_of(k * chunk, 16), chunk), :] = same.astype(WIDE).astype(LOW)
            return carry

        lax.fori_loop(0, lists, one, 0)

    down = lax.broadcasted_iota(jnp.int32, (VOCAB_BLOCK, lists * chunk), 0) + bases[step]
    wide_hot[...] = (down == near_ref[0]).astype(WIDE).astype(LOW)
    grad[...] = jnp.dot(wide_hot[...], buffers[slot], preferred_element_type=WIDE)

    def more(p, carry):
        mark(p * chunk)

        def one(k, inner):
            begin = starts[k * steps + step] // 16 * 16 + p * chunk
            at = jnp.minimum(begin, length - chunk)
            src = rows_hbm.at[pl.ds(pl.multiple_of(k * length + at, 16), chunk)]
            pltpu.make_async_copy(
                src, spare.at[pl.ds(pl.multiple_of(k * chunk, 16), chunk)], sems.at[2]
            ).start()
            return inner

        lax.fori_loop(0, lists, one, 0)
        pltpu.make_async_copy(spare, spare, sems.at[2]).wait()
        grad[...] += contract_rows(hot[...], spare[...])
        return carry

    lax.fori_loop(1, passes[step], more, 0)


def table_square_kernel(lists, length, steps, starts, passes, bases, rows_hbm, ids_ref, near_ref, out, buffers, hot, wide_hot, grad, sems):
    step = pl.program_id(0)
    block_grad(lists, length, steps, step, starts, passes, bases, rows_hbm, ids_ref, near_ref, buffers, hot, wide_hot, grad, sems)
    part = jnp.sum((grad[...] * grad[...]).reshape(-1, 8, D), axis=0)
    part = jnp.where(passes[step] > 0, part, 0.0)

    @pl.when(step == 0)
    def _():
        out[...] = part

    @pl.when(step > 0)
    def _():
        out[...] += part


def table_adam_kernel(
    lists, length, steps, rate, decay, starts, passes, bases, clip, rows_hbm, ids_ref, near_ref, w, m, v, w_new, m_new, v_new, low, buffers, hot, wide_hot, grad, sems
):
    step = pl.program_id(0)
    block_grad(lists, length, steps, step, starts, passes, bases, rows_hbm, ids_ref, near_ref, buffers, hot, wide_hot, grad, sems)
    weight, mom, sec = adam_update(w[...], grad[...] * clip[0], m[...], v[...], rate, decay)
    w_new[...] = weight
    m_new[...] = mom
    v_new[...] = sec
    low[...] = weight.astype(LOW)


def table_scratch(lists):
    chunk = chunk_of(lists)
    return [
        pltpu.VMEM((3, lists * chunk, D), LOW),
        pltpu.VMEM((lists * chunk, VOCAB_BLOCK), LOW),
        pltpu.VMEM((VOCAB_BLOCK, lists * chunk), LOW),
        pltpu.VMEM((VOCAB_BLOCK, D), WIDE),
        pltpu.SemaphoreType.DMA((3,)),
    ]


def chunk_scalars(ids_sorted, bases):
    chunk = chunk_of(ids_sorted.shape[0])
    edges = bases[None, :, None]
    starts = jnp.sum((ids_sorted[:, None, :] < edges).astype(jnp.int32), axis=-1)
    ends = jnp.sum((ids_sorted[:, None, :] < edges + VOCAB_BLOCK).astype(jnp.int32), axis=-1)
    passes = jnp.max((ends - starts // 16 * 16 + chunk - 1) // chunk, axis=0)
    lists, length = ids_sorted.shape
    groups = length // 16
    begin = (starts // 16).T
    at = jnp.minimum(begin, groups - chunk // 16)
    by_group = ids_sorted.reshape(lists, groups, 16).transpose(1, 0, 2).reshape(groups, -1)
    pieces = []
    for k in range(chunk // 16):
        wanted = jnp.repeat(at + k, 16, axis=1)
        found = jnp.zeros(wanted.shape, jnp.int32)
        for g in range(groups):
            found = jnp.where(wanted == g, by_group[g][None], found)
        found = jnp.where(wanted >= jnp.repeat(begin, 16, axis=1), found, -(1 << 30))
        pieces.append(found.reshape(-1, lists, 16))
    near = jnp.stack(pieces, axis=2).reshape(begin.shape[0], 1, -1)
    return starts.reshape(-1), jnp.maximum(passes, 1), near


def table_square(ids_sorted, ids_column, rows_flat, rank, ranks, vocab_rows):
    lists, length = ids_sorted.shape
    total = vocab_rows // VOCAB_BLOCK
    steps = -(-total // ranks)
    blocks = rank + ranks * jnp.arange(steps, dtype=jnp.int32)
    bases = blocks * VOCAB_BLOCK
    starts, passes, near = chunk_scalars(ids_sorted, bases)
    passes = jnp.where(blocks < total, passes, 0)
    out = pl.pallas_call(
        functools.partial(table_square_kernel, lists, length, steps),
        grid_spec=pltpu.PrefetchScalarGridSpec(
            num_scalar_prefetch=3,
            grid=(steps,),
            in_specs=[
                pl.BlockSpec(memory_space=pl.ANY),
                pl.BlockSpec(
                    (lists * length, 1), lambda g, *_: (0, 0), pipeline_mode=pl.Buffered(1)
                ),
                pl.BlockSpec((1, 1, near.shape[2]), lambda g, *_: (g, 0, 0)),
            ],
            out_specs=pl.BlockSpec((8, D), lambda g, *_: (0, 0)),
            scratch_shapes=table_scratch(lists),
        ),
        out_shape=jax.ShapeDtypeStruct((8, D), WIDE),
        compiler_params=pltpu.CompilerParams(vmem_limit_bytes=56 << 20),
        name="table_square",
    )(starts, passes, bases, rows_flat, ids_column, near)
    return jnp.sum(out)


def table_adam(ids_sorted, ids_column, rows_flat, clip_scale, table, mom, sec, rate, decay):
    lists, length = ids_sorted.shape
    vocab_rows = table.shape[0]
    steps = vocab_rows // VOCAB_BLOCK
    bases = jnp.arange(steps, dtype=jnp.int32) * VOCAB_BLOCK
    starts, passes, near = chunk_scalars(ids_sorted, bases)
    block = pl.BlockSpec((VOCAB_BLOCK, D), lambda g, *_: (g, 0))
    wide = jax.ShapeDtypeStruct(table.shape, WIDE)
    return pl.pallas_call(
        functools.partial(table_adam_kernel, lists, length, steps, rate, decay),
        grid_spec=pltpu.PrefetchScalarGridSpec(
            num_scalar_prefetch=4,
            grid=(steps,),
            in_specs=[
                pl.BlockSpec(memory_space=pl.ANY),
                pl.BlockSpec(
                    (lists * length, 1), lambda g, *_: (0, 0), pipeline_mode=pl.Buffered(1)
                ),
                pl.BlockSpec((1, 1, near.shape[2]), lambda g, *_: (g, 0, 0)),
                block,
                block,
                block,
            ],
            out_specs=[block] * 4,
            scratch_shapes=table_scratch(lists),
        ),
        out_shape=[wide, wide, wide, jax.ShapeDtypeStruct(table.shape, LOW)],
        compiler_params=pltpu.CompilerParams(vmem_limit_bytes=60 << 20),
        cost_estimate=pl.CostEstimate(
            flops=steps * 2 * VOCAB_BLOCK * lists * chunk_of(lists) * D,
            bytes_accessed=table.size * 26,
            transcendentals=table.size,
        ),
        name="table_adam",
    )(starts, passes, bases, clip_scale.reshape(1), rows_flat, ids_column, near, table, mom, sec)


HEAD_BLOCK = 512


def head_adam_kernel(rate, decay, clip, grad, w, m, v, w_new, m_new, v_new, low):
    scaled = grad[...].astype(WIDE) * clip[0]
    weight, mom, sec = adam_update(w[...], scaled, m[...], v[...], rate, decay)
    w_new[...] = weight
    m_new[...] = mom
    v_new[...] = sec
    low[...] = weight.astype(LOW)


def head_adam(grad, clip_scale, head, mom, sec, rate, decay):
    vocab = head.shape[1]
    block = pl.BlockSpec((HEAD_BLOCK, D), lambda g, *_: (g, 0))
    wide = jax.ShapeDtypeStruct((vocab, D), WIDE)
    results = pl.pallas_call(
        functools.partial(head_adam_kernel, rate, decay),
        grid_spec=pltpu.PrefetchScalarGridSpec(
            num_scalar_prefetch=1,
            grid=(-(-vocab // HEAD_BLOCK),),
            in_specs=[block] * 4,
            out_specs=[block] * 4,
        ),
        out_shape=[wide, wide, wide, jax.ShapeDtypeStruct((vocab, D), LOW)],
        compiler_params=pltpu.CompilerParams(vmem_limit_bytes=56 << 20),
        cost_estimate=pl.CostEstimate(
            flops=head.size * 20, bytes_accessed=head.size * 28, transcendentals=head.size
        ),
        name="head_adam",
    )(clip_scale.reshape(1), grad, head.T, mom.T, sec.T)
    return [item.T for item in results]


def small_gather_kernel(axes, sizes, *refs):
    n = (len(refs) - 2) // 2
    blocks, outs, send, recv = refs[:n], refs[n : 2 * n], refs[2 * n], refs[2 * n + 1]
    mine = [lax.axis_index(axis) for axis in axes]
    slot = 0
    for index, size in zip(mine, sizes):
        slot = slot * size + index
    offsets = [()]
    for size in sizes:
        offsets = [o + (k,) for o in offsets for k in range(size)]
    peers = [
        {axis: (index + k) % size for axis, index, size, k in zip(axes, mine, sizes, offset)}
        for offset in offsets[1:]
    ]
    barrier = pltpu.get_barrier_semaphore()
    for peer in peers:
        pl.semaphore_signal(barrier, inc=1, device_id=peer, device_id_type=MESH)
    pl.semaphore_wait(barrier, len(peers))
    copies = []
    for m in range(n):
        for k, peer in enumerate(peers):
            copy = pltpu.make_async_remote_copy(
                src_ref=blocks[m],
                dst_ref=outs[m].at[slot],
                send_sem=send.at[m * len(peers) + k],
                recv_sem=recv.at[m * len(peers) + k],
                device_id=peer,
                device_id_type=MESH,
            )
            copy.start()
            copies.append(copy)
        outs[m][slot] = blocks[m][...]
    for copy in copies:
        copy.wait()


def small_gather(blocks, axes, identity):
    sizes = [lax.axis_size(axis) for axis in axes]
    count = math.prod(sizes)
    copies = (count - 1) * len(blocks)
    whole = pl.BlockSpec(memory_space=pltpu.VMEM)
    return pl.pallas_call(
        functools.partial(small_gather_kernel, axes, sizes),
        out_shape=[jax.ShapeDtypeStruct((count,) + b.shape, b.dtype) for b in blocks],
        in_specs=[whole] * len(blocks),
        out_specs=[whole] * len(blocks),
        scratch_shapes=[pltpu.SemaphoreType.DMA((copies,))] * 2,
        compiler_params=pltpu.CompilerParams(collective_id=identity, has_side_effects=True),
        name=f"small_gather_{identity}",
    )(*blocks)


def per_device(
    token_ids,
    next_ids,
    seq_lengths,
    embedding,
    embedding_mom,
    embedding_sec,
    head_table,
    head_mom,
    head_sec,
    w_qkv,
    qkv_mom,
    qkv_sec,
    w_out,
    out_mom,
    out_sec,
    w_gateup,
    gateup_mom,
    gateup_sec,
    w_down,
    down_mom,
    down_sec,
    gains,
    gains_mom,
    gains_sec,
):
    planes = lax.axis_size("fsdp")
    replicas = lax.axis_size("dp")
    first = lax.axis_index("section") == 0
    first_f = first.astype(WIDE)
    me = lax.axis_index("fsdp")
    token_total = jnp.sum(seq_lengths).astype(WIDE)
    tokens = MB * ROW

    my_ids = jnp.stack([token_ids.reshape(-1), next_ids.reshape(-1)])
    ids_all, gains_all = small_gather([my_ids, gains[0]], ("dp", "fsdp"), 3)
    ids_all = ids_all.reshape(replicas, planes, 2, tokens)
    gains_full = gains_all[:planes].transpose(1, 0, 2).reshape(3, D)
    gains_full = lax.optimization_barrier(gains_full.astype(LOW)).astype(WIDE)
    group_ids = pick(ids_all, lax.axis_index("dp"))
    rel_ids = jnp.stack([pick(group_ids, (me - step) % planes) for step in range(planes)])
    my_kind = jnp.where(first, rel_ids[:, 0], rel_ids[:, 1])
    vocab_rows = embedding.shape[0]
    vocab_start = me * vocab_rows
    local = my_kind - vocab_start
    inside = (local >= 0) & (local < vocab_rows)
    found = jnp.take(embedding, jnp.clip(local, 0, vocab_rows - 1), axis=0)
    found = lax.optimization_barrier(jnp.where(inside[..., None], found, 0.0).astype(LOW))
    looked = found[0].astype(WIDE)
    for step in range(1, planes):
        looked = looked + shift(found[step], "fsdp", planes - step).astype(WIDE)
    next_embed = swap(looked.astype(LOW), "section", 1).astype(WIDE)

    lists = ids_all.transpose(2, 0, 1, 3).reshape(-1, tokens) - vocab_start
    place = jnp.arange(tokens)
    before = (lists[:, None, :] < lists[:, :, None]) | (
        (lists[:, None, :] == lists[:, :, None]) & (place[None, None, :] < place[None, :, None])
    )
    ranks = jnp.sum(before.astype(jnp.int32), axis=-1)
    sorted_ids = jnp.sum(
        jnp.where(ranks[:, None, :] == place[None, :, None], lists[:, None, :], 0), axis=-1
    )
    own_list = (
        lax.axis_index("section") * replicas + lax.axis_index("dp")
    ) * planes + me
    arrange = (pick(ranks, own_list)[None, :] == place[:, None]).astype(LOW)

    full = gather_weights(
        planes,
        replicas,
        [w_qkv[0].astype(LOW), w_out[0].astype(LOW), w_gateup[0].astype(LOW), w_down[0].astype(LOW)],
    )
    layer_weights = (full[0], full[1], full[2], full[3], gains_full[0], gains_full[1])
    head_gain = gains_full[2]

    first_out, _ = layer_fwd(looked, layer_weights)
    middle = swap(first_out.astype(LOW), "section", 1).astype(WIDE)
    layer_in = jnp.where(first, looked, middle)
    layer_out, saved = layer_fwd(layer_in, layer_weights)
    final_state = norm_fwd(layer_out, head_gain)
    arrived = swap(final_state.astype(LOW), "section", 1).astype(WIDE)
    merged_in = jnp.where(first, arrived + next_embed, layer_out)
    head_in = norm_fwd(merged_in, head_gain)

    lengths = seq_lengths.reshape(replicas, planes, MB)[lax.axis_index("dp")]
    lengths = jnp.stack([pick(lengths, (me - step) % planes) for step in range(planes)])
    targets_main = rel_ids[:, 1].reshape(planes, MB, ROW)
    shifted = jnp.concatenate([targets_main[..., 1:], targets_main[..., :1]], axis=-1)
    targets = jnp.where(first, shifted, targets_main)
    limit = lengths - first.astype(jnp.int32)
    positions = jnp.arange(ROW, dtype=jnp.int32)
    weights_tok = (positions < limit[..., None]).astype(WIDE) * jnp.where(first, MTP_WEIGHT, 1.0)
    left = [saved[0], saved[6], saved[8]]
    left_all = spread(
        lambda index: jnp.concatenate(left + [sub_quarter(saved[10], planes, index)], axis=1)
    )
    loss_part, mine, theirs, grad_in = head_pass(
        head_in.astype(LOW),
        targets.reshape(-1),
        weights_tok.reshape(-1),
        head_table.T,
        vocab_start,
        token_total,
    )
    sorted_ids, loss_part = lax.optimization_barrier((sorted_ids, loss_part))
    merged_grad, mtp_gain = norm_back(merged_in, head_gain, grad_in)
    merged_low = merged_grad.astype(LOW)
    sent = swap(merged_low, "section", 1).astype(WIDE)
    top_grad, top_gain = norm_back(layer_out, head_gain, grad_in + sent)
    head_gain_grad = jnp.where(first, mtp_gain, top_gain)
    half = add_low(mine, swap(theirs, "section", 1))
    top_grad, left_all, half = lax.optimization_barrier((top_grad, left_all, half))
    below, _, _ = layer_back(layer_in, layer_weights, saved, top_grad)
    side = half.shape[0] // 2
    piece_a, piece_b = keep_half(half[:side], 1), keep_half(half[side:], 2)
    below, piece_a, piece_b = lax.optimization_barrier((below.astype(LOW), piece_a, piece_b))
    upstream = jnp.where(first, swap(below, "section", 1).astype(WIDE), top_grad)
    grad_inputs, right, gain_parts = layer_back(layer_in, layer_weights, saved, upstream)
    piece_a, piece_b = keep_half(piece_a, 2), keep_half(piece_b, 1)
    grad_inputs, piece_a, piece_b = lax.optimization_barrier((grad_inputs, piece_a, piece_b))

    grad_packed, after_low, grad_gu, upstream_low = right
    tops = spread(lambda index: upstream_low)
    early = spread(lambda index: quarter(grad_gu, index))
    late = spread(
        lambda index: jnp.concatenate([quarter(after_low, index), quarter(grad_packed, index)], axis=1)
    )
    cut = D // SHARE
    parts = [
        contract_rows(left_all[:, 2 * D : 3 * D], early),
        contract_rows(left_all[:, 3 * D :], tops),
        contract_rows(left_all[:, :D], late[:, cut:]),
        contract_rows(left_all[:, D : 2 * D], late[:, :cut]),
    ]
    parts = [part.astype(LOW) for part in parts]
    gains_grad = jnp.stack([gain_parts[0], gain_parts[1], head_gain_grad])
    gains_grad = jnp.sum(small_gather([gains_grad], ("dp", "fsdp"), 4)[0], axis=0)
    gains_grad = lax.dynamic_slice_in_dim(gains_grad, me * (D // planes), D // planes, 1)

    row_grads = jnp.where(first, grad_inputs.astype(LOW), sent.astype(LOW))
    row_grads = jnp.dot(arrange, row_grads, preferred_element_type=WIDE).astype(LOW)
    rows_all, grad_head, slots = exchange(planes, row_grads, (piece_a, piece_b), parts)
    rows_flat = rows_all.reshape(-1, D)
    ids_column = sorted_ids.reshape(-1, 1)

    def square(item):
        wide = item.astype(WIDE)
        return jnp.sum(wide * wide)

    shards = []
    for part, slot in zip(parts, slots):
        mine = pick(part.reshape((planes,) + slot.shape[1:]), me).astype(WIDE)
        shards.append((mine + jnp.sum(slot.astype(WIDE), axis=0)).astype(LOW))
    group = lax.axis_index("section") * replicas + lax.axis_index("dp")
    squares = table_square(sorted_ids, ids_column, rows_flat, group, 2 * replicas, vocab_rows)
    for item in shards + [piece_a, piece_b]:
        squares = squares + square(item)
    squares = squares + square(gains_grad) / replicas
    totals = jnp.stack([squares, loss_part / planes])[:, None] * jnp.ones((1, 128), WIDE)
    totals = jnp.sum(small_gather([totals], ("section", "dp", "fsdp"), 5)[0], axis=0)[:, 0]
    grad_norm = jnp.sqrt(totals[0])
    loss_total = totals[1]
    clip_scale = CLIP / jnp.maximum(grad_norm, CLIP)

    shards, clip_scale = lax.optimization_barrier((shards, clip_scale))
    widths = [0, 2 * D, 3 * D, 3 * D + 3 * cut, 4 * D]
    packed = jnp.concatenate(shards, axis=1)
    rank = plane_rank()
    others = [packed] + [swap(packed, "dp", mask) for mask in range(1, SHARE)]
    layer_grads = [
        in_order([other[:, lo:hi] for other in others], rank, 0 if index == 1 else 1).astype(WIDE)
        for index, (lo, hi) in enumerate(zip(widths[:-1], widths[1:]))
    ]
    params = (w_qkv[0], w_out[0], w_gateup[0], w_down[0], gains[0])
    grads_all = (
        layer_grads[2],
        layer_grads[3],
        layer_grads[0],
        layer_grads[1],
        gains_grad,
    )
    moments = (
        (qkv_mom[0], qkv_sec[0]),
        (out_mom[0], out_sec[0]),
        (gateup_mom[0], gateup_sec[0]),
        (down_mom[0], down_sec[0]),
        (gains_mom[0], gains_sec[0]),
    )
    rates = (0.03, 0.12, 0.03, 0.03, 0.6)
    decays = (0.1, 0.1, 0.1, 0.1, 0.0)
    outputs = [loss_total, token_total, grad_norm]
    outputs += table_adam(
        sorted_ids,
        ids_column,
        rows_flat,
        clip_scale,
        embedding,
        embedding_mom,
        embedding_sec,
        0.6,
        0.1,
    )
    outputs += head_adam(grad_head, clip_scale, head_table, head_mom, head_sec, 0.03, 0.1)
    for index in range(5):
        weight_new, mom_new, sec_new = adam_update(
            params[index],
            grads_all[index] * clip_scale,
            moments[index][0],
            moments[index][1],
            rates[index],
            decays[index],
        )
        outputs.extend([weight_new[None], mom_new[None], sec_new[None]])
        if index < 4:
            outputs.append(weight_new.astype(LOW)[None])
    return tuple(outputs)


def solution(mesh):
    placed = (
        P(("dp", "fsdp"), None),
        P(("dp", "fsdp"), None),
        P(),
        P("fsdp", None),
        P("fsdp", None),
        P("fsdp", None),
        P(None, "fsdp"),
        P(None, "fsdp"),
        P(None, "fsdp"),
        P("section", "fsdp", None),
        P("section", "fsdp", None),
        P("section", "fsdp", None),
        P("section", "fsdp", None),
        P("section", "fsdp", None),
        P("section", "fsdp", None),
        P("section", "fsdp", None),
        P("section", "fsdp", None),
        P("section", "fsdp", None),
        P("section", "fsdp", None),
        P("section", "fsdp", None),
        P("section", "fsdp", None),
        P("section", None, "fsdp"),
        P("section", None, "fsdp"),
        P("section", None, "fsdp"),
    )
    return jax.shard_map(
        per_device,
        mesh=mesh,
        in_specs=placed,
        out_specs=(
            P(),
            P(),
            P(),
            P("fsdp", None),
            P("fsdp", None),
            P("fsdp", None),
            P("fsdp", None),
            P(None, "fsdp"),
            P(None, "fsdp"),
            P(None, "fsdp"),
            P(None, "fsdp"),
            P("section", "fsdp", None),
            P("section", "fsdp", None),
            P("section", "fsdp", None),
            P("section", "fsdp", None),
            P("section", "fsdp", None),
            P("section", "fsdp", None),
            P("section", "fsdp", None),
            P("section", "fsdp", None),
            P("section", "fsdp", None),
            P("section", "fsdp", None),
            P("section", "fsdp", None),
            P("section", "fsdp", None),
            P("section", "fsdp", None),
            P("section", "fsdp", None),
            P("section", "fsdp", None),
            P("section", "fsdp", None),
            P("section", None, "fsdp"),
            P("section", None, "fsdp"),
            P("section", None, "fsdp"),
        ),
        check_vma=False,
    )
```

```python
import functools
import math

import jax
import jax.numpy as jnp
from jax import lax
from jax.experimental import pallas as pl
from jax.experimental.pallas import tpu as pltpu
from jax.sharding import PartitionSpec as P

D = 768
HEADS = 12
HEAD_DIM = 64
FF = 3072
ROW = 128
MB = 2
STEP_COUNT = 10
SHARE = 4


EPS = 1e-05
MTP_WEIGHT = 0.3
CLIP = 0.01
BETA1 = 0.9
BETA2 = 0.95
ADAM_EPS = 1e-08
LOW = jnp.bfloat16
WIDE = jnp.float32

AHEAD = 2
MESH = pl.DeviceIdType.MESH

def weights_kernel(planes, units, rows, *refs):
    n = len(rows)
    own, full = refs[:n], refs[n : 2 * n]
    send, recv, local = refs[2 * n :]
    z = lax.axis_index("fsdp")
    i = lax.axis_index("dp")
    x, y = i % 2, i // 2
    q = i
    xn, yn = i + 1 - 2 * x, (i + 2) % 4
    near, far = z + 1 - 2 * (z % 2), planes - 1 - z
    beyond = planes - 1 - near
    to_x, to_y, to_near, to_far = {"dp": xn}, {"dp": yn}, {"fsdp": near}, {"fsdp": far}
    barrier = pltpu.get_barrier_semaphore()
    for device in (to_x, to_y, to_near, to_far):
        pl.semaphore_signal(barrier, inc=1, device_id=device, device_id_type=MESH)
    pl.semaphore_wait(barrier, 4)
    keep = []
    for m in range(n):
        c = pltpu.make_async_copy(
            own[m], full[m].at[pl.ds(pl.multiple_of(z * rows[m], 16), rows[m]), :], local.at[m]
        )
        c.start()
        keep.append(c)
    started = []

    def put(src, dst, k, device):
        copy = pltpu.make_async_remote_copy(
            src_ref=src,
            dst_ref=dst,
            send_sem=send.at[k],
            recv_sem=recv.at[k],
            device_id=device,
            device_id_type=MESH,
        )
        copy.start()
        started.append(copy)
        return copy

    def block(u, plane, part):
        m, cols, _ = units[u]
        r = rows[m] // 4
        return full[m].at[pl.ds(pl.multiple_of(plane * rows[m] + part * r, 16), r), pl.ds(*cols)]

    sources = (near, far, beyond)
    zs, seconds, thirds = {}, {}, []
    total = len(units)

    def first(u):
        m, cols, _ = units[u]
        r = rows[m] // 4
        src = own[m].at[pl.ds(pl.multiple_of(q * r, 16), r), pl.ds(*cols)]
        zs[u, 0] = put(src, block(u, z, q), 12 * u, to_near)
        zs[u, 1] = put(src, block(u, z, q), 12 * u + 1, to_far)

    def onward(u):
        zs[u, 1].wait_recv()
        zs[u, 2] = put(block(u, far, q), block(u, far, q), 12 * u + 2, to_near)

    def second(u, j):
        if j != 1:
            zs[u, j].wait_recv()
        b = block(u, sources[j], q)
        seconds[u, j] = put(b, b, 12 * u + 3 + j, to_y if units[u][2] else to_x)

    def third(u, j):
        seconds[u, j].wait_recv()
        order = units[u][2]
        for w, part in enumerate((q, yn if order else xn)):
            b = block(u, sources[j], part)
            thirds.append(put(b, b, 12 * u + 6 + 2 * j + w, to_x if order else to_y))

    pairs = [(u, u + 1) for u in range(0, total, 2)]
    for ahead in range(AHEAD):
        for u in pairs[ahead]:
            first(u)
    for t in range(len(pairs) + 2):
        if t < len(pairs):
            for u in pairs[t]:
                onward(u)
            if t + AHEAD < len(pairs):
                for u in pairs[t + AHEAD]:
                    first(u)
            for j in (0, 1):
                for u in pairs[t]:
                    second(u, j)
        if 1 <= t <= len(pairs):
            for u in pairs[t - 1]:
                second(u, 2)
            for j in (0, 1):
                for u in pairs[t - 1]:
                    third(u, j)
        if t >= 2:
            for u in pairs[t - 2]:
                third(u, 2)
    for c in thirds:
        c.wait_recv()
    for c in started:
        c.wait_send()
    for c in keep:
        c.wait()


def gather_weights(planes, replicas, shards):
    rows = [w.shape[0] for w in shards]
    if planes != 4 or replicas != 4 or any(r % (SHARE * 16) for r in rows):
        return [lax.all_gather(w, "fsdp", axis=0, tiled=True) for w in shards]
    units = []
    for m, w in enumerate(shards):
        width = w.shape[1]
        parts = 4 if width > 4096 else 2
        step = width // parts
        for p in range(parts):
            units.append((m, (p * step, step), p % 2))
    copies = len(units) * 12
    return pl.pallas_call(
        functools.partial(weights_kernel, planes, units, rows),
        out_shape=[jax.ShapeDtypeStruct((planes * w.shape[0], w.shape[1]), w.dtype) for w in shards],
        in_specs=[pl.BlockSpec(memory_space=pltpu.VMEM)] * len(shards),
        out_specs=[pl.BlockSpec(memory_space=pl.ANY)] * len(shards),
        scratch_shapes=[pltpu.SemaphoreType.DMA((copies,)), pltpu.SemaphoreType.DMA((copies,)), pltpu.SemaphoreType.DMA((len(shards),))],
        compiler_params=pltpu.CompilerParams(collective_id=1, has_side_effects=True),
        name="gather_weights",
    )(*shards)


def norm_fwd(values, scale_gain):
    inverse = lax.rsqrt(jnp.mean(values * values, axis=-1, keepdims=True) + EPS)
    return values * inverse * scale_gain


def norm_back(values, scale_gain, upstream):
    _, pullback = jax.vjp(norm_fwd, values, scale_gain)
    return pullback(upstream)


def rope_tables(row_count, head_width):
    half_width = head_width // 2
    position = jnp.arange(row_count, dtype=jnp.float32)[:, None]
    frequency = 10000.0 ** (-jnp.arange(half_width, dtype=jnp.float32) / half_width)
    angles = position * frequency[None, :]
    return (jnp.cos(angles), jnp.sin(angles))


def rotate(values, cosine, sine_table):
    half_width = values.shape[-1] // 2
    first, second = (values[..., :half_width], values[..., half_width:])
    return jnp.concatenate(
        [first * cosine - second * sine_table, second * cosine + first * sine_table], axis=-1
    )


def contract_rows(left, right):
    return lax.dot_general(
        left, right, (((0,), (0,)), ((), ())), preferred_element_type=jnp.float32
    )


def contract_cols(left, right):
    return lax.dot_general(
        left, right, (((1,), (1,)), ((), ())), preferred_element_type=jnp.float32
    )


def swiglu(gate_up):
    return jax.nn.silu(gate_up[:, :FF]) * gate_up[:, FF:]


def shift(block, axis, distance):
    count = lax.axis_size(axis)
    return lax.ppermute(block, axis, [(i, (i + distance) % count) for i in range(count)])


def swap(block, axis, mask):
    count = lax.axis_size(axis)
    return lax.ppermute(block, axis, [(i, i ^ mask) for i in range(count)])


def pick(array, index, axis=0):
    return lax.dynamic_index_in_dim(array, index, axis, keepdims=False)


def layer_fwd(inputs, weights):
    w_qkv, w_out, w_gateup, w_down, attn_gain, ffn_gain = weights
    normed = norm_fwd(inputs, attn_gain).astype(LOW)
    packed = jnp.dot(normed, w_qkv, preferred_element_type=WIDE)
    split = packed.reshape(MB, ROW, 3, HEADS, HEAD_DIM).transpose(2, 0, 3, 1, 4)
    split = split.reshape(3, MB * HEADS, ROW, HEAD_DIM)
    cosine, sine_table = rope_tables(ROW, HEAD_DIM)
    queries = rotate(split[0], cosine, sine_table).astype(LOW)
    keys_rot = rotate(split[1], cosine, sine_table).astype(LOW)
    values_low = split[2].astype(LOW)
    scores = jnp.einsum(
        "hqd,hkd->hqk", queries, keys_rot, preferred_element_type=WIDE
    ) * HEAD_DIM ** (-0.5)
    position = jnp.arange(ROW)
    causal = position[:, None] >= position[None, :]
    scores = jnp.where(causal[None], scores, -1e30)
    shifted = jnp.exp(scores - jnp.max(scores, axis=-1, keepdims=True))
    probs = shifted / jnp.sum(shifted, axis=-1, keepdims=True)
    probs_low = probs.astype(LOW)
    mixed = jnp.einsum("hqk,hkd->hqd", probs_low, values_low, preferred_element_type=WIDE)
    mixed = mixed.reshape(MB, HEADS, ROW, HEAD_DIM).transpose(0, 2, 1, 3)
    mixed_low = mixed.reshape(MB * ROW, D).astype(LOW)
    after_attn = inputs + jnp.dot(mixed_low, w_out, preferred_element_type=WIDE)
    normed_ffn = norm_fwd(after_attn, ffn_gain).astype(LOW)
    gate_up = jnp.dot(normed_ffn, w_gateup, preferred_element_type=WIDE)
    hidden = swiglu(gate_up).astype(LOW)
    output = after_attn + jnp.dot(hidden, w_down, preferred_element_type=WIDE)
    saved = (
        normed,
        queries,
        keys_rot,
        values_low,
        probs,
        probs_low,
        mixed_low,
        after_attn,
        normed_ffn,
        gate_up,
        hidden,
    )
    return (output, saved)


def layer_back(inputs, weights, saved, upstream):
    w_qkv, w_out, w_gateup, w_down, attn_gain, ffn_gain = weights
    (
        normed,
        queries,
        keys_rot,
        values_low,
        probs,
        probs_low,
        mixed_low,
        after_attn,
        normed_ffn,
        gate_up,
        hidden,
    ) = saved
    upstream_low = upstream.astype(LOW)
    grad_hidden = contract_cols(upstream_low, w_down)
    _, pullback = jax.vjp(swiglu, gate_up)
    grad_gu = pullback(grad_hidden)[0].astype(LOW)
    grad_nffn = contract_cols(grad_gu, w_gateup)
    back_ffn, grad_ffn_gain = norm_back(after_attn, ffn_gain, grad_nffn)
    grad_after = upstream + back_ffn
    after_low = grad_after.astype(LOW)
    grad_mixed = contract_cols(after_low, w_out).astype(LOW)
    grad_mixed = grad_mixed.reshape(MB, ROW, HEADS, HEAD_DIM).transpose(0, 2, 1, 3)
    grad_mixed = grad_mixed.reshape(MB * HEADS, ROW, HEAD_DIM)
    grad_probs = jnp.einsum("hqd,hkd->hqk", grad_mixed, values_low, preferred_element_type=WIDE)
    grad_values = jnp.einsum("hqk,hqd->hkd", probs_low, grad_mixed, preferred_element_type=WIDE)
    grad_scores = probs * (grad_probs - jnp.sum(probs * grad_probs, axis=-1, keepdims=True))
    grad_scores = grad_scores.astype(LOW)
    scale_attn = HEAD_DIM ** (-0.5)
    grad_query = (
        jnp.einsum("hqk,hkd->hqd", grad_scores, keys_rot, preferred_element_type=WIDE)
        * scale_attn
    )
    grad_key = (
        jnp.einsum("hqk,hqd->hkd", grad_scores, queries, preferred_element_type=WIDE)
        * scale_attn
    )
    cosine, sine_table = rope_tables(ROW, HEAD_DIM)
    grad_query = rotate(grad_query, cosine, -sine_table)
    grad_key = rotate(grad_key, cosine, -sine_table)
    grad_packed = jnp.stack([grad_query, grad_key, grad_values]).astype(LOW)
    grad_packed = grad_packed.reshape(3, MB, HEADS, ROW, HEAD_DIM).transpose(1, 3, 0, 2, 4)
    grad_packed = grad_packed.reshape(MB * ROW, 3 * D)
    grad_normed = contract_cols(grad_packed, w_qkv)
    back_attn, grad_attn_gain = norm_back(inputs, attn_gain, grad_normed)
    grad_inputs = grad_after + back_attn
    return (
        grad_inputs,
        (grad_packed, after_low, grad_gu, upstream_low),
        (grad_attn_gain, grad_ffn_gain),
    )


def plane_rank():
    return lax.axis_index("dp")


def quarter(block, index):
    width = block.shape[1] // SHARE
    return lax.dynamic_slice_in_dim(block, index * width, width, 1)


def sub_quarter(block, planes, index):
    rows, width = block.shape
    split = block.reshape(rows, planes, SHARE, width // planes // SHARE)
    return lax.dynamic_index_in_dim(split, index, 2, keepdims=False).reshape(rows, -1)


def spread(make):
    rank = plane_rank()
    own = make(rank)
    rows = own.shape[0]
    full = lax.dynamic_update_slice(jnp.zeros((SHARE * rows, own.shape[1]), LOW), own, (0, 0))
    for mask in range(1, SHARE):
        piece = swap(make(rank ^ mask), "dp", mask)
        full = lax.dynamic_update_slice(full, piece, (mask * rows, 0))
    return full


def in_order(pieces, rank, axis):
    low = rank % 2 == 0
    top = rank // 2 == 0
    pairs = []
    for k in (0, 2):
        pairs.append(
            (jnp.where(low, pieces[k], pieces[k + 1]), jnp.where(low, pieces[k + 1], pieces[k]))
        )
    lower = [jnp.where(top, pairs[0][j], pairs[1][j]) for j in range(2)]
    upper = [jnp.where(top, pairs[1][j], pairs[0][j]) for j in range(2)]
    return jnp.concatenate(lower + upper, axis=axis)


def relative_blocks():
    s = lax.axis_index("section")
    i = lax.axis_index("dp")
    x, y = i % 2, i // 2
    blocks = []
    for es in (0, 1):
        for kind in (0, 1):
            for e1 in (0, 1):
                for e2 in (0, 1):
                    a, b = (x, y) if kind == 0 else (y, x)
                    within = ((a + e1) % 2) * 2 + (b + e2) % 2
                    blocks.append(((s + es) % 2) * 8 + kind * 4 + within)
    return jnp.stack(blocks).astype(jnp.int32)


TOKENS = 256


def head_piece(vocab):
    return -(-vocab // 256) * 16


def table_block(vocab, base, h_ref):
    inside = lax.broadcasted_iota(jnp.int32, h_ref.shape, 0) + base < vocab
    return jnp.where(inside, h_ref[...], 0.0).astype(LOW)


def head_scores(vocab, base, table, rows):
    logits = contract_cols(table, rows)
    index = lax.broadcasted_iota(jnp.int32, logits.shape, 0) + base
    return jnp.where(index < vocab, logits, -1e30), index


def head_stats_kernel(vocab, h_ref, rows_ref, target_ref, out):
    step = pl.program_id(0)
    base = step * h_ref.shape[0]
    table = table_block(vocab, base, h_ref)

    @pl.when(step == 0)
    def _():
        out[0:1, :] = jnp.full((1, out.shape[1]), -1e30, WIDE)
        out[1:3, :] = jnp.zeros((2, out.shape[1]), WIDE)

    for c in range(rows_ref.shape[0] // TOKENS):
        span = slice(c * TOKENS, (c + 1) * TOKENS)
        logits, index = head_scores(vocab, base, table, rows_ref[span, :])
        before = out[0:1, span]
        peak = jnp.maximum(before, jnp.max(logits, axis=0, keepdims=True))
        summed = jnp.sum(jnp.exp(logits - peak), axis=0, keepdims=True)
        picked = jnp.sum(jnp.where(index == target_ref[:, span], logits, 0.0), axis=0, keepdims=True)
        out[0:1, span] = peak
        out[1:2, span] = out[1:2, span] * jnp.exp(before - peak) + summed
        out[2:3, span] += picked


def once(shape):
    return pl.BlockSpec(shape, lambda g, *_: (0,) * len(shape), pipeline_mode=pl.Buffered(1))


def head_stats(head, rows, targets):
    vocab, count = head.shape[0], rows.shape[0]
    piece = head_piece(vocab)
    return pl.pallas_call(
        functools.partial(head_stats_kernel, vocab),
        grid=(-(-vocab // piece),),
        in_specs=[pl.BlockSpec((piece, D), lambda g: (g, 0)), once((count, D)), once((1, count))],
        out_specs=pl.BlockSpec((8, count), lambda g: (0, 0)),
        out_shape=jax.ShapeDtypeStruct((8, count), WIDE),
        compiler_params=pltpu.CompilerParams(vmem_limit_bytes=50 << 20),
        cost_estimate=pl.CostEstimate(
            flops=2 * vocab * count * D, bytes_accessed=vocab * D * 4, transcendentals=vocab * count
        ),
        name="head_stats",
    )(head, rows, targets)


def head_grads_kernel(vocab, order, h_ref, rows_ref, target_ref, lse_ref, factor_ref, g_ref, c_ref, flipped, delta):
    step = pl.program_id(0)
    base = order[step] * h_ref.shape[0]
    table = table_block(vocab, base, h_ref)
    flipped[...] = table.astype(WIDE).T.astype(LOW)

    @pl.when(step == 0)
    def _():
        c_ref[...] = jnp.zeros(c_ref.shape, WIDE)

    for c in range(rows_ref.shape[0] // TOKENS):
        span = slice(c * TOKENS, (c + 1) * TOKENS)
        logits, index = head_scores(vocab, base, table, rows_ref[span, :])
        onehot = (index == target_ref[:, span]).astype(WIDE)
        delta[:, span] = (
            (jnp.exp(logits - lse_ref[:, span]) - onehot) * factor_ref[:, span]
        ).astype(LOW)
    g_ref[...] = jnp.dot(delta[...], rows_ref[...], preferred_element_type=WIDE).astype(LOW)
    for c in range(rows_ref.shape[0] // TOKENS):
        span = slice(c * TOKENS, (c + 1) * TOKENS)
        c_ref[:, span] += jnp.dot(flipped[...], delta[:, span], preferred_element_type=WIDE)


def head_grads(head, rows, targets, lse, factor):
    vocab, count = head.shape[0], rows.shape[0]
    piece = head_piece(vocab)
    return pl.pallas_call(
        functools.partial(head_grads_kernel, vocab),
        grid_spec=pltpu.PrefetchScalarGridSpec(
            num_scalar_prefetch=1,
            grid=(16,),
            in_specs=[
                pl.BlockSpec((piece, D), lambda g, order: (order[g], 0)),
                once((count, D)),
                once((1, count)),
                once((1, count)),
                once((1, count)),
            ],
            out_specs=[
                pl.BlockSpec((piece, D), lambda g, order: (g, 0)),
                pl.BlockSpec((D, count), lambda g, order: (0, 0)),
            ],
            scratch_shapes=[pltpu.VMEM((D, piece), LOW), pltpu.VMEM((piece, count), LOW)],
        ),
        out_shape=[
            jax.ShapeDtypeStruct((16 * piece, D), LOW),
            jax.ShapeDtypeStruct((D, count), WIDE),
        ],
        compiler_params=pltpu.CompilerParams(vmem_limit_bytes=56 << 20),
        cost_estimate=pl.CostEstimate(
            flops=6 * vocab * count * D, bytes_accessed=vocab * D * 8, transcendentals=vocab * count
        ),
        name="head_grads",
    )(relative_blocks(), head, rows, targets, lse, factor)


def head_pass(rows_low, targets, weights_tok, head, vocab_start, token_total):
    planes = lax.axis_size("fsdp")
    gathered = jnp.concatenate(
        [rows_low] + [shift(rows_low, "fsdp", step) for step in range(1, planes)], axis=0
    )
    local = targets - vocab_start
    local = jnp.where((local >= 0) & (local < head.shape[0]), local, -1)[None, :]
    stats = head_stats(head, gathered, local)[:3].reshape(3, planes, -1)
    parts = [stats] + [
        jnp.roll(shift(stats, "fsdp", step), step, axis=1) for step in range(1, planes)
    ]
    parts = jnp.stack(parts)
    peak = jnp.max(parts[:, 0], axis=0)
    total = jnp.sum(parts[:, 1] * jnp.exp(parts[:, 0] - peak[None]), axis=0)
    lse = (peak + jnp.log(total)).reshape(-1)
    loss_part = jnp.sum((lse - jnp.sum(parts[:, 2], axis=0).reshape(-1)) * weights_tok)
    factor = weights_tok / token_total
    grad_head, partial = head_grads(head, gathered, local, lse[None, :], factor[None, :])
    partial = partial.T.reshape(planes, -1, D)
    grad_rows = partial[0]
    for step in range(1, planes):
        grad_rows = grad_rows + shift(partial[step].astype(LOW), "fsdp", planes - step).astype(WIDE)
    middle = grad_head.shape[0] // 2
    return (loss_part, grad_head[:middle], grad_head[middle:], grad_rows)


def add_low(one, other):
    return (one.astype(WIDE) + other.astype(WIDE)).astype(LOW)


def keep_half(block, mask):
    half = block.shape[0] // 2
    return add_low(block[:half], swap(block[half:], "dp", mask))


def adam_update(weight, grad, first_mom, second_mom, rate, decay):
    mom_new = BETA1 * first_mom + (1.0 - BETA1) * grad
    sec_new = BETA2 * second_mom + (1.0 - BETA2) * grad * grad
    mom_hat = mom_new / (1.0 - BETA1**STEP_COUNT)
    sec_hat = sec_new / (1.0 - BETA2**STEP_COUNT)
    weight_new = weight - rate * (mom_hat / (jnp.sqrt(sec_hat) + ADAM_EPS) + decay * weight)
    return (weight_new, mom_new, sec_new)


def exchange_kernel(planes, rows_ref, pa, pb, *refs):
    paired = planes == 4
    n = (len(refs) - 7) // (4 if paired else 2)
    parts, rows_all, head, slots = refs[:n], refs[n], refs[n + 1], refs[n + 2 : 2 * n + 2]
    send, recv, core_send, core_recv, local = refs[2 * n + 2 : 2 * n + 7]
    totals, extras = refs[2 * n + 7 : 3 * n + 7], refs[3 * n + 7 :]
    s = lax.axis_index("section")
    i = lax.axis_index("dp")
    z = lax.axis_index("fsdp")
    x, y = i % 2, i // 2
    xn, yn, diag = i + 1 - 2 * x, (i + 2) % 4, 3 - i
    partner = z + 1 - 2 * (z % 2)
    to_x, to_y, to_core = {"dp": xn}, {"dp": yn}, {"section": 1 - s}
    barrier = pltpu.get_barrier_semaphore()
    for device in [to_x, to_y, to_core] + [{"fsdp": (z + k) % planes} for k in range(1, planes)]:
        pl.semaphore_signal(barrier, inc=1, device_id=device, device_id_type=MESH)
    pl.semaphore_wait(barrier, planes + 2)
    counts = [0, 0]
    sent = []

    def put(src, dst, device):
        over = device is to_core
        k = counts[over]
        counts[over] += 1
        copy = pltpu.make_async_remote_copy(
            src_ref=src,
            dst_ref=dst,
            send_sem=(core_send if over else send).at[k],
            recv_sem=(core_recv if over else recv).at[k],
            device_id=device,
            device_id_type=MESH,
        )
        copy.start()
        sent.append(copy)
        return copy

    def take(*copies):
        for copy in copies:
            copy.wait_recv()

    piece = pa.shape[0]
    side = 4 * piece

    def head_a(xx, yy, count):
        return head.at[pl.ds(pl.multiple_of(s * 2 * side + xx * 2 * piece + yy * piece, 16), count)]

    def head_b(xx, yy, count):
        return head.at[
            pl.ds(pl.multiple_of(s * 2 * side + side + yy * 2 * piece + xx * piece, 16), count)
        ]

    own = []
    for k, (src, dst) in enumerate(
        [(rows_ref, rows_all.at[s, i, z]), (pa, head_a(x, y, piece)), (pb, head_b(x, y, piece))]
    ):
        copy = pltpu.make_async_copy(src, dst, local.at[k])
        copy.start()
        own.append(copy)
    reduce = []

    def part_of(m, plane):
        height = slots[m].shape[1]
        return parts[m].at[pl.ds(pl.multiple_of(plane * height, 16), height)]

    fetched, passed = [], []
    if paired:
        for m in range(n):
            copy = pltpu.make_async_copy(part_of(m, planes - 1 - z), totals[m], local.at[3 + m])
            copy.start()
            fetched.append(copy)
    near = [put(rows_ref, rows_all.at[s, i, z], {"fsdp": (z + k) % planes}) for k in range(1, planes)]
    head1 = [put(pa, head_a(x, y, piece), to_y), put(pb, head_b(x, y, piece), to_x)]
    if not paired:
        for m in range(n):
            for k in range(1, planes):
                target = (z + k) % planes
                reduce.append(put(part_of(m, target), slots[m].at[k - 1], {"fsdp": target}))
    for copy in own:
        copy.wait()
    take(*near)
    if paired:
        for m in range(n):
            passed.append(put(part_of(m, planes - 1 - partner), extras[m], {"fsdp": partner}))
    mid = planes // 2
    early, late = pl.ds(0, mid), pl.ds(mid, planes - mid)
    a1 = put(rows_all.at[s, i, early], rows_all.at[s, i, early], to_x)
    b1 = put(rows_all.at[s, i, late], rows_all.at[s, i, late], to_y)
    core = [put(rows_all.at[s, i], rows_all.at[s, i], to_core)]
    take(*head1)
    block = head_a(x, 0, 2 * piece)
    ha = put(block, block, to_x)
    block = head_b(0, y, 2 * piece)
    hb = put(block, block, to_y)
    take(a1, b1)
    second = []
    for who, span, device in ((i, early, to_y), (xn, early, to_y), (i, late, to_x), (yn, late, to_x)):
        block = rows_all.at[s, who, span]
        second.append(put(block, block, device))
    for who, span in ((xn, early), (yn, late)):
        block = rows_all.at[s, who, span]
        core.append(put(block, block, to_core))
    if paired:
        for copy in fetched:
            copy.wait()
        for m in range(n):
            passed[m].wait_recv()
            held = totals[m][...].astype(WIDE) + extras[m][...].astype(WIDE)
            totals[m][...] = held.astype(LOW)
            reduce.append(put(totals[m], slots[m].at[1], {"fsdp": planes - 1 - z}))
            reduce.append(put(part_of(m, partner), slots[m].at[0], {"fsdp": partner}))
    take(ha, hb)
    block = head.at[pl.ds(pl.multiple_of(s * 2 * side, 16), 2 * side)]
    core.append(put(block, block, to_core))
    take(*second)
    for who, span in ((yn, early), (diag, early), (xn, late), (diag, late)):
        block = rows_all.at[s, who, span]
        core.append(put(block, block, to_core))
    take(*reduce)
    take(*core)
    for copy in sent:
        copy.wait_send()


def exchange(planes, row_grads, pieces, parts):
    piece, vocab = pieces[0].shape
    shape = jax.ShapeDtypeStruct
    outs = [shape((2, 4, planes) + row_grads.shape, LOW), shape((16 * piece, vocab), LOW)]
    blocks = [(p.shape[0] // planes, p.shape[1]) for p in parts]
    paired = planes == 4
    outs += [shape((2 if paired else planes - 1,) + b, LOW) for b in blocks]
    copies = (planes - 1) * (1 + len(parts)) + 2 + 2 + 2 + 4
    anywhere = pl.BlockSpec(memory_space=pl.ANY)
    result = pl.pallas_call(
        functools.partial(exchange_kernel, planes),
        out_shape=outs,
        in_specs=[pl.BlockSpec(memory_space=pltpu.VMEM)] * 3 + [anywhere] * len(parts),
        out_specs=[anywhere] * len(outs),
        scratch_shapes=[pltpu.SemaphoreType.DMA((copies,))] * 2
        + [pltpu.SemaphoreType.DMA((8,))] * 2
        + [pltpu.SemaphoreType.DMA((3 + len(parts),))]
        + ([pltpu.VMEM(b, LOW) for b in blocks] * 2 if paired else []),
        compiler_params=pltpu.CompilerParams(
            collective_id=2, has_side_effects=True, vmem_limit_bytes=16 << 20
        ),
        name="exchange",
    )(row_grads, *pieces, *parts)
    return result[0], result[1], result[2:]


def block_of(vocab_rows):
    return 800 if vocab_rows % 800 == 0 else 400


def chunk_of(lists):
    return 32 if lists <= 64 else 16


def start_chunks(lists, length, stride, step, steps, starts, rows_hbm, buffer, sem):
    chunk = chunk_of(lists)

    def one(k, carry):
        at = jnp.minimum(starts[k * steps + step] // 16 * 16, length - chunk)
        src = rows_hbm.at[pl.ds(pl.multiple_of(k * stride + at, 16), chunk)]
        pltpu.make_async_copy(src, buffer.at[pl.ds(pl.multiple_of(k * chunk, 16), chunk)], sem).start()
        return carry

    lax.fori_loop(0, lists, one, 0)


def block_grad(
    lists, length, steps, step, starts, passes, bases, rows_hbm, ids_ref, near_ref, buffers, hot, wide_hot, grad, sems
):
    chunk = chunk_of(lists)
    slot = step % 2
    spare = buffers.at[2]
    width = grad.shape[0]
    stride = rows_hbm.shape[0] // lists

    @pl.when(step == 0)
    def _():
        start_chunks(lists, length, stride, 0, steps, starts, rows_hbm, buffers.at[0], sems.at[0])

    @pl.when(step + 1 < steps)
    def _():
        start_chunks(lists, length, stride, step + 1, steps, starts, rows_hbm, buffers.at[1 - slot], sems.at[1 - slot])

    pltpu.make_async_copy(buffers.at[slot], buffers.at[slot], sems.at[slot]).wait()
    lanes = lax.broadcasted_iota(jnp.int32, (chunk, width), 1) + bases[step]
    within = lax.broadcasted_iota(jnp.int32, (chunk, width), 0)

    def mark(shifted):
        def one(k, carry):
            begin = starts[k * steps + step] // 16 * 16 + shifted
            at = jnp.minimum(begin, length - chunk)
            ids = ids_ref[pl.ds(pl.multiple_of(k * length + at, 16), chunk), :]
            same = (ids == lanes) & (within >= begin - at)
            hot[pl.ds(pl.multiple_of(k * chunk, 16), chunk), :] = same.astype(WIDE).astype(LOW)
            return carry

        lax.fori_loop(0, lists, one, 0)

    down = lax.broadcasted_iota(jnp.int32, (width, lists * chunk), 0) + bases[step]
    wide_hot[...] = (down == near_ref[0]).astype(WIDE).astype(LOW)
    grad[...] = jnp.dot(wide_hot[...], buffers[slot], preferred_element_type=WIDE)

    def more(p, carry):
        mark(p * chunk)

        def one(k, inner):
            begin = starts[k * steps + step] // 16 * 16 + p * chunk
            at = jnp.minimum(begin, length - chunk)
            src = rows_hbm.at[pl.ds(pl.multiple_of(k * stride + at, 16), chunk)]
            pltpu.make_async_copy(
                src, spare.at[pl.ds(pl.multiple_of(k * chunk, 16), chunk)], sems.at[2]
            ).start()
            return inner

        lax.fori_loop(0, lists, one, 0)
        pltpu.make_async_copy(spare, spare, sems.at[2]).wait()
        grad[...] += contract_rows(hot[...], spare[...])
        return carry

    lax.fori_loop(1, passes[step], more, 0)


def table_square_kernel(lists, length, steps, starts, passes, bases, rows_hbm, ids_ref, near_ref, out, buffers, hot, wide_hot, grad, sems):
    step = pl.program_id(0)
    block_grad(lists, length, steps, step, starts, passes, bases, rows_hbm, ids_ref, near_ref, buffers, hot, wide_hot, grad, sems)
    part = jnp.sum((grad[...] * grad[...]).reshape(-1, 8, D), axis=0)
    part = jnp.where(passes[step] > 0, part, 0.0)

    @pl.when(step == 0)
    def _():
        out[...] = part

    @pl.when(step > 0)
    def _():
        out[...] += part


def table_adam_kernel(
    lists, length, steps, rate, decay, starts, passes, bases, clip, rows_hbm, ids_ref, near_ref, w, m, v, w_new, m_new, v_new, low, buffers, hot, wide_hot, grad, sems
):
    step = pl.program_id(0)
    block_grad(lists, length, steps, step, starts, passes, bases, rows_hbm, ids_ref, near_ref, buffers, hot, wide_hot, grad, sems)
    weight, mom, sec = adam_update(w[...], grad[...] * clip[0], m[...], v[...], rate, decay)
    w_new[...] = weight
    m_new[...] = mom
    v_new[...] = sec
    low[...] = weight.astype(LOW)


def table_scratch(lists, width):
    chunk = chunk_of(lists)
    return [
        pltpu.VMEM((3, lists * chunk, D), LOW),
        pltpu.VMEM((lists * chunk, width), LOW),
        pltpu.VMEM((width, lists * chunk), LOW),
        pltpu.VMEM((width, D), WIDE),
        pltpu.SemaphoreType.DMA((3,)),
    ]


def chunk_scalars(ids_sorted, bases, width):
    chunk = chunk_of(ids_sorted.shape[0])
    edges = bases[None, :, None]
    starts = jnp.sum((ids_sorted[:, None, :] < edges).astype(jnp.int32), axis=-1)
    ends = jnp.sum((ids_sorted[:, None, :] < edges + width).astype(jnp.int32), axis=-1)
    passes = jnp.max((ends - starts // 16 * 16 + chunk - 1) // chunk, axis=0)
    lists, length = ids_sorted.shape
    groups = length // 16
    begin = (starts // 16).T
    at = jnp.minimum(begin, groups - chunk // 16)
    by_group = ids_sorted.reshape(lists, groups, 16).transpose(1, 0, 2).reshape(groups, -1)
    widen = jnp.arange(lists * 16)[None, :] // 16 == jnp.arange(lists)[:, None]
    both = jnp.concatenate([at, begin], axis=0).astype(LOW)
    both = jnp.dot(both, widen.astype(LOW), preferred_element_type=WIDE).astype(jnp.int32)
    both = lax.optimization_barrier(both)
    steps = begin.shape[0]
    pieces = []
    for k in range(chunk // 16):
        wanted = both[:steps] + k
        found = jnp.zeros(wanted.shape, jnp.int32)
        for g in range(groups):
            found = jnp.where(wanted == g, by_group[g][None], found)
        found = jnp.where(wanted >= both[steps:], found, -(1 << 30))
        pieces.append(lax.optimization_barrier(found).reshape(-1, lists, 16))
    near = jnp.stack(pieces, axis=2).reshape(begin.shape[0], 1, -1)
    return starts.reshape(-1), jnp.maximum(passes, 1), near


def table_square(ids_sorted, ids_column, rows_flat, rank, ranks, vocab_rows):
    lists, length = ids_sorted.shape
    width = block_of(vocab_rows)
    total = vocab_rows // width
    steps = -(-total // ranks)
    blocks = rank + ranks * jnp.arange(steps, dtype=jnp.int32)
    bases = blocks * width
    starts, passes, near = chunk_scalars(ids_sorted, bases, width)
    passes = jnp.where(blocks < total, passes, 0)
    out = pl.pallas_call(
        functools.partial(table_square_kernel, lists, length, steps),
        grid_spec=pltpu.PrefetchScalarGridSpec(
            num_scalar_prefetch=3,
            grid=(steps,),
            in_specs=[
                pl.BlockSpec(memory_space=pl.ANY),
                pl.BlockSpec(
                    (lists * length, 1), lambda g, *_: (0, 0), pipeline_mode=pl.Buffered(1)
                ),
                pl.BlockSpec((1, 1, near.shape[2]), lambda g, *_: (g, 0, 0)),
            ],
            out_specs=pl.BlockSpec((8, D), lambda g, *_: (0, 0)),
            scratch_shapes=table_scratch(lists, width),
        ),
        out_shape=jax.ShapeDtypeStruct((8, D), WIDE),
        compiler_params=pltpu.CompilerParams(vmem_limit_bytes=56 << 20),
        name="table_square",
    )(starts, passes, bases, rows_flat, ids_column, near)
    return jnp.sum(out)


def table_adam(ids_sorted, ids_column, rows_flat, clip_scale, table, mom, sec, rate, decay):
    lists, length = ids_sorted.shape
    vocab_rows = table.shape[0]
    width = block_of(vocab_rows)
    steps = vocab_rows // width
    bases = jnp.arange(steps, dtype=jnp.int32) * width
    starts, passes, near = chunk_scalars(ids_sorted, bases, width)
    block = pl.BlockSpec((width, D), lambda g, *_: (g, 0))
    wide = jax.ShapeDtypeStruct(table.shape, WIDE)
    return pl.pallas_call(
        functools.partial(table_adam_kernel, lists, length, steps, rate, decay),
        grid_spec=pltpu.PrefetchScalarGridSpec(
            num_scalar_prefetch=4,
            grid=(steps,),
            in_specs=[
                pl.BlockSpec(memory_space=pl.ANY),
                pl.BlockSpec(
                    (lists * length, 1), lambda g, *_: (0, 0), pipeline_mode=pl.Buffered(1)
                ),
                pl.BlockSpec((1, 1, near.shape[2]), lambda g, *_: (g, 0, 0)),
                block,
                block,
                block,
            ],
            out_specs=[block] * 4,
            scratch_shapes=table_scratch(lists, width),
        ),
        out_shape=[wide, wide, wide, jax.ShapeDtypeStruct(table.shape, LOW)],
        compiler_params=pltpu.CompilerParams(vmem_limit_bytes=60 << 20),
        cost_estimate=pl.CostEstimate(
            flops=steps * 2 * width * lists * chunk_of(lists) * D,
            bytes_accessed=table.size * 26,
            transcendentals=table.size,
        ),
        name="table_adam",
    )(starts, passes, bases, clip_scale.reshape(1), rows_flat, ids_column, near, table, mom, sec)


HEAD_BLOCK = 800


def head_adam_kernel(rate, decay, clip, grad, w, m, v, w_new, m_new, v_new, low):
    scaled = grad[...].astype(WIDE) * clip[0]
    weight, mom, sec = adam_update(w[...], scaled, m[...], v[...], rate, decay)
    w_new[...] = weight
    m_new[...] = mom
    v_new[...] = sec
    low[...] = weight.astype(LOW)


def head_adam(grad, clip_scale, head, mom, sec, rate, decay):
    vocab = head.shape[1]
    block = pl.BlockSpec((HEAD_BLOCK, D), lambda g, *_: (g, 0))
    wide = jax.ShapeDtypeStruct((vocab, D), WIDE)
    results = pl.pallas_call(
        functools.partial(head_adam_kernel, rate, decay),
        grid_spec=pltpu.PrefetchScalarGridSpec(
            num_scalar_prefetch=1,
            grid=(-(-vocab // HEAD_BLOCK),),
            in_specs=[block] * 4,
            out_specs=[block] * 4,
        ),
        out_shape=[wide, wide, wide, jax.ShapeDtypeStruct((vocab, D), LOW)],
        compiler_params=pltpu.CompilerParams(vmem_limit_bytes=56 << 20),
        cost_estimate=pl.CostEstimate(
            flops=head.size * 20, bytes_accessed=head.size * 28, transcendentals=head.size
        ),
        name="head_adam",
    )(clip_scale.reshape(1), grad, head.T, mom.T, sec.T)
    return [item.T for item in results]


def small_gather_kernel(axes, sizes, *refs):
    n = (len(refs) - 2) // 2
    blocks, outs, send, recv = refs[:n], refs[n : 2 * n], refs[2 * n], refs[2 * n + 1]
    mine = [lax.axis_index(axis) for axis in axes]
    slot = 0
    for index, size in zip(mine, sizes):
        slot = slot * size + index
    offsets = [()]
    for size in sizes:
        offsets = [o + (k,) for o in offsets for k in range(size)]
    peers = [
        {axis: (index + k) % size for axis, index, size, k in zip(axes, mine, sizes, offset)}
        for offset in offsets[1:]
    ]
    barrier = pltpu.get_barrier_semaphore()
    for peer in peers:
        pl.semaphore_signal(barrier, inc=1, device_id=peer, device_id_type=MESH)
    pl.semaphore_wait(barrier, len(peers))
    copies = []
    for m in range(n):
        for k, peer in enumerate(peers):
            copy = pltpu.make_async_remote_copy(
                src_ref=blocks[m],
                dst_ref=outs[m].at[slot],
                send_sem=send.at[m * len(peers) + k],
                recv_sem=recv.at[m * len(peers) + k],
                device_id=peer,
                device_id_type=MESH,
            )
            copy.start()
            copies.append(copy)
        outs[m][slot] = blocks[m][...]
    for copy in copies:
        copy.wait()


def small_gather(blocks, axes, identity):
    sizes = [lax.axis_size(axis) for axis in axes]
    count = math.prod(sizes)
    copies = (count - 1) * len(blocks)
    whole = pl.BlockSpec(memory_space=pltpu.VMEM)
    return pl.pallas_call(
        functools.partial(small_gather_kernel, axes, sizes),
        out_shape=[jax.ShapeDtypeStruct((count,) + b.shape, b.dtype) for b in blocks],
        in_specs=[whole] * len(blocks),
        out_specs=[whole] * len(blocks),
        scratch_shapes=[pltpu.SemaphoreType.DMA((copies,))] * 2,
        compiler_params=pltpu.CompilerParams(collective_id=identity, has_side_effects=True),
        name=f"small_gather_{identity}",
    )(*blocks)


def per_device(
    token_ids,
    next_ids,
    seq_lengths,
    embedding,
    embedding_mom,
    embedding_sec,
    head_table,
    head_mom,
    head_sec,
    w_qkv,
    qkv_mom,
    qkv_sec,
    w_out,
    out_mom,
    out_sec,
    w_gateup,
    gateup_mom,
    gateup_sec,
    w_down,
    down_mom,
    down_sec,
    gains,
    gains_mom,
    gains_sec,
):
    planes = lax.axis_size("fsdp")
    replicas = lax.axis_size("dp")
    first = lax.axis_index("section") == 0
    first_f = first.astype(WIDE)
    me = lax.axis_index("fsdp")
    token_total = jnp.sum(seq_lengths).astype(WIDE)
    tokens = MB * ROW

    my_ids = jnp.stack([token_ids.reshape(-1), next_ids.reshape(-1)])
    ids_all, gains_all = small_gather([my_ids, gains[0]], ("dp", "fsdp"), 3)
    ids_all = ids_all.reshape(replicas, planes, 2, tokens)
    gains_full = gains_all[:planes].transpose(1, 0, 2).reshape(3, D)
    gains_full = lax.optimization_barrier(gains_full.astype(LOW)).astype(WIDE)
    group_ids = pick(ids_all, lax.axis_index("dp"))
    rel_ids = jnp.stack([pick(group_ids, (me - step) % planes) for step in range(planes)])
    my_kind = jnp.where(first, rel_ids[:, 0], rel_ids[:, 1])
    vocab_rows = embedding.shape[0]
    vocab_start = me * vocab_rows
    local = my_kind - vocab_start
    inside = (local >= 0) & (local < vocab_rows)
    found = jnp.take(embedding, jnp.clip(local, 0, vocab_rows - 1), axis=0)
    found = lax.optimization_barrier(jnp.where(inside[..., None], found, 0.0).astype(LOW))
    looked = found[0].astype(WIDE)
    for step in range(1, planes):
        looked = looked + shift(found[step], "fsdp", planes - step).astype(WIDE)
    next_embed = swap(looked.astype(LOW), "section", 1).astype(WIDE)

    lists = ids_all.transpose(2, 0, 1, 3).reshape(-1, tokens) - vocab_start
    place = jnp.arange(tokens)
    before = (lists[:, None, :] < lists[:, :, None]) | (
        (lists[:, None, :] == lists[:, :, None]) & (place[None, None, :] < place[None, :, None])
    )
    ranks = jnp.sum(before.astype(jnp.int32), axis=-1)
    sorted_ids = jnp.sum(
        jnp.where(ranks[:, None, :] == place[None, :, None], lists[:, None, :], 0), axis=-1
    )
    own_list = (
        lax.axis_index("section") * replicas + lax.axis_index("dp")
    ) * planes + me
    arrange = (pick(ranks, own_list)[None, :] == place[:, None]).astype(LOW)

    full = gather_weights(
        planes,
        replicas,
        [w_qkv[0].astype(LOW), w_out[0].astype(LOW), w_gateup[0].astype(LOW), w_down[0].astype(LOW)],
    )
    layer_weights = (full[0], full[1], full[2], full[3], gains_full[0], gains_full[1])
    head_gain = gains_full[2]

    first_out, _ = layer_fwd(looked, layer_weights)
    middle = swap(first_out.astype(LOW), "section", 1).astype(WIDE)
    layer_in = jnp.where(first, looked, middle)
    layer_out, saved = layer_fwd(layer_in, layer_weights)
    final_state = norm_fwd(layer_out, head_gain)
    arrived = swap(final_state.astype(LOW), "section", 1).astype(WIDE)
    merged_in = jnp.where(first, arrived + next_embed, layer_out)
    head_in = norm_fwd(merged_in, head_gain)

    lengths = seq_lengths.reshape(replicas, planes, MB)[lax.axis_index("dp")]
    lengths = jnp.stack([pick(lengths, (me - step) % planes) for step in range(planes)])
    targets_main = rel_ids[:, 1].reshape(planes, MB, ROW)
    shifted = jnp.concatenate([targets_main[..., 1:], targets_main[..., :1]], axis=-1)
    targets = jnp.where(first, shifted, targets_main)
    limit = lengths - first.astype(jnp.int32)
    positions = jnp.arange(ROW, dtype=jnp.int32)
    weights_tok = (positions < limit[..., None]).astype(WIDE) * jnp.where(first, MTP_WEIGHT, 1.0)
    left = [saved[0], saved[6], saved[8]]
    left_all = spread(
        lambda index: jnp.concatenate(left + [sub_quarter(saved[10], planes, index)], axis=1)
    )
    loss_part, mine, theirs, grad_in = head_pass(
        head_in.astype(LOW),
        targets.reshape(-1),
        weights_tok.reshape(-1),
        head_table.T,
        vocab_start,
        token_total,
    )
    sorted_ids, loss_part = lax.optimization_barrier((sorted_ids, loss_part))
    merged_grad, mtp_gain = norm_back(merged_in, head_gain, grad_in)
    merged_low = merged_grad.astype(LOW)
    sent = swap(merged_low, "section", 1).astype(WIDE)
    top_grad, top_gain = norm_back(layer_out, head_gain, grad_in + sent)
    head_gain_grad = jnp.where(first, mtp_gain, top_gain)
    half = add_low(mine, swap(theirs, "section", 1))
    top_grad, left_all, half = lax.optimization_barrier((top_grad, left_all, half))
    below, _, _ = layer_back(layer_in, layer_weights, saved, top_grad)
    side = half.shape[0] // 2
    piece_a, piece_b = keep_half(half[:side], 1), keep_half(half[side:], 2)
    below, piece_a, piece_b = lax.optimization_barrier((below.astype(LOW), piece_a, piece_b))
    upstream = jnp.where(first, swap(below, "section", 1).astype(WIDE), top_grad)
    grad_inputs, right, gain_parts = layer_back(layer_in, layer_weights, saved, upstream)
    piece_a, piece_b = keep_half(piece_a, 2), keep_half(piece_b, 1)
    grad_inputs, piece_a, piece_b = lax.optimization_barrier((grad_inputs, piece_a, piece_b))

    grad_packed, after_low, grad_gu, upstream_low = right
    tops = spread(lambda index: upstream_low)
    early = spread(lambda index: quarter(grad_gu, index))
    late = spread(
        lambda index: jnp.concatenate([quarter(after_low, index), quarter(grad_packed, index)], axis=1)
    )
    cut = D // SHARE
    parts = [
        contract_rows(left_all[:, 2 * D : 3 * D], early),
        contract_rows(left_all[:, 3 * D :], tops),
        contract_rows(left_all[:, :D], late[:, cut:]),
        contract_rows(left_all[:, D : 2 * D], late[:, :cut]),
    ]
    parts = [part.astype(LOW) for part in parts]
    gains_grad = jnp.stack([gain_parts[0], gain_parts[1], head_gain_grad])

    row_grads = jnp.where(first, grad_inputs.astype(LOW), sent.astype(LOW))
    row_grads = jnp.dot(arrange, row_grads, preferred_element_type=WIDE).astype(LOW)
    row_grads = jnp.concatenate(
        [row_grads, gains_grad.astype(LOW), jnp.zeros((13, D), LOW)], axis=0
    )
    rows_all, grad_head, slots = exchange(planes, row_grads, (piece_a, piece_b), parts)
    rows_flat = rows_all.reshape(-1, D)
    gains_grad = pick(rows_all[:, :, :, tokens : tokens + 3], lax.axis_index("section"))
    gains_grad = jnp.sum(gains_grad.astype(WIDE), axis=(0, 1))
    gains_grad = lax.dynamic_slice_in_dim(gains_grad, me * (D // planes), D // planes, 1)
    ids_column = sorted_ids.reshape(-1, 1)

    def square(item):
        wide = item.astype(WIDE)
        return jnp.sum(wide * wide)

    shards = []
    for part, slot in zip(parts, slots):
        mine = pick(part.reshape((planes,) + slot.shape[1:]), me).astype(WIDE)
        shards.append((mine + jnp.sum(slot.astype(WIDE), axis=0)).astype(LOW))
    group = lax.axis_index("section") * replicas + lax.axis_index("dp")
    squares = table_square(sorted_ids, ids_column, rows_flat, group, 2 * replicas, vocab_rows)
    for item in shards + [piece_a, piece_b]:
        squares = squares + square(item)
    squares = squares + square(gains_grad) / replicas
    totals = jnp.stack([squares, loss_part / planes])[:, None] * jnp.ones((1, 128), WIDE)
    totals = jnp.sum(small_gather([totals], ("section", "dp", "fsdp"), 4)[0], axis=0)[:, 0]
    grad_norm = jnp.sqrt(totals[0])
    loss_total = totals[1]
    clip_scale = CLIP / jnp.maximum(grad_norm, CLIP)

    shards, clip_scale = lax.optimization_barrier((shards, clip_scale))
    widths = [0, 2 * D, 3 * D, 3 * D + 3 * cut, 4 * D]
    packed = jnp.concatenate(shards, axis=1)
    rank = plane_rank()
    others = [packed] + [swap(packed, "dp", mask) for mask in range(1, SHARE)]
    layer_grads = [
        in_order([other[:, lo:hi] for other in others], rank, 0 if index == 1 else 1).astype(WIDE)
        for index, (lo, hi) in enumerate(zip(widths[:-1], widths[1:]))
    ]
    params = (w_qkv[0], w_out[0], w_gateup[0], w_down[0], gains[0])
    grads_all = (
        layer_grads[2],
        layer_grads[3],
        layer_grads[0],
        layer_grads[1],
        gains_grad,
    )
    moments = (
        (qkv_mom[0], qkv_sec[0]),
        (out_mom[0], out_sec[0]),
        (gateup_mom[0], gateup_sec[0]),
        (down_mom[0], down_sec[0]),
        (gains_mom[0], gains_sec[0]),
    )
    rates = (0.03, 0.12, 0.03, 0.03, 0.6)
    decays = (0.1, 0.1, 0.1, 0.1, 0.0)
    outputs = [loss_total, token_total, grad_norm]
    outputs += table_adam(
        sorted_ids,
        ids_column,
        rows_flat,
        clip_scale,
        embedding,
        embedding_mom,
        embedding_sec,
        0.6,
        0.1,
    )
    outputs += head_adam(grad_head, clip_scale, head_table, head_mom, head_sec, 0.03, 0.1)
    for index in range(5):
        weight_new, mom_new, sec_new = adam_update(
            params[index],
            grads_all[index] * clip_scale,
            moments[index][0],
            moments[index][1],
            rates[index],
            decays[index],
        )
        outputs.extend([weight_new[None], mom_new[None], sec_new[None]])
        if index < 4:
            outputs.append(weight_new.astype(LOW)[None])
    return tuple(outputs)


def solution(mesh):
    placed = (
        P(("dp", "fsdp"), None),
        P(("dp", "fsdp"), None),
        P(),
        P("fsdp", None),
        P("fsdp", None),
        P("fsdp", None),
        P(None, "fsdp"),
        P(None, "fsdp"),
        P(None, "fsdp"),
        P("section", "fsdp", None),
        P("section", "fsdp", None),
        P("section", "fsdp", None),
        P("section", "fsdp", None),
        P("section", "fsdp", None),
        P("section", "fsdp", None),
        P("section", "fsdp", None),
        P("section", "fsdp", None),
        P("section", "fsdp", None),
        P("section", "fsdp", None),
        P("section", "fsdp", None),
        P("section", "fsdp", None),
        P("section", None, "fsdp"),
        P("section", None, "fsdp"),
        P("section", None, "fsdp"),
    )
    return jax.shard_map(
        per_device,
        mesh=mesh,
        in_specs=placed,
        out_specs=(
            P(),
            P(),
            P(),
            P("fsdp", None),
            P("fsdp", None),
            P("fsdp", None),
            P("fsdp", None),
            P(None, "fsdp"),
            P(None, "fsdp"),
            P(None, "fsdp"),
            P(None, "fsdp"),
            P("section", "fsdp", None),
            P("section", "fsdp", None),
            P("section", "fsdp", None),
            P("section", "fsdp", None),
            P("section", "fsdp", None),
            P("section", "fsdp", None),
            P("section", "fsdp", None),
            P("section", "fsdp", None),
            P("section", "fsdp", None),
            P("section", "fsdp", None),
            P("section", "fsdp", None),
            P("section", "fsdp", None),
            P("section", "fsdp", None),
            P("section", "fsdp", None),
            P("section", "fsdp", None),
            P("section", "fsdp", None),
            P("section", None, "fsdp"),
            P("section", None, "fsdp"),
            P("section", None, "fsdp"),
        ),
        check_vma=False,
    )
```

```python
import functools
import math

import jax
import jax.numpy as jnp
from jax import lax
from jax.experimental import pallas as pl
from jax.experimental.pallas import tpu as pltpu
from jax.sharding import PartitionSpec as P

D = 768
HEADS = 12
HEAD_DIM = 64
FF = 3072
ROW = 128
MB = 2
STEP_COUNT = 10
SHARE = 4


EPS = 1e-05
MTP_WEIGHT = 0.3
CLIP = 0.01
BETA1 = 0.9
BETA2 = 0.95
ADAM_EPS = 1e-08
LOW = jnp.bfloat16
WIDE = jnp.float32

AHEAD = 2
MESH = pl.DeviceIdType.MESH

def weights_kernel(planes, units, rows, *refs):
    n = len(rows)
    own, full = refs[:n], refs[n : 2 * n]
    send, recv, local = refs[2 * n :]
    z = lax.axis_index("fsdp")
    i = lax.axis_index("dp")
    x, y = i % 2, i // 2
    q = i
    xn, yn = i + 1 - 2 * x, (i + 2) % 4
    near, far = z + 1 - 2 * (z % 2), planes - 1 - z
    beyond = planes - 1 - near
    to_x, to_y, to_near, to_far = {"dp": xn}, {"dp": yn}, {"fsdp": near}, {"fsdp": far}
    barrier = pltpu.get_barrier_semaphore()
    for device in (to_x, to_y, to_near, to_far):
        pl.semaphore_signal(barrier, inc=1, device_id=device, device_id_type=MESH)
    pl.semaphore_wait(barrier, 4)
    keep = []
    for m in range(n):
        c = pltpu.make_async_copy(
            own[m], full[m].at[pl.ds(pl.multiple_of(z * rows[m], 16), rows[m]), :], local.at[m]
        )
        c.start()
        keep.append(c)
    started = []

    def put(src, dst, k, device):
        copy = pltpu.make_async_remote_copy(
            src_ref=src,
            dst_ref=dst,
            send_sem=send.at[k],
            recv_sem=recv.at[k],
            device_id=device,
            device_id_type=MESH,
        )
        copy.start()
        started.append(copy)
        return copy

    def block(u, plane, part):
        m, cols, _ = units[u]
        r = rows[m] // 4
        return full[m].at[pl.ds(pl.multiple_of(plane * rows[m] + part * r, 16), r), pl.ds(*cols)]

    sources = (near, far, beyond)
    zs, seconds, thirds = {}, {}, []
    total = len(units)

    def first(u):
        m, cols, _ = units[u]
        r = rows[m] // 4
        src = own[m].at[pl.ds(pl.multiple_of(q * r, 16), r), pl.ds(*cols)]
        zs[u, 0] = put(src, block(u, z, q), 12 * u, to_near)
        zs[u, 1] = put(src, block(u, z, q), 12 * u + 1, to_far)

    def onward(u):
        zs[u, 1].wait_recv()
        zs[u, 2] = put(block(u, far, q), block(u, far, q), 12 * u + 2, to_near)

    def second(u, j):
        if j != 1:
            zs[u, j].wait_recv()
        b = block(u, sources[j], q)
        seconds[u, j] = put(b, b, 12 * u + 3 + j, to_y if units[u][2] else to_x)

    def third(u, j):
        seconds[u, j].wait_recv()
        order = units[u][2]
        for w, part in enumerate((q, yn if order else xn)):
            b = block(u, sources[j], part)
            thirds.append(put(b, b, 12 * u + 6 + 2 * j + w, to_x if order else to_y))

    pairs = [(u, u + 1) for u in range(0, total, 2)]
    for ahead in range(AHEAD):
        for u in pairs[ahead]:
            first(u)
    for t in range(len(pairs) + 2):
        if t < len(pairs):
            for u in pairs[t]:
                onward(u)
            if t + AHEAD < len(pairs):
                for u in pairs[t + AHEAD]:
                    first(u)
            for j in (0, 1):
                for u in pairs[t]:
                    second(u, j)
        if 1 <= t <= len(pairs):
            for u in pairs[t - 1]:
                second(u, 2)
            for j in (0, 1):
                for u in pairs[t - 1]:
                    third(u, j)
        if t >= 2:
            for u in pairs[t - 2]:
                third(u, 2)
    for c in thirds:
        c.wait_recv()
    for c in started:
        c.wait_send()
    for c in keep:
        c.wait()


def gather_weights(planes, replicas, shards):
    rows = [w.shape[0] for w in shards]
    if planes != 4 or replicas != 4 or any(r % (SHARE * 16) for r in rows):
        return [lax.all_gather(w, "fsdp", axis=0, tiled=True) for w in shards]
    units = []
    for m, w in enumerate(shards):
        width = w.shape[1]
        parts = 4 if width > 4096 else 2
        step = width // parts
        for p in range(parts):
            units.append((m, (p * step, step), p % 2))
    copies = len(units) * 12
    return pl.pallas_call(
        functools.partial(weights_kernel, planes, units, rows),
        out_shape=[jax.ShapeDtypeStruct((planes * w.shape[0], w.shape[1]), w.dtype) for w in shards],
        in_specs=[pl.BlockSpec(memory_space=pltpu.VMEM)] * len(shards),
        out_specs=[pl.BlockSpec(memory_space=pl.ANY)] * len(shards),
        scratch_shapes=[pltpu.SemaphoreType.DMA((copies,)), pltpu.SemaphoreType.DMA((copies,)), pltpu.SemaphoreType.DMA((len(shards),))],
        compiler_params=pltpu.CompilerParams(collective_id=1, has_side_effects=True),
        name="gather_weights",
    )(*shards)


def norm_fwd(values, scale_gain):
    inverse = lax.rsqrt(jnp.mean(values * values, axis=-1, keepdims=True) + EPS)
    return values * inverse * scale_gain


def norm_back(values, scale_gain, upstream):
    _, pullback = jax.vjp(norm_fwd, values, scale_gain)
    return pullback(upstream)


def rope_tables(row_count, head_width):
    half_width = head_width // 2
    position = jnp.arange(row_count, dtype=jnp.float32)[:, None]
    frequency = 10000.0 ** (-jnp.arange(half_width, dtype=jnp.float32) / half_width)
    angles = position * frequency[None, :]
    return (jnp.cos(angles), jnp.sin(angles))


def rotate(values, cosine, sine_table):
    half_width = values.shape[-1] // 2
    first, second = (values[..., :half_width], values[..., half_width:])
    return jnp.concatenate(
        [first * cosine - second * sine_table, second * cosine + first * sine_table], axis=-1
    )


def contract_rows(left, right):
    return lax.dot_general(
        left, right, (((0,), (0,)), ((), ())), preferred_element_type=jnp.float32
    )


def contract_cols(left, right):
    return lax.dot_general(
        left, right, (((1,), (1,)), ((), ())), preferred_element_type=jnp.float32
    )


def swiglu(gate_up):
    return jax.nn.silu(gate_up[:, :FF]) * gate_up[:, FF:]


def shift(block, axis, distance):
    count = lax.axis_size(axis)
    return lax.ppermute(block, axis, [(i, (i + distance) % count) for i in range(count)])


def swap(block, axis, mask):
    count = lax.axis_size(axis)
    return lax.ppermute(block, axis, [(i, i ^ mask) for i in range(count)])


def pick(array, index, axis=0):
    return lax.dynamic_index_in_dim(array, index, axis, keepdims=False)


def layer_fwd(inputs, weights):
    w_qkv, w_out, w_gateup, w_down, attn_gain, ffn_gain = weights
    normed = norm_fwd(inputs, attn_gain).astype(LOW)
    packed = jnp.dot(normed, w_qkv, preferred_element_type=WIDE)
    split = packed.reshape(MB, ROW, 3, HEADS, HEAD_DIM).transpose(2, 0, 3, 1, 4)
    split = split.reshape(3, MB * HEADS, ROW, HEAD_DIM)
    cosine, sine_table = rope_tables(ROW, HEAD_DIM)
    queries = rotate(split[0], cosine, sine_table).astype(LOW)
    keys_rot = rotate(split[1], cosine, sine_table).astype(LOW)
    values_low = split[2].astype(LOW)
    scores = jnp.einsum(
        "hqd,hkd->hqk", queries, keys_rot, preferred_element_type=WIDE
    ) * HEAD_DIM ** (-0.5)
    position = jnp.arange(ROW)
    causal = position[:, None] >= position[None, :]
    scores = jnp.where(causal[None], scores, -1e30)
    shifted = jnp.exp(scores - jnp.max(scores, axis=-1, keepdims=True))
    probs = shifted / jnp.sum(shifted, axis=-1, keepdims=True)
    probs_low = probs.astype(LOW)
    mixed = jnp.einsum("hqk,hkd->hqd", probs_low, values_low, preferred_element_type=WIDE)
    mixed = mixed.reshape(MB, HEADS, ROW, HEAD_DIM).transpose(0, 2, 1, 3)
    mixed_low = mixed.reshape(MB * ROW, D).astype(LOW)
    after_attn = inputs + jnp.dot(mixed_low, w_out, preferred_element_type=WIDE)
    normed_ffn = norm_fwd(after_attn, ffn_gain).astype(LOW)
    gate_up = jnp.dot(normed_ffn, w_gateup, preferred_element_type=WIDE)
    hidden = swiglu(gate_up).astype(LOW)
    output = after_attn + jnp.dot(hidden, w_down, preferred_element_type=WIDE)
    saved = (
        normed,
        queries,
        keys_rot,
        values_low,
        probs,
        probs_low,
        mixed_low,
        after_attn,
        normed_ffn,
        gate_up,
        hidden,
    )
    return (output, saved)


def layer_back(inputs, weights, saved, upstream):
    w_qkv, w_out, w_gateup, w_down, attn_gain, ffn_gain = weights
    (
        normed,
        queries,
        keys_rot,
        values_low,
        probs,
        probs_low,
        mixed_low,
        after_attn,
        normed_ffn,
        gate_up,
        hidden,
    ) = saved
    upstream_low = upstream.astype(LOW)
    grad_hidden = contract_cols(upstream_low, w_down)
    _, pullback = jax.vjp(swiglu, gate_up)
    grad_gu = pullback(grad_hidden)[0].astype(LOW)
    grad_nffn = contract_cols(grad_gu, w_gateup)
    back_ffn, grad_ffn_gain = norm_back(after_attn, ffn_gain, grad_nffn)
    grad_after = upstream + back_ffn
    after_low = grad_after.astype(LOW)
    grad_mixed = contract_cols(after_low, w_out).astype(LOW)
    grad_mixed = grad_mixed.reshape(MB, ROW, HEADS, HEAD_DIM).transpose(0, 2, 1, 3)
    grad_mixed = grad_mixed.reshape(MB * HEADS, ROW, HEAD_DIM)
    grad_probs = jnp.einsum("hqd,hkd->hqk", grad_mixed, values_low, preferred_element_type=WIDE)
    grad_values = jnp.einsum("hqk,hqd->hkd", probs_low, grad_mixed, preferred_element_type=WIDE)
    grad_scores = probs * (grad_probs - jnp.sum(probs * grad_probs, axis=-1, keepdims=True))
    grad_scores = grad_scores.astype(LOW)
    scale_attn = HEAD_DIM ** (-0.5)
    grad_query = (
        jnp.einsum("hqk,hkd->hqd", grad_scores, keys_rot, preferred_element_type=WIDE)
        * scale_attn
    )
    grad_key = (
        jnp.einsum("hqk,hqd->hkd", grad_scores, queries, preferred_element_type=WIDE)
        * scale_attn
    )
    cosine, sine_table = rope_tables(ROW, HEAD_DIM)
    grad_query = rotate(grad_query, cosine, -sine_table)
    grad_key = rotate(grad_key, cosine, -sine_table)
    grad_packed = jnp.stack([grad_query, grad_key, grad_values]).astype(LOW)
    grad_packed = grad_packed.reshape(3, MB, HEADS, ROW, HEAD_DIM).transpose(1, 3, 0, 2, 4)
    grad_packed = grad_packed.reshape(MB * ROW, 3 * D)
    grad_normed = contract_cols(grad_packed, w_qkv)
    back_attn, grad_attn_gain = norm_back(inputs, attn_gain, grad_normed)
    grad_inputs = grad_after + back_attn
    return (
        grad_inputs,
        (grad_packed, after_low, grad_gu, upstream_low),
        (grad_attn_gain, grad_ffn_gain),
    )


def plane_rank():
    return lax.axis_index("dp")


def quarter(block, index):
    width = block.shape[1] // SHARE
    return lax.dynamic_slice_in_dim(block, index * width, width, 1)


def sub_quarter(block, planes, index):
    rows, width = block.shape
    split = block.reshape(rows, planes, SHARE, width // planes // SHARE)
    return lax.dynamic_index_in_dim(split, index, 2, keepdims=False).reshape(rows, -1)


def spread(make):
    rank = plane_rank()
    own = make(rank)
    rows = own.shape[0]
    full = lax.dynamic_update_slice(jnp.zeros((SHARE * rows, own.shape[1]), LOW), own, (0, 0))
    for mask in range(1, SHARE):
        piece = swap(make(rank ^ mask), "dp", mask)
        full = lax.dynamic_update_slice(full, piece, (mask * rows, 0))
    return full


def in_order(pieces, rank, axis):
    low = rank % 2 == 0
    top = rank // 2 == 0
    pairs = []
    for k in (0, 2):
        pairs.append(
            (jnp.where(low, pieces[k], pieces[k + 1]), jnp.where(low, pieces[k + 1], pieces[k]))
        )
    lower = [jnp.where(top, pairs[0][j], pairs[1][j]) for j in range(2)]
    upper = [jnp.where(top, pairs[1][j], pairs[0][j]) for j in range(2)]
    return jnp.concatenate(lower + upper, axis=axis)


def relative_blocks():
    s = lax.axis_index("section")
    i = lax.axis_index("dp")
    x, y = i % 2, i // 2
    blocks = []
    for es in (0, 1):
        for kind in (0, 1):
            for e1 in (0, 1):
                for e2 in (0, 1):
                    a, b = (x, y) if kind == 0 else (y, x)
                    within = ((a + e1) % 2) * 2 + (b + e2) % 2
                    blocks.append(((s + es) % 2) * 8 + kind * 4 + within)
    return jnp.stack(blocks).astype(jnp.int32)


TOKENS = 256


def head_piece(vocab):
    return -(-vocab // 256) * 16


def table_block(vocab, base, h_ref):
    inside = lax.broadcasted_iota(jnp.int32, h_ref.shape, 0) + base < vocab
    return jnp.where(inside, h_ref[...], 0.0).astype(LOW)


def head_scores(vocab, base, table, rows):
    logits = contract_cols(table, rows)
    index = lax.broadcasted_iota(jnp.int32, logits.shape, 0) + base
    return jnp.where(index < vocab, logits, -1e30), index


def head_stats_kernel(vocab, h_ref, rows_ref, target_ref, out):
    step = pl.program_id(0)
    base = step * h_ref.shape[0]
    table = table_block(vocab, base, h_ref)

    @pl.when(step == 0)
    def _():
        out[0:1, :] = jnp.full((1, out.shape[1]), -1e30, WIDE)
        out[1:3, :] = jnp.zeros((2, out.shape[1]), WIDE)

    for c in range(rows_ref.shape[0] // TOKENS):
        span = slice(c * TOKENS, (c + 1) * TOKENS)
        logits, index = head_scores(vocab, base, table, rows_ref[span, :])
        before = out[0:1, span]
        peak = jnp.maximum(before, jnp.max(logits, axis=0, keepdims=True))
        summed = jnp.sum(jnp.exp(logits - peak), axis=0, keepdims=True)
        picked = jnp.sum(jnp.where(index == target_ref[:, span], logits, 0.0), axis=0, keepdims=True)
        out[0:1, span] = peak
        out[1:2, span] = out[1:2, span] * jnp.exp(before - peak) + summed
        out[2:3, span] += picked


def once(shape):
    return pl.BlockSpec(shape, lambda g, *_: (0,) * len(shape), pipeline_mode=pl.Buffered(1))


def head_stats(head, rows, targets):
    vocab, count = head.shape[0], rows.shape[0]
    piece = head_piece(vocab)
    return pl.pallas_call(
        functools.partial(head_stats_kernel, vocab),
        grid=(-(-vocab // piece),),
        in_specs=[pl.BlockSpec((piece, D), lambda g: (g, 0)), once((count, D)), once((1, count))],
        out_specs=pl.BlockSpec((8, count), lambda g: (0, 0)),
        out_shape=jax.ShapeDtypeStruct((8, count), WIDE),
        compiler_params=pltpu.CompilerParams(vmem_limit_bytes=50 << 20),
        cost_estimate=pl.CostEstimate(
            flops=2 * vocab * count * D, bytes_accessed=vocab * D * 4, transcendentals=vocab * count
        ),
        name="head_stats",
    )(head, rows, targets)


def head_grads_kernel(vocab, order, h_ref, rows_ref, target_ref, lse_ref, factor_ref, g_ref, c_ref, flipped, delta):
    step = pl.program_id(0)
    base = order[step] * h_ref.shape[0]
    table = table_block(vocab, base, h_ref)
    flipped[...] = table.astype(WIDE).T.astype(LOW)

    @pl.when(step == 0)
    def _():
        c_ref[...] = jnp.zeros(c_ref.shape, WIDE)

    for c in range(rows_ref.shape[0] // TOKENS):
        span = slice(c * TOKENS, (c + 1) * TOKENS)
        logits, index = head_scores(vocab, base, table, rows_ref[span, :])
        onehot = (index == target_ref[:, span]).astype(WIDE)
        delta[:, span] = (
            (jnp.exp(logits - lse_ref[:, span]) - onehot) * factor_ref[:, span]
        ).astype(LOW)
    g_ref[...] = jnp.dot(delta[...], rows_ref[...], preferred_element_type=WIDE).astype(LOW)
    for c in range(rows_ref.shape[0] // TOKENS):
        span = slice(c * TOKENS, (c + 1) * TOKENS)
        c_ref[:, span] += jnp.dot(flipped[...], delta[:, span], preferred_element_type=WIDE)


def head_grads(head, rows, targets, lse, factor):
    vocab, count = head.shape[0], rows.shape[0]
    piece = head_piece(vocab)
    return pl.pallas_call(
        functools.partial(head_grads_kernel, vocab),
        grid_spec=pltpu.PrefetchScalarGridSpec(
            num_scalar_prefetch=1,
            grid=(16,),
            in_specs=[
                pl.BlockSpec((piece, D), lambda g, order: (order[g], 0)),
                once((count, D)),
                once((1, count)),
                once((1, count)),
                once((1, count)),
            ],
            out_specs=[
                pl.BlockSpec((piece, D), lambda g, order: (g, 0)),
                pl.BlockSpec((D, count), lambda g, order: (0, 0)),
            ],
            scratch_shapes=[pltpu.VMEM((D, piece), LOW), pltpu.VMEM((piece, count), LOW)],
        ),
        out_shape=[
            jax.ShapeDtypeStruct((16 * piece, D), LOW),
            jax.ShapeDtypeStruct((D, count), WIDE),
        ],
        compiler_params=pltpu.CompilerParams(vmem_limit_bytes=56 << 20),
        cost_estimate=pl.CostEstimate(
            flops=6 * vocab * count * D, bytes_accessed=vocab * D * 8, transcendentals=vocab * count
        ),
        name="head_grads",
    )(relative_blocks(), head, rows, targets, lse, factor)


def head_pass(rows_low, targets, weights_tok, head, vocab_start, token_total):
    planes = lax.axis_size("fsdp")
    gathered = jnp.concatenate(
        [rows_low] + [shift(rows_low, "fsdp", step) for step in range(1, planes)], axis=0
    )
    local = targets - vocab_start
    local = jnp.where((local >= 0) & (local < head.shape[0]), local, -1)[None, :]
    stats = head_stats(head, gathered, local)[:3].reshape(3, planes, -1)
    parts = [stats] + [
        jnp.roll(shift(stats, "fsdp", step), step, axis=1) for step in range(1, planes)
    ]
    parts = jnp.stack(parts)
    peak = jnp.max(parts[:, 0], axis=0)
    total = jnp.sum(parts[:, 1] * jnp.exp(parts[:, 0] - peak[None]), axis=0)
    lse = (peak + jnp.log(total)).reshape(-1)
    loss_part = jnp.sum((lse - jnp.sum(parts[:, 2], axis=0).reshape(-1)) * weights_tok)
    factor = weights_tok / token_total
    grad_head, partial = head_grads(head, gathered, local, lse[None, :], factor[None, :])
    partial = partial.T.reshape(planes, -1, D)
    grad_rows = partial[0]
    for step in range(1, planes):
        grad_rows = grad_rows + shift(partial[step].astype(LOW), "fsdp", planes - step).astype(WIDE)
    middle = grad_head.shape[0] // 2
    return (loss_part, grad_head[:middle], grad_head[middle:], grad_rows)


def add_low(one, other):
    return (one.astype(WIDE) + other.astype(WIDE)).astype(LOW)


def keep_half(block, mask):
    half = block.shape[0] // 2
    return add_low(block[:half], swap(block[half:], "dp", mask))


def adam_update(weight, grad, first_mom, second_mom, rate, decay):
    mom_new = BETA1 * first_mom + (1.0 - BETA1) * grad
    sec_new = BETA2 * second_mom + (1.0 - BETA2) * grad * grad
    mom_hat = mom_new / (1.0 - BETA1**STEP_COUNT)
    sec_hat = sec_new / (1.0 - BETA2**STEP_COUNT)
    weight_new = weight - rate * (mom_hat / (jnp.sqrt(sec_hat) + ADAM_EPS) + decay * weight)
    return (weight_new, mom_new, sec_new)


def exchange_kernel(planes, rows_ref, pa, pb, *refs):
    paired = planes == 4
    n = (len(refs) - 7) // (4 if paired else 2)
    parts, rows_all, head, slots = refs[:n], refs[n], refs[n + 1], refs[n + 2 : 2 * n + 2]
    send, recv, core_send, core_recv, local = refs[2 * n + 2 : 2 * n + 7]
    totals, extras = refs[2 * n + 7 : 3 * n + 7], refs[3 * n + 7 :]
    s = lax.axis_index("section")
    i = lax.axis_index("dp")
    z = lax.axis_index("fsdp")
    x, y = i % 2, i // 2
    xn, yn, diag = i + 1 - 2 * x, (i + 2) % 4, 3 - i
    partner = z + 1 - 2 * (z % 2)
    to_x, to_y, to_core = {"dp": xn}, {"dp": yn}, {"section": 1 - s}
    barrier = pltpu.get_barrier_semaphore()
    for device in [to_x, to_y, to_core] + [{"fsdp": (z + k) % planes} for k in range(1, planes)]:
        pl.semaphore_signal(barrier, inc=1, device_id=device, device_id_type=MESH)
    pl.semaphore_wait(barrier, planes + 2)
    counts = [0, 0]
    sent = []

    def put(src, dst, device):
        over = device is to_core
        k = counts[over]
        counts[over] += 1
        copy = pltpu.make_async_remote_copy(
            src_ref=src,
            dst_ref=dst,
            send_sem=(core_send if over else send).at[k],
            recv_sem=(core_recv if over else recv).at[k],
            device_id=device,
            device_id_type=MESH,
        )
        copy.start()
        sent.append(copy)
        return copy

    def take(*copies):
        for copy in copies:
            copy.wait_recv()

    piece = pa.shape[0]
    side = 4 * piece

    def head_a(xx, yy, count):
        return head.at[pl.ds(pl.multiple_of(s * 2 * side + xx * 2 * piece + yy * piece, 16), count)]

    def head_b(xx, yy, count):
        return head.at[
            pl.ds(pl.multiple_of(s * 2 * side + side + yy * 2 * piece + xx * piece, 16), count)
        ]

    own = []
    for k, (src, dst) in enumerate(
        [(rows_ref, rows_all.at[s, i, z]), (pa, head_a(x, y, piece)), (pb, head_b(x, y, piece))]
    ):
        copy = pltpu.make_async_copy(src, dst, local.at[k])
        copy.start()
        own.append(copy)
    reduce = []

    def part_of(m, plane):
        height = slots[m].shape[1]
        return parts[m].at[pl.ds(pl.multiple_of(plane * height, 16), height)]

    fetched, passed = [], []
    if paired:
        for m in range(n):
            copy = pltpu.make_async_copy(part_of(m, planes - 1 - z), totals[m], local.at[3 + m])
            copy.start()
            fetched.append(copy)
    near = [put(rows_ref, rows_all.at[s, i, z], {"fsdp": (z + k) % planes}) for k in range(1, planes)]
    head1 = [put(pa, head_a(x, y, piece), to_y), put(pb, head_b(x, y, piece), to_x)]
    if not paired:
        for m in range(n):
            for k in range(1, planes):
                target = (z + k) % planes
                reduce.append(put(part_of(m, target), slots[m].at[k - 1], {"fsdp": target}))
    for copy in own:
        copy.wait()
    take(*near)
    if paired:
        for m in range(n):
            passed.append(put(part_of(m, planes - 1 - partner), extras[m], {"fsdp": partner}))
    mid = planes // 2
    early, late = pl.ds(0, mid), pl.ds(mid, planes - mid)
    a1 = put(rows_all.at[s, i, early], rows_all.at[s, i, early], to_x)
    b1 = put(rows_all.at[s, i, late], rows_all.at[s, i, late], to_y)
    core = [put(rows_all.at[s, i], rows_all.at[s, i], to_core)]
    take(*head1)
    block = head_a(x, 0, 2 * piece)
    ha = put(block, block, to_x)
    block = head_b(0, y, 2 * piece)
    hb = put(block, block, to_y)
    take(a1, b1)
    second = []
    for who, span, device in ((i, early, to_y), (xn, early, to_y), (i, late, to_x), (yn, late, to_x)):
        block = rows_all.at[s, who, span]
        second.append(put(block, block, device))
    for who, span in ((xn, early), (yn, late)):
        block = rows_all.at[s, who, span]
        core.append(put(block, block, to_core))
    if paired:
        for copy in fetched:
            copy.wait()
        for m in range(n):
            passed[m].wait_recv()
            held = totals[m][...].astype(WIDE) + extras[m][...].astype(WIDE)
            totals[m][...] = held.astype(LOW)
            reduce.append(put(totals[m], slots[m].at[1], {"fsdp": planes - 1 - z}))
            reduce.append(put(part_of(m, partner), slots[m].at[0], {"fsdp": partner}))
    take(ha, hb)
    block = head.at[pl.ds(pl.multiple_of(s * 2 * side, 16), 2 * side)]
    core.append(put(block, block, to_core))
    take(*second)
    for who, span in ((yn, early), (diag, early), (xn, late), (diag, late)):
        block = rows_all.at[s, who, span]
        core.append(put(block, block, to_core))
    take(*reduce)
    take(*core)
    for copy in sent:
        copy.wait_send()


def exchange(planes, row_grads, pieces, parts):
    piece, vocab = pieces[0].shape
    shape = jax.ShapeDtypeStruct
    outs = [shape((2, 4, planes) + row_grads.shape, LOW), shape((16 * piece, vocab), LOW)]
    blocks = [(p.shape[0] // planes, p.shape[1]) for p in parts]
    paired = planes == 4
    outs += [shape((2 if paired else planes - 1,) + b, LOW) for b in blocks]
    copies = (planes - 1) * (1 + len(parts)) + 2 + 2 + 2 + 4
    anywhere = pl.BlockSpec(memory_space=pl.ANY)
    result = pl.pallas_call(
        functools.partial(exchange_kernel, planes),
        out_shape=outs,
        in_specs=[pl.BlockSpec(memory_space=pltpu.VMEM)] * 3 + [anywhere] * len(parts),
        out_specs=[anywhere] * len(outs),
        scratch_shapes=[pltpu.SemaphoreType.DMA((copies,))] * 2
        + [pltpu.SemaphoreType.DMA((8,))] * 2
        + [pltpu.SemaphoreType.DMA((3 + len(parts),))]
        + ([pltpu.VMEM(b, LOW) for b in blocks] * 2 if paired else []),
        compiler_params=pltpu.CompilerParams(
            collective_id=2, has_side_effects=True, vmem_limit_bytes=16 << 20
        ),
        name="exchange",
    )(row_grads, *pieces, *parts)
    return result[0], result[1], result[2:]


def block_of(vocab_rows):
    return 800 if vocab_rows % 800 == 0 else 400


def chunk_of(lists):
    return 32 if lists <= 64 else 16


def start_chunks(lists, length, stride, step, steps, starts, rows_hbm, buffer, sem):
    chunk = chunk_of(lists)

    def one(k, carry):
        at = jnp.minimum(starts[k * steps + step] // 16 * 16, length - chunk)
        src = rows_hbm.at[pl.ds(pl.multiple_of(k * stride + at, 16), chunk)]
        pltpu.make_async_copy(src, buffer.at[pl.ds(pl.multiple_of(k * chunk, 16), chunk)], sem).start()
        return carry

    lax.fori_loop(0, lists, one, 0)


def block_grad(
    lists, length, steps, step, starts, passes, bases, rows_hbm, ids_ref, near_ref, buffers, hot, wide_hot, grad, sems
):
    chunk = chunk_of(lists)
    slot = step % 2
    spare = buffers.at[2]
    width = grad.shape[0]
    stride = rows_hbm.shape[0] // lists

    @pl.when(step == 0)
    def _():
        start_chunks(lists, length, stride, 0, steps, starts, rows_hbm, buffers.at[0], sems.at[0])

    @pl.when(step + 1 < steps)
    def _():
        start_chunks(lists, length, stride, step + 1, steps, starts, rows_hbm, buffers.at[1 - slot], sems.at[1 - slot])

    pltpu.make_async_copy(buffers.at[slot], buffers.at[slot], sems.at[slot]).wait()
    lanes = lax.broadcasted_iota(jnp.int32, (chunk, width), 1) + bases[step]
    within = lax.broadcasted_iota(jnp.int32, (chunk, width), 0)

    def mark(shifted):
        def one(k, carry):
            begin = starts[k * steps + step] // 16 * 16 + shifted
            at = jnp.minimum(begin, length - chunk)
            ids = ids_ref[pl.ds(pl.multiple_of(k * length + at, 16), chunk), :]
            same = (ids == lanes) & (within >= begin - at)
            hot[pl.ds(pl.multiple_of(k * chunk, 16), chunk), :] = same.astype(WIDE).astype(LOW)
            return carry

        lax.fori_loop(0, lists, one, 0)

    down = lax.broadcasted_iota(jnp.int32, (width, lists * chunk), 0) + bases[step]
    wide_hot[...] = (down == near_ref[0]).astype(WIDE).astype(LOW)
    grad[...] = jnp.dot(wide_hot[...], buffers[slot], preferred_element_type=WIDE)

    def more(p, carry):
        mark(p * chunk)

        def one(k, inner):
            begin = starts[k * steps + step] // 16 * 16 + p * chunk
            at = jnp.minimum(begin, length - chunk)
            src = rows_hbm.at[pl.ds(pl.multiple_of(k * stride + at, 16), chunk)]
            pltpu.make_async_copy(
                src, spare.at[pl.ds(pl.multiple_of(k * chunk, 16), chunk)], sems.at[2]
            ).start()
            return inner

        lax.fori_loop(0, lists, one, 0)
        pltpu.make_async_copy(spare, spare, sems.at[2]).wait()
        grad[...] += contract_rows(hot[...], spare[...])
        return carry

    lax.fori_loop(1, passes[step], more, 0)


def table_square_kernel(lists, length, steps, starts, passes, bases, rows_hbm, ids_ref, near_ref, out, buffers, hot, wide_hot, grad, sems):
    step = pl.program_id(0)
    block_grad(lists, length, steps, step, starts, passes, bases, rows_hbm, ids_ref, near_ref, buffers, hot, wide_hot, grad, sems)
    part = jnp.sum((grad[...] * grad[...]).reshape(-1, 8, D), axis=0)
    part = jnp.where(passes[step] > 0, part, 0.0)

    @pl.when(step == 0)
    def _():
        out[...] = part

    @pl.when(step > 0)
    def _():
        out[...] += part


def table_adam_kernel(
    lists, length, steps, rate, decay, starts, passes, bases, clip, rows_hbm, ids_ref, near_ref, w, m, v, w_new, m_new, v_new, low, buffers, hot, wide_hot, grad, sems
):
    step = pl.program_id(0)
    block_grad(lists, length, steps, step, starts, passes, bases, rows_hbm, ids_ref, near_ref, buffers, hot, wide_hot, grad, sems)
    weight, mom, sec = adam_update(w[...], grad[...] * clip[0], m[...], v[...], rate, decay)
    w_new[...] = weight
    m_new[...] = mom
    v_new[...] = sec
    low[...] = weight.astype(LOW)


def table_scratch(lists, width):
    chunk = chunk_of(lists)
    return [
        pltpu.VMEM((3, lists * chunk, D), LOW),
        pltpu.VMEM((lists * chunk, width), LOW),
        pltpu.VMEM((width, lists * chunk), LOW),
        pltpu.VMEM((width, D), WIDE),
        pltpu.SemaphoreType.DMA((3,)),
    ]


def chunk_scalars(ids_sorted, bases, width):
    chunk = chunk_of(ids_sorted.shape[0])
    edges = bases[None, :, None]
    starts = jnp.sum((ids_sorted[:, None, :] < edges).astype(jnp.int32), axis=-1)
    ends = jnp.sum((ids_sorted[:, None, :] < edges + width).astype(jnp.int32), axis=-1)
    passes = jnp.max((ends - starts // 16 * 16 + chunk - 1) // chunk, axis=0)
    lists, length = ids_sorted.shape
    groups = length // 16
    begin = (starts // 16).T
    at = jnp.minimum(begin, groups - chunk // 16)
    by_group = ids_sorted.reshape(lists, groups, 16).transpose(1, 0, 2).reshape(groups, -1)
    widen = jnp.arange(lists * 16)[None, :] // 16 == jnp.arange(lists)[:, None]
    both = jnp.concatenate([at, begin], axis=0).astype(LOW)
    both = jnp.dot(both, widen.astype(LOW), preferred_element_type=WIDE).astype(jnp.int32)
    both = lax.optimization_barrier(both)
    steps = begin.shape[0]
    pieces = []
    for k in range(chunk // 16):
        wanted = both[:steps] + k
        found = jnp.zeros(wanted.shape, jnp.int32)
        for g in range(groups):
            found = jnp.where(wanted == g, by_group[g][None], found)
        found = jnp.where(wanted >= both[steps:], found, -(1 << 30))
        pieces.append(lax.optimization_barrier(found).reshape(-1, lists, 16))
    near = jnp.stack(pieces, axis=2).reshape(begin.shape[0], 1, -1)
    return starts.reshape(-1), jnp.maximum(passes, 1), near


def table_square(ids_sorted, ids_column, rows_flat, rank, ranks, vocab_rows):
    lists, length = ids_sorted.shape
    width = block_of(vocab_rows)
    total = vocab_rows // width
    steps = -(-total // ranks)
    blocks = rank + ranks * jnp.arange(steps, dtype=jnp.int32)
    bases = blocks * width
    starts, passes, near = chunk_scalars(ids_sorted, bases, width)
    passes = jnp.where(blocks < total, passes, 0)
    out = pl.pallas_call(
        functools.partial(table_square_kernel, lists, length, steps),
        grid_spec=pltpu.PrefetchScalarGridSpec(
            num_scalar_prefetch=3,
            grid=(steps,),
            in_specs=[
                pl.BlockSpec(memory_space=pl.ANY),
                pl.BlockSpec(
                    (lists * length, 1), lambda g, *_: (0, 0), pipeline_mode=pl.Buffered(1)
                ),
                pl.BlockSpec((1, 1, near.shape[2]), lambda g, *_: (g, 0, 0)),
            ],
            out_specs=pl.BlockSpec((8, D), lambda g, *_: (0, 0)),
            scratch_shapes=table_scratch(lists, width),
        ),
        out_shape=jax.ShapeDtypeStruct((8, D), WIDE),
        compiler_params=pltpu.CompilerParams(vmem_limit_bytes=56 << 20),
        name="table_square",
    )(starts, passes, bases, rows_flat, ids_column, near)
    return jnp.sum(out)


def table_adam(ids_sorted, ids_column, rows_flat, clip_scale, table, mom, sec, rate, decay):
    lists, length = ids_sorted.shape
    vocab_rows = table.shape[0]
    width = block_of(vocab_rows)
    steps = vocab_rows // width
    bases = jnp.arange(steps, dtype=jnp.int32) * width
    starts, passes, near = chunk_scalars(ids_sorted, bases, width)
    block = pl.BlockSpec((width, D), lambda g, *_: (g, 0))
    wide = jax.ShapeDtypeStruct(table.shape, WIDE)
    return pl.pallas_call(
        functools.partial(table_adam_kernel, lists, length, steps, rate, decay),
        grid_spec=pltpu.PrefetchScalarGridSpec(
            num_scalar_prefetch=4,
            grid=(steps,),
            in_specs=[
                pl.BlockSpec(memory_space=pl.ANY),
                pl.BlockSpec(
                    (lists * length, 1), lambda g, *_: (0, 0), pipeline_mode=pl.Buffered(1)
                ),
                pl.BlockSpec((1, 1, near.shape[2]), lambda g, *_: (g, 0, 0)),
                block,
                block,
                block,
            ],
            out_specs=[block] * 4,
            scratch_shapes=table_scratch(lists, width),
        ),
        out_shape=[wide, wide, wide, jax.ShapeDtypeStruct(table.shape, LOW)],
        compiler_params=pltpu.CompilerParams(vmem_limit_bytes=60 << 20),
        cost_estimate=pl.CostEstimate(
            flops=steps * 2 * width * lists * chunk_of(lists) * D,
            bytes_accessed=table.size * 26,
            transcendentals=table.size,
        ),
        name="table_adam",
    )(starts, passes, bases, clip_scale.reshape(1), rows_flat, ids_column, near, table, mom, sec)


HEAD_BLOCK = 800


def head_adam_kernel(rate, decay, clip, grad, w, m, v, w_new, m_new, v_new, low):
    scaled = grad[...].astype(WIDE) * clip[0]
    weight, mom, sec = adam_update(w[...], scaled, m[...], v[...], rate, decay)
    w_new[...] = weight
    m_new[...] = mom
    v_new[...] = sec
    low[...] = weight.astype(LOW)


def head_adam(grad, clip_scale, head, mom, sec, rate, decay):
    vocab = head.shape[1]
    block = pl.BlockSpec((HEAD_BLOCK, D), lambda g, *_: (g, 0))
    wide = jax.ShapeDtypeStruct((vocab, D), WIDE)
    results = pl.pallas_call(
        functools.partial(head_adam_kernel, rate, decay),
        grid_spec=pltpu.PrefetchScalarGridSpec(
            num_scalar_prefetch=1,
            grid=(-(-vocab // HEAD_BLOCK),),
            in_specs=[block] * 4,
            out_specs=[block] * 4,
        ),
        out_shape=[wide, wide, wide, jax.ShapeDtypeStruct((vocab, D), LOW)],
        compiler_params=pltpu.CompilerParams(vmem_limit_bytes=56 << 20),
        cost_estimate=pl.CostEstimate(
            flops=head.size * 20, bytes_accessed=head.size * 28, transcendentals=head.size
        ),
        name="head_adam",
    )(clip_scale.reshape(1), grad, head.T, mom.T, sec.T)
    return [item.T for item in results]


def small_gather_kernel(axes, sizes, *refs):
    n = (len(refs) - 2) // 2
    blocks, outs, send, recv = refs[:n], refs[n : 2 * n], refs[2 * n], refs[2 * n + 1]
    mine = [lax.axis_index(axis) for axis in axes]
    slot = 0
    for index, size in zip(mine, sizes):
        slot = slot * size + index
    offsets = [()]
    for size in sizes:
        offsets = [o + (k,) for o in offsets for k in range(size)]
    peers = [
        {axis: (index + k) % size for axis, index, size, k in zip(axes, mine, sizes, offset)}
        for offset in offsets[1:]
    ]
    barrier = pltpu.get_barrier_semaphore()
    for peer in peers:
        pl.semaphore_signal(barrier, inc=1, device_id=peer, device_id_type=MESH)
    pl.semaphore_wait(barrier, len(peers))
    copies = []
    for m in range(n):
        for k, peer in enumerate(peers):
            copy = pltpu.make_async_remote_copy(
                src_ref=blocks[m],
                dst_ref=outs[m].at[slot],
                send_sem=send.at[m * len(peers) + k],
                recv_sem=recv.at[m * len(peers) + k],
                device_id=peer,
                device_id_type=MESH,
            )
            copy.start()
            copies.append(copy)
        outs[m][slot] = blocks[m][...]
    for copy in copies:
        copy.wait()


def small_gather(blocks, axes, identity):
    sizes = [lax.axis_size(axis) for axis in axes]
    count = math.prod(sizes)
    copies = (count - 1) * len(blocks)
    whole = pl.BlockSpec(memory_space=pltpu.VMEM)
    return pl.pallas_call(
        functools.partial(small_gather_kernel, axes, sizes),
        out_shape=[jax.ShapeDtypeStruct((count,) + b.shape, b.dtype) for b in blocks],
        in_specs=[whole] * len(blocks),
        out_specs=[whole] * len(blocks),
        scratch_shapes=[pltpu.SemaphoreType.DMA((copies,))] * 2,
        compiler_params=pltpu.CompilerParams(collective_id=identity, has_side_effects=True),
        name=f"small_gather_{identity}",
    )(*blocks)


def finish_kernel(n, me, *refs):
    parts, slots, pieces = refs[:n], refs[n : 2 * n], refs[2 * n : 2 * n + 2]
    shards, out = refs[2 * n + 2 : 3 * n + 2], refs[3 * n + 2]
    total = jnp.zeros((), WIDE)
    for m in range(n):
        held = parts[m][...].astype(WIDE)
        for k in range(slots[m].shape[0]):
            held = held + slots[m][k].astype(WIDE)
        low = held.astype(LOW)
        shards[m][...] = low
        held = low.astype(WIDE)
        total = total + jnp.sum(held * held)
    for piece in pieces:
        held = piece[...].astype(WIDE)
        total = total + jnp.sum(held * held)
    out[...] = jnp.full(out.shape, total, WIDE)


def finish(me, parts, slots, pieces):
    blocks = [slot.shape[1:] for slot in slots]
    whole = lambda shape: pl.BlockSpec(shape, lambda g, *_: (0,) * len(shape))
    results = pl.pallas_call(
        functools.partial(finish_kernel, len(parts)),
        grid_spec=pltpu.PrefetchScalarGridSpec(
            num_scalar_prefetch=1,
            grid=(1,),
            in_specs=[pl.BlockSpec(block, lambda g, me: (me[0], 0)) for block in blocks]
            + [whole(item.shape) for item in list(slots) + list(pieces)],
            out_specs=[whole(block) for block in blocks] + [whole((8, 128))],
        ),
        out_shape=[jax.ShapeDtypeStruct(block, LOW) for block in blocks]
        + [jax.ShapeDtypeStruct((8, 128), WIDE)],
        compiler_params=pltpu.CompilerParams(vmem_limit_bytes=40 << 20),
        name="finish",
    )(me.astype(jnp.int32).reshape(1), *parts, *slots, *pieces)
    return list(results[:-1]), results[-1][0, 0]


def per_device(
    token_ids,
    next_ids,
    seq_lengths,
    embedding,
    embedding_mom,
    embedding_sec,
    head_table,
    head_mom,
    head_sec,
    w_qkv,
    qkv_mom,
    qkv_sec,
    w_out,
    out_mom,
    out_sec,
    w_gateup,
    gateup_mom,
    gateup_sec,
    w_down,
    down_mom,
    down_sec,
    gains,
    gains_mom,
    gains_sec,
):
    planes = lax.axis_size("fsdp")
    replicas = lax.axis_size("dp")
    first = lax.axis_index("section") == 0
    first_f = first.astype(WIDE)
    me = lax.axis_index("fsdp")
    token_total = jnp.sum(seq_lengths).astype(WIDE)
    tokens = MB * ROW

    my_ids = jnp.stack([token_ids.reshape(-1), next_ids.reshape(-1)])
    ids_all, gains_all = small_gather([my_ids, gains[0]], ("dp", "fsdp"), 3)
    ids_all = ids_all.reshape(replicas, planes, 2, tokens)
    gains_full = gains_all[:planes].transpose(1, 0, 2).reshape(3, D)
    gains_full = lax.optimization_barrier(gains_full.astype(LOW)).astype(WIDE)
    group_ids = pick(ids_all, lax.axis_index("dp"))
    rel_ids = jnp.stack([pick(group_ids, (me - step) % planes) for step in range(planes)])
    my_kind = jnp.where(first, rel_ids[:, 0], rel_ids[:, 1])
    vocab_rows = embedding.shape[0]
    vocab_start = me * vocab_rows
    local = my_kind - vocab_start
    inside = (local >= 0) & (local < vocab_rows)
    found = jnp.take(embedding, jnp.clip(local, 0, vocab_rows - 1), axis=0)
    found = lax.optimization_barrier(jnp.where(inside[..., None], found, 0.0).astype(LOW))
    looked = found[0].astype(WIDE)
    for step in range(1, planes):
        looked = looked + shift(found[step], "fsdp", planes - step).astype(WIDE)
    next_embed = swap(looked.astype(LOW), "section", 1).astype(WIDE)

    lists = ids_all.transpose(2, 0, 1, 3).reshape(-1, tokens) - vocab_start
    place = jnp.arange(tokens)
    before = (lists[:, None, :] < lists[:, :, None]) | (
        (lists[:, None, :] == lists[:, :, None]) & (place[None, None, :] < place[None, :, None])
    )
    ranks = jnp.sum(before.astype(jnp.int32), axis=-1)
    sorted_ids = jnp.sum(
        jnp.where(ranks[:, None, :] == place[None, :, None], lists[:, None, :], 0), axis=-1
    )
    own_list = (
        lax.axis_index("section") * replicas + lax.axis_index("dp")
    ) * planes + me
    arrange = (pick(ranks, own_list)[None, :] == place[:, None]).astype(LOW)

    full = gather_weights(
        planes,
        replicas,
        [w_qkv[0].astype(LOW), w_out[0].astype(LOW), w_gateup[0].astype(LOW), w_down[0].astype(LOW)],
    )
    layer_weights = (full[0], full[1], full[2], full[3], gains_full[0], gains_full[1])
    head_gain = gains_full[2]

    first_out, _ = layer_fwd(looked, layer_weights)
    middle = swap(first_out.astype(LOW), "section", 1).astype(WIDE)
    layer_in = jnp.where(first, looked, middle)
    layer_out, saved = layer_fwd(layer_in, layer_weights)
    final_state = norm_fwd(layer_out, head_gain)
    arrived = swap(final_state.astype(LOW), "section", 1).astype(WIDE)
    merged_in = jnp.where(first, arrived + next_embed, layer_out)
    head_in = norm_fwd(merged_in, head_gain)

    lengths = seq_lengths.reshape(replicas, planes, MB)[lax.axis_index("dp")]
    lengths = jnp.stack([pick(lengths, (me - step) % planes) for step in range(planes)])
    targets_main = rel_ids[:, 1].reshape(planes, MB, ROW)
    shifted = jnp.concatenate([targets_main[..., 1:], targets_main[..., :1]], axis=-1)
    targets = jnp.where(first, shifted, targets_main)
    limit = lengths - first.astype(jnp.int32)
    positions = jnp.arange(ROW, dtype=jnp.int32)
    weights_tok = (positions < limit[..., None]).astype(WIDE) * jnp.where(first, MTP_WEIGHT, 1.0)
    left = [saved[0], saved[6], saved[8]]
    left_all = spread(
        lambda index: jnp.concatenate(left + [sub_quarter(saved[10], planes, index)], axis=1)
    )
    loss_part, mine, theirs, grad_in = head_pass(
        head_in.astype(LOW),
        targets.reshape(-1),
        weights_tok.reshape(-1),
        head_table.T,
        vocab_start,
        token_total,
    )
    sorted_ids, loss_part = lax.optimization_barrier((sorted_ids, loss_part))
    merged_grad, mtp_gain = norm_back(merged_in, head_gain, grad_in)
    merged_low = merged_grad.astype(LOW)
    sent = swap(merged_low, "section", 1).astype(WIDE)
    top_grad, top_gain = norm_back(layer_out, head_gain, grad_in + sent)
    head_gain_grad = jnp.where(first, mtp_gain, top_gain)
    half = add_low(mine, swap(theirs, "section", 1))
    top_grad, left_all = lax.optimization_barrier((top_grad, left_all))
    below, _, _ = layer_back(layer_in, layer_weights, saved, top_grad)
    below, half = lax.optimization_barrier((below.astype(LOW), half))
    side = half.shape[0] // 2
    piece_a, piece_b = keep_half(half[:side], 1), keep_half(half[side:], 2)
    upstream = jnp.where(first, swap(below, "section", 1).astype(WIDE), top_grad)
    grad_inputs, right, gain_parts = layer_back(layer_in, layer_weights, saved, upstream)
    grad_inputs, piece_a, piece_b = lax.optimization_barrier((grad_inputs, piece_a, piece_b))
    piece_a, piece_b = keep_half(piece_a, 2), keep_half(piece_b, 1)

    grad_packed, after_low, grad_gu, upstream_low = right
    tops = spread(lambda index: upstream_low)
    early = spread(lambda index: quarter(grad_gu, index))
    late = spread(
        lambda index: jnp.concatenate([quarter(after_low, index), quarter(grad_packed, index)], axis=1)
    )
    cut = D // SHARE
    parts = [
        contract_rows(left_all[:, 2 * D : 3 * D], early),
        contract_rows(left_all[:, 3 * D :], tops),
        contract_rows(left_all[:, :D], late[:, cut:]),
        contract_rows(left_all[:, D : 2 * D], late[:, :cut]),
    ]
    parts = [part.astype(LOW) for part in parts]
    gains_grad = jnp.stack([gain_parts[0], gain_parts[1], head_gain_grad])

    row_grads = jnp.where(first, grad_inputs.astype(LOW), sent.astype(LOW))
    row_grads = jnp.dot(arrange, row_grads, preferred_element_type=WIDE).astype(LOW)
    row_grads = jnp.concatenate(
        [row_grads, gains_grad.astype(LOW), jnp.zeros((13, D), LOW)], axis=0
    )
    rows_all, grad_head, slots = exchange(planes, row_grads, (piece_a, piece_b), parts)
    rows_flat = rows_all.reshape(-1, D)
    gains_grad = pick(rows_all[:, :, :, tokens : tokens + 3], lax.axis_index("section"))
    gains_grad = jnp.sum(gains_grad.astype(WIDE), axis=(0, 1))
    gains_grad = lax.dynamic_slice_in_dim(gains_grad, me * (D // planes), D // planes, 1)
    ids_column = sorted_ids.reshape(-1, 1)

    shards, shard_squares = finish(me, parts, slots, (piece_a, piece_b))
    group = lax.axis_index("section") * replicas + lax.axis_index("dp")
    squares = table_square(sorted_ids, ids_column, rows_flat, group, 2 * replicas, vocab_rows)
    squares = squares + shard_squares + jnp.sum(gains_grad * gains_grad) / replicas
    totals = jnp.stack([squares, loss_part / planes])[:, None] * jnp.ones((1, 128), WIDE)
    totals = jnp.sum(small_gather([totals], ("section", "dp", "fsdp"), 4)[0], axis=0)[:, 0]
    grad_norm = jnp.sqrt(totals[0])
    loss_total = totals[1]
    clip_scale = CLIP / jnp.maximum(grad_norm, CLIP)

    shards, clip_scale = lax.optimization_barrier((shards, clip_scale))
    widths = [0, 2 * D, 3 * D, 3 * D + 3 * cut, 4 * D]
    packed = jnp.concatenate(shards, axis=1)
    rank = plane_rank()
    others = [packed] + [swap(packed, "dp", mask) for mask in range(1, SHARE)]
    layer_grads = [
        in_order([other[:, lo:hi] for other in others], rank, 0 if index == 1 else 1).astype(WIDE)
        for index, (lo, hi) in enumerate(zip(widths[:-1], widths[1:]))
    ]
    params = (w_qkv[0], w_out[0], w_gateup[0], w_down[0], gains[0])
    grads_all = (
        layer_grads[2],
        layer_grads[3],
        layer_grads[0],
        layer_grads[1],
        gains_grad,
    )
    moments = (
        (qkv_mom[0], qkv_sec[0]),
        (out_mom[0], out_sec[0]),
        (gateup_mom[0], gateup_sec[0]),
        (down_mom[0], down_sec[0]),
        (gains_mom[0], gains_sec[0]),
    )
    rates = (0.03, 0.12, 0.03, 0.03, 0.6)
    decays = (0.1, 0.1, 0.1, 0.1, 0.0)
    outputs = [loss_total, token_total, grad_norm]
    outputs += table_adam(
        sorted_ids,
        ids_column,
        rows_flat,
        clip_scale,
        embedding,
        embedding_mom,
        embedding_sec,
        0.6,
        0.1,
    )
    outputs += head_adam(grad_head, clip_scale, head_table, head_mom, head_sec, 0.03, 0.1)
    for index in range(5):
        weight_new, mom_new, sec_new = adam_update(
            params[index],
            grads_all[index] * clip_scale,
            moments[index][0],
            moments[index][1],
            rates[index],
            decays[index],
        )
        outputs.extend([weight_new[None], mom_new[None], sec_new[None]])
        if index < 4:
            outputs.append(weight_new.astype(LOW)[None])
    return tuple(outputs)


def solution(mesh):
    placed = (
        P(("dp", "fsdp"), None),
        P(("dp", "fsdp"), None),
        P(),
        P("fsdp", None),
        P("fsdp", None),
        P("fsdp", None),
        P(None, "fsdp"),
        P(None, "fsdp"),
        P(None, "fsdp"),
        P("section", "fsdp", None),
        P("section", "fsdp", None),
        P("section", "fsdp", None),
        P("section", "fsdp", None),
        P("section", "fsdp", None),
        P("section", "fsdp", None),
        P("section", "fsdp", None),
        P("section", "fsdp", None),
        P("section", "fsdp", None),
        P("section", "fsdp", None),
        P("section", "fsdp", None),
        P("section", "fsdp", None),
        P("section", None, "fsdp"),
        P("section", None, "fsdp"),
        P("section", None, "fsdp"),
    )
    return jax.shard_map(
        per_device,
        mesh=mesh,
        in_specs=placed,
        out_specs=(
            P(),
            P(),
            P(),
            P("fsdp", None),
            P("fsdp", None),
            P("fsdp", None),
            P("fsdp", None),
            P(None, "fsdp"),
            P(None, "fsdp"),
            P(None, "fsdp"),
            P(None, "fsdp"),
            P("section", "fsdp", None),
            P("section", "fsdp", None),
            P("section", "fsdp", None),
            P("section", "fsdp", None),
            P("section", "fsdp", None),
            P("section", "fsdp", None),
            P("section", "fsdp", None),
            P("section", "fsdp", None),
            P("section", "fsdp", None),
            P("section", "fsdp", None),
            P("section", "fsdp", None),
            P("section", "fsdp", None),
            P("section", "fsdp", None),
            P("section", "fsdp", None),
            P("section", "fsdp", None),
            P("section", "fsdp", None),
            P("section", None, "fsdp"),
            P("section", None, "fsdp"),
            P("section", None, "fsdp"),
        ),
        check_vma=False,
    )
```

```python
import functools
import math

import jax
import jax.numpy as jnp
from jax import lax
from jax.experimental import pallas as pl
from jax.experimental.pallas import tpu as pltpu
from jax.sharding import PartitionSpec as P

D = 768
HEADS = 12
HEAD_DIM = 64
FF = 3072
ROW = 128
MB = 2
STEP_COUNT = 10
SHARE = 4


EPS = 1e-05
MTP_WEIGHT = 0.3
CLIP = 0.01
BETA1 = 0.9
BETA2 = 0.95
ADAM_EPS = 1e-08
LOW = jnp.bfloat16
WIDE = jnp.float32

AHEAD = 2
MESH = pl.DeviceIdType.MESH

def weights_kernel(planes, units, rows, *refs):
    n = len(rows)
    own, full = refs[:n], refs[n : 2 * n]
    send, recv, local = refs[2 * n :]
    z = lax.axis_index("fsdp")
    i = lax.axis_index("dp")
    x, y = i % 2, i // 2
    q = i
    xn, yn = i + 1 - 2 * x, (i + 2) % 4
    near, far = z + 1 - 2 * (z % 2), planes - 1 - z
    beyond = planes - 1 - near
    to_x, to_y, to_near, to_far = {"dp": xn}, {"dp": yn}, {"fsdp": near}, {"fsdp": far}
    barrier = pltpu.get_barrier_semaphore()
    for device in (to_x, to_y, to_near, to_far):
        pl.semaphore_signal(barrier, inc=1, device_id=device, device_id_type=MESH)
    pl.semaphore_wait(barrier, 4)
    keep = []
    for m in range(n):
        c = pltpu.make_async_copy(
            own[m], full[m].at[pl.ds(pl.multiple_of(z * rows[m], 16), rows[m]), :], local.at[m]
        )
        c.start()
        keep.append(c)
    started = []

    def put(src, dst, k, device):
        copy = pltpu.make_async_remote_copy(
            src_ref=src,
            dst_ref=dst,
            send_sem=send.at[k],
            recv_sem=recv.at[k],
            device_id=device,
            device_id_type=MESH,
        )
        copy.start()
        started.append(copy)
        return copy

    def block(u, plane, part):
        m, cols, _ = units[u]
        r = rows[m] // 4
        return full[m].at[pl.ds(pl.multiple_of(plane * rows[m] + part * r, 16), r), pl.ds(*cols)]

    sources = (near, far, beyond)
    zs, seconds, thirds = {}, {}, []
    total = len(units)

    def first(u):
        m, cols, _ = units[u]
        r = rows[m] // 4
        src = own[m].at[pl.ds(pl.multiple_of(q * r, 16), r), pl.ds(*cols)]
        zs[u, 0] = put(src, block(u, z, q), 12 * u, to_near)
        zs[u, 1] = put(src, block(u, z, q), 12 * u + 1, to_far)

    def onward(u):
        zs[u, 1].wait_recv()
        zs[u, 2] = put(block(u, far, q), block(u, far, q), 12 * u + 2, to_near)

    def second(u, j):
        if j != 1:
            zs[u, j].wait_recv()
        b = block(u, sources[j], q)
        seconds[u, j] = put(b, b, 12 * u + 3 + j, to_y if units[u][2] else to_x)

    def third(u, j):
        seconds[u, j].wait_recv()
        order = units[u][2]
        for w, part in enumerate((q, yn if order else xn)):
            b = block(u, sources[j], part)
            thirds.append(put(b, b, 12 * u + 6 + 2 * j + w, to_x if order else to_y))

    pairs = [(u, u + 1) for u in range(0, total, 2)]
    for ahead in range(AHEAD):
        for u in pairs[ahead]:
            first(u)
    for t in range(len(pairs) + 2):
        if t < len(pairs):
            for u in pairs[t]:
                onward(u)
            if t + AHEAD < len(pairs):
                for u in pairs[t + AHEAD]:
                    first(u)
            for j in (0, 1):
                for u in pairs[t]:
                    second(u, j)
        if 1 <= t <= len(pairs):
            for u in pairs[t - 1]:
                second(u, 2)
            for j in (0, 1):
                for u in pairs[t - 1]:
                    third(u, j)
        if t >= 2:
            for u in pairs[t - 2]:
                third(u, 2)
    for c in thirds:
        c.wait_recv()
    for c in started:
        c.wait_send()
    for c in keep:
        c.wait()


def gather_weights(planes, replicas, shards):
    rows = [w.shape[0] for w in shards]
    if planes != 4 or replicas != 4 or any(r % (SHARE * 16) for r in rows):
        return [lax.all_gather(w, "fsdp", axis=0, tiled=True) for w in shards]
    units = []
    for m, w in enumerate(shards):
        width = w.shape[1]
        parts = 4 if width > 4096 else 2
        step = width // parts
        for p in range(parts):
            units.append((m, (p * step, step), p % 2))
    copies = len(units) * 12
    return pl.pallas_call(
        functools.partial(weights_kernel, planes, units, rows),
        out_shape=[jax.ShapeDtypeStruct((planes * w.shape[0], w.shape[1]), w.dtype) for w in shards],
        in_specs=[pl.BlockSpec(memory_space=pltpu.VMEM)] * len(shards),
        out_specs=[pl.BlockSpec(memory_space=pl.ANY)] * len(shards),
        scratch_shapes=[pltpu.SemaphoreType.DMA((copies,)), pltpu.SemaphoreType.DMA((copies,)), pltpu.SemaphoreType.DMA((len(shards),))],
        compiler_params=pltpu.CompilerParams(collective_id=1, has_side_effects=True),
        name="gather_weights",
    )(*shards)


def norm_fwd(values, scale_gain):
    inverse = lax.rsqrt(jnp.mean(values * values, axis=-1, keepdims=True) + EPS)
    return values * inverse * scale_gain


def norm_back(values, scale_gain, upstream):
    _, pullback = jax.vjp(norm_fwd, values, scale_gain)
    return pullback(upstream)


def rope_tables(row_count, head_width):
    half_width = head_width // 2
    position = jnp.arange(row_count, dtype=jnp.float32)[:, None]
    frequency = 10000.0 ** (-jnp.arange(half_width, dtype=jnp.float32) / half_width)
    angles = position * frequency[None, :]
    return (jnp.cos(angles), jnp.sin(angles))


def rotate(values, cosine, sine_table):
    half_width = values.shape[-1] // 2
    first, second = (values[..., :half_width], values[..., half_width:])
    return jnp.concatenate(
        [first * cosine - second * sine_table, second * cosine + first * sine_table], axis=-1
    )


def contract_rows(left, right):
    return lax.dot_general(
        left, right, (((0,), (0,)), ((), ())), preferred_element_type=jnp.float32
    )


def contract_cols(left, right):
    return lax.dot_general(
        left, right, (((1,), (1,)), ((), ())), preferred_element_type=jnp.float32
    )


def swiglu(gate_up):
    return jax.nn.silu(gate_up[:, :FF]) * gate_up[:, FF:]


def shift(block, axis, distance):
    count = lax.axis_size(axis)
    return lax.ppermute(block, axis, [(i, (i + distance) % count) for i in range(count)])


def swap(block, axis, mask):
    count = lax.axis_size(axis)
    return lax.ppermute(block, axis, [(i, i ^ mask) for i in range(count)])


def pick(array, index, axis=0):
    return lax.dynamic_index_in_dim(array, index, axis, keepdims=False)


def layer_fwd(inputs, weights):
    w_qkv, w_out, w_gateup, w_down, attn_gain, ffn_gain = weights
    normed = norm_fwd(inputs, attn_gain).astype(LOW)
    packed = jnp.dot(normed, w_qkv, preferred_element_type=WIDE)
    split = packed.reshape(MB, ROW, 3, HEADS, HEAD_DIM).transpose(2, 0, 3, 1, 4)
    split = split.reshape(3, MB * HEADS, ROW, HEAD_DIM)
    cosine, sine_table = rope_tables(ROW, HEAD_DIM)
    queries = rotate(split[0], cosine, sine_table).astype(LOW)
    keys_rot = rotate(split[1], cosine, sine_table).astype(LOW)
    values_low = split[2].astype(LOW)
    scores = jnp.einsum(
        "hqd,hkd->hqk", queries, keys_rot, preferred_element_type=WIDE
    ) * HEAD_DIM ** (-0.5)
    position = jnp.arange(ROW)
    causal = position[:, None] >= position[None, :]
    scores = jnp.where(causal[None], scores, -1e30)
    shifted = jnp.exp(scores - jnp.max(scores, axis=-1, keepdims=True))
    probs = shifted / jnp.sum(shifted, axis=-1, keepdims=True)
    probs_low = probs.astype(LOW)
    mixed = jnp.einsum("hqk,hkd->hqd", probs_low, values_low, preferred_element_type=WIDE)
    mixed = mixed.reshape(MB, HEADS, ROW, HEAD_DIM).transpose(0, 2, 1, 3)
    mixed_low = mixed.reshape(MB * ROW, D).astype(LOW)
    after_attn = inputs + jnp.dot(mixed_low, w_out, preferred_element_type=WIDE)
    normed_ffn = norm_fwd(after_attn, ffn_gain).astype(LOW)
    gate_up = jnp.dot(normed_ffn, w_gateup, preferred_element_type=WIDE)
    hidden = swiglu(gate_up).astype(LOW)
    output = after_attn + jnp.dot(hidden, w_down, preferred_element_type=WIDE)
    saved = (
        normed,
        queries,
        keys_rot,
        values_low,
        probs,
        probs_low,
        mixed_low,
        after_attn,
        normed_ffn,
        gate_up,
        hidden,
    )
    return (output, saved)


def layer_back(inputs, weights, saved, upstream):
    w_qkv, w_out, w_gateup, w_down, attn_gain, ffn_gain = weights
    (
        normed,
        queries,
        keys_rot,
        values_low,
        probs,
        probs_low,
        mixed_low,
        after_attn,
        normed_ffn,
        gate_up,
        hidden,
    ) = saved
    upstream_low = upstream.astype(LOW)
    grad_hidden = contract_cols(upstream_low, w_down)
    _, pullback = jax.vjp(swiglu, gate_up)
    grad_gu = pullback(grad_hidden)[0].astype(LOW)
    grad_nffn = contract_cols(grad_gu, w_gateup)
    back_ffn, grad_ffn_gain = norm_back(after_attn, ffn_gain, grad_nffn)
    grad_after = upstream + back_ffn
    after_low = grad_after.astype(LOW)
    grad_mixed = contract_cols(after_low, w_out).astype(LOW)
    grad_mixed = grad_mixed.reshape(MB, ROW, HEADS, HEAD_DIM).transpose(0, 2, 1, 3)
    grad_mixed = grad_mixed.reshape(MB * HEADS, ROW, HEAD_DIM)
    grad_probs = jnp.einsum("hqd,hkd->hqk", grad_mixed, values_low, preferred_element_type=WIDE)
    grad_values = jnp.einsum("hqk,hqd->hkd", probs_low, grad_mixed, preferred_element_type=WIDE)
    grad_scores = probs * (grad_probs - jnp.sum(probs * grad_probs, axis=-1, keepdims=True))
    grad_scores = grad_scores.astype(LOW)
    scale_attn = HEAD_DIM ** (-0.5)
    grad_query = (
        jnp.einsum("hqk,hkd->hqd", grad_scores, keys_rot, preferred_element_type=WIDE)
        * scale_attn
    )
    grad_key = (
        jnp.einsum("hqk,hqd->hkd", grad_scores, queries, preferred_element_type=WIDE)
        * scale_attn
    )
    cosine, sine_table = rope_tables(ROW, HEAD_DIM)
    grad_query = rotate(grad_query, cosine, -sine_table)
    grad_key = rotate(grad_key, cosine, -sine_table)
    grad_packed = jnp.stack([grad_query, grad_key, grad_values]).astype(LOW)
    grad_packed = grad_packed.reshape(3, MB, HEADS, ROW, HEAD_DIM).transpose(1, 3, 0, 2, 4)
    grad_packed = grad_packed.reshape(MB * ROW, 3 * D)
    grad_normed = contract_cols(grad_packed, w_qkv)
    back_attn, grad_attn_gain = norm_back(inputs, attn_gain, grad_normed)
    grad_inputs = grad_after + back_attn
    return (
        grad_inputs,
        (grad_packed, after_low, grad_gu, upstream_low),
        (grad_attn_gain, grad_ffn_gain),
    )


def plane_rank():
    return lax.axis_index("dp")


def quarter(block, index):
    width = block.shape[1] // SHARE
    return lax.dynamic_slice_in_dim(block, index * width, width, 1)


def sub_quarter(block, planes, index):
    rows, width = block.shape
    split = block.reshape(rows, planes, SHARE, width // planes // SHARE)
    return lax.dynamic_index_in_dim(split, index, 2, keepdims=False).reshape(rows, -1)


def spread(make):
    rank = plane_rank()
    own = make(rank)
    rows = own.shape[0]
    full = lax.dynamic_update_slice(jnp.zeros((SHARE * rows, own.shape[1]), LOW), own, (0, 0))
    for mask in range(1, SHARE):
        piece = swap(make(rank ^ mask), "dp", mask)
        full = lax.dynamic_update_slice(full, piece, (mask * rows, 0))
    return full


def in_order(pieces, rank, axis):
    low = rank % 2 == 0
    top = rank // 2 == 0
    pairs = []
    for k in (0, 2):
        pairs.append(
            (jnp.where(low, pieces[k], pieces[k + 1]), jnp.where(low, pieces[k + 1], pieces[k]))
        )
    lower = [jnp.where(top, pairs[0][j], pairs[1][j]) for j in range(2)]
    upper = [jnp.where(top, pairs[1][j], pairs[0][j]) for j in range(2)]
    return jnp.concatenate(lower + upper, axis=axis)


def relative_blocks():
    s = lax.axis_index("section")
    i = lax.axis_index("dp")
    x, y = i % 2, i // 2
    blocks = []
    for es in (0, 1):
        for kind in (0, 1):
            for e1 in (0, 1):
                for e2 in (0, 1):
                    a, b = (x, y) if kind == 0 else (y, x)
                    within = ((a + e1) % 2) * 2 + (b + e2) % 2
                    blocks.append(((s + es) % 2) * 8 + kind * 4 + within)
    return jnp.stack(blocks).astype(jnp.int32)


TOKENS = 256


def head_piece(vocab):
    return -(-vocab // 256) * 16


def table_block(vocab, base, h_ref):
    inside = lax.broadcasted_iota(jnp.int32, h_ref.shape, 0) + base < vocab
    return jnp.where(inside, h_ref[...], 0.0).astype(LOW)


def head_scores(vocab, base, table, rows):
    logits = contract_cols(table, rows)
    index = lax.broadcasted_iota(jnp.int32, logits.shape, 0) + base
    return jnp.where(index < vocab, logits, -1e30), index


def head_stats_kernel(vocab, h_ref, rows_ref, target_ref, out):
    step = pl.program_id(0)
    base = step * h_ref.shape[0]
    table = table_block(vocab, base, h_ref)

    @pl.when(step == 0)
    def _():
        out[0:1, :] = jnp.full((1, out.shape[1]), -1e30, WIDE)
        out[1:3, :] = jnp.zeros((2, out.shape[1]), WIDE)

    for c in range(rows_ref.shape[0] // TOKENS):
        span = slice(c * TOKENS, (c + 1) * TOKENS)
        logits, index = head_scores(vocab, base, table, rows_ref[span, :])
        before = out[0:1, span]
        peak = jnp.maximum(before, jnp.max(logits, axis=0, keepdims=True))
        summed = jnp.sum(jnp.exp(logits - peak), axis=0, keepdims=True)
        picked = jnp.sum(jnp.where(index == target_ref[:, span], logits, 0.0), axis=0, keepdims=True)
        out[0:1, span] = peak
        out[1:2, span] = out[1:2, span] * jnp.exp(before - peak) + summed
        out[2:3, span] += picked


def once(shape):
    return pl.BlockSpec(shape, lambda g, *_: (0,) * len(shape), pipeline_mode=pl.Buffered(1))


def head_stats(head, rows, targets):
    vocab, count = head.shape[0], rows.shape[0]
    piece = head_piece(vocab)
    return pl.pallas_call(
        functools.partial(head_stats_kernel, vocab),
        grid=(-(-vocab // piece),),
        in_specs=[pl.BlockSpec((piece, D), lambda g: (g, 0)), once((count, D)), once((1, count))],
        out_specs=pl.BlockSpec((8, count), lambda g: (0, 0)),
        out_shape=jax.ShapeDtypeStruct((8, count), WIDE),
        compiler_params=pltpu.CompilerParams(vmem_limit_bytes=50 << 20),
        cost_estimate=pl.CostEstimate(
            flops=2 * vocab * count * D, bytes_accessed=vocab * D * 4, transcendentals=vocab * count
        ),
        name="head_stats",
    )(head, rows, targets)


def head_grads_kernel(vocab, order, h_ref, rows_ref, target_ref, lse_ref, factor_ref, g_ref, c_ref, flipped, delta):
    step = pl.program_id(0)
    base = order[step] * h_ref.shape[0]
    table = table_block(vocab, base, h_ref)
    flipped[...] = table.astype(WIDE).T.astype(LOW)

    @pl.when(step == 0)
    def _():
        c_ref[...] = jnp.zeros(c_ref.shape, WIDE)

    for c in range(rows_ref.shape[0] // TOKENS):
        span = slice(c * TOKENS, (c + 1) * TOKENS)
        logits, index = head_scores(vocab, base, table, rows_ref[span, :])
        onehot = (index == target_ref[:, span]).astype(WIDE)
        delta[:, span] = (
            (jnp.exp(logits - lse_ref[:, span]) - onehot) * factor_ref[:, span]
        ).astype(LOW)
    g_ref[...] = jnp.dot(delta[...], rows_ref[...], preferred_element_type=WIDE).astype(LOW)
    for c in range(rows_ref.shape[0] // TOKENS):
        span = slice(c * TOKENS, (c + 1) * TOKENS)
        c_ref[:, span] += jnp.dot(flipped[...], delta[:, span], preferred_element_type=WIDE)


def head_grads(head, rows, targets, lse, factor):
    vocab, count = head.shape[0], rows.shape[0]
    piece = head_piece(vocab)
    return pl.pallas_call(
        functools.partial(head_grads_kernel, vocab),
        grid_spec=pltpu.PrefetchScalarGridSpec(
            num_scalar_prefetch=1,
            grid=(16,),
            in_specs=[
                pl.BlockSpec((piece, D), lambda g, order: (order[g], 0)),
                once((count, D)),
                once((1, count)),
                once((1, count)),
                once((1, count)),
            ],
            out_specs=[
                pl.BlockSpec((piece, D), lambda g, order: (g, 0)),
                pl.BlockSpec((D, count), lambda g, order: (0, 0)),
            ],
            scratch_shapes=[pltpu.VMEM((D, piece), LOW), pltpu.VMEM((piece, count), LOW)],
        ),
        out_shape=[
            jax.ShapeDtypeStruct((16 * piece, D), LOW),
            jax.ShapeDtypeStruct((D, count), WIDE),
        ],
        compiler_params=pltpu.CompilerParams(vmem_limit_bytes=56 << 20),
        cost_estimate=pl.CostEstimate(
            flops=6 * vocab * count * D, bytes_accessed=vocab * D * 8, transcendentals=vocab * count
        ),
        name="head_grads",
    )(relative_blocks(), head, rows, targets, lse, factor)


def head_pass(rows_low, targets, weights_tok, head, vocab_start, token_total):
    planes = lax.axis_size("fsdp")
    gathered = jnp.concatenate(
        [rows_low] + [shift(rows_low, "fsdp", step) for step in range(1, planes)], axis=0
    )
    local = targets - vocab_start
    local = jnp.where((local >= 0) & (local < head.shape[0]), local, -1)[None, :]
    stats = head_stats(head, gathered, local)[:3].reshape(3, planes, -1)
    parts = [stats] + [
        jnp.roll(shift(stats, "fsdp", step), step, axis=1) for step in range(1, planes)
    ]
    parts = jnp.stack(parts)
    peak = jnp.max(parts[:, 0], axis=0)
    total = jnp.sum(parts[:, 1] * jnp.exp(parts[:, 0] - peak[None]), axis=0)
    lse = (peak + jnp.log(total)).reshape(-1)
    loss_part = jnp.sum((lse - jnp.sum(parts[:, 2], axis=0).reshape(-1)) * weights_tok)
    factor = weights_tok / token_total
    grad_head, partial = head_grads(head, gathered, local, lse[None, :], factor[None, :])
    partial = partial.T.reshape(planes, -1, D)
    grad_rows = partial[0]
    for step in range(1, planes):
        grad_rows = grad_rows + shift(partial[step].astype(LOW), "fsdp", planes - step).astype(WIDE)
    middle = grad_head.shape[0] // 2
    return (loss_part, grad_head[:middle], grad_head[middle:], grad_rows)


def add_low(one, other):
    return (one.astype(WIDE) + other.astype(WIDE)).astype(LOW)


def keep_half(block, mask):
    half = block.shape[0] // 2
    return add_low(block[:half], swap(block[half:], "dp", mask))


def adam_update(weight, grad, first_mom, second_mom, rate, decay):
    mom_new = BETA1 * first_mom + (1.0 - BETA1) * grad
    sec_new = BETA2 * second_mom + (1.0 - BETA2) * grad * grad
    mom_hat = mom_new / (1.0 - BETA1**STEP_COUNT)
    sec_hat = sec_new / (1.0 - BETA2**STEP_COUNT)
    weight_new = weight - rate * (mom_hat / (jnp.sqrt(sec_hat) + ADAM_EPS) + decay * weight)
    return (weight_new, mom_new, sec_new)


def exchange_kernel(planes, rows_ref, pa, pb, *refs):
    paired = planes == 4
    n = (len(refs) - 7) // (4 if paired else 2)
    parts, rows_all, head, slots = refs[:n], refs[n], refs[n + 1], refs[n + 2 : 2 * n + 2]
    send, recv, core_send, core_recv, local = refs[2 * n + 2 : 2 * n + 7]
    totals, extras = refs[2 * n + 7 : 3 * n + 7], refs[3 * n + 7 :]
    s = lax.axis_index("section")
    i = lax.axis_index("dp")
    z = lax.axis_index("fsdp")
    x, y = i % 2, i // 2
    xn, yn, diag = i + 1 - 2 * x, (i + 2) % 4, 3 - i
    partner = z + 1 - 2 * (z % 2)
    to_x, to_y, to_core = {"dp": xn}, {"dp": yn}, {"section": 1 - s}
    barrier = pltpu.get_barrier_semaphore()
    for device in [to_x, to_y, to_core] + [{"fsdp": (z + k) % planes} for k in range(1, planes)]:
        pl.semaphore_signal(barrier, inc=1, device_id=device, device_id_type=MESH)
    pl.semaphore_wait(barrier, planes + 2)
    counts = [0, 0]
    sent = []

    def put(src, dst, device):
        over = device is to_core
        k = counts[over]
        counts[over] += 1
        copy = pltpu.make_async_remote_copy(
            src_ref=src,
            dst_ref=dst,
            send_sem=(core_send if over else send).at[k],
            recv_sem=(core_recv if over else recv).at[k],
            device_id=device,
            device_id_type=MESH,
        )
        copy.start()
        sent.append(copy)
        return copy

    def take(*copies):
        for copy in copies:
            copy.wait_recv()

    piece = pa.shape[0]
    side = 4 * piece

    def head_a(xx, yy, count):
        return head.at[pl.ds(pl.multiple_of(s * 2 * side + xx * 2 * piece + yy * piece, 16), count)]

    def head_b(xx, yy, count):
        return head.at[
            pl.ds(pl.multiple_of(s * 2 * side + side + yy * 2 * piece + xx * piece, 16), count)
        ]

    own = []
    for k, (src, dst) in enumerate(
        [(rows_ref, rows_all.at[s, i, z]), (pa, head_a(x, y, piece)), (pb, head_b(x, y, piece))]
    ):
        copy = pltpu.make_async_copy(src, dst, local.at[k])
        copy.start()
        own.append(copy)
    reduce = []

    def part_of(m, plane):
        height = slots[m].shape[1]
        return parts[m].at[pl.ds(pl.multiple_of(plane * height, 16), height)]

    fetched, passed = [], []
    if paired:
        for m in range(n):
            copy = pltpu.make_async_copy(part_of(m, planes - 1 - z), totals[m], local.at[3 + m])
            copy.start()
            fetched.append(copy)
    near = [put(rows_ref, rows_all.at[s, i, z], {"fsdp": (z + k) % planes}) for k in range(1, planes)]
    head1 = [put(pa, head_a(x, y, piece), to_y), put(pb, head_b(x, y, piece), to_x)]
    if not paired:
        for m in range(n):
            for k in range(1, planes):
                target = (z + k) % planes
                reduce.append(put(part_of(m, target), slots[m].at[k - 1], {"fsdp": target}))
    for copy in own:
        copy.wait()
    take(*near)
    if paired:
        for m in range(n):
            passed.append(put(part_of(m, planes - 1 - partner), extras[m], {"fsdp": partner}))
    mid = planes // 2
    early, late = pl.ds(0, mid), pl.ds(mid, planes - mid)
    a1 = put(rows_all.at[s, i, early], rows_all.at[s, i, early], to_x)
    b1 = put(rows_all.at[s, i, late], rows_all.at[s, i, late], to_y)
    core = [put(rows_all.at[s, i], rows_all.at[s, i], to_core)]
    take(*head1)
    block = head_a(x, 0, 2 * piece)
    ha = put(block, block, to_x)
    block = head_b(0, y, 2 * piece)
    hb = put(block, block, to_y)
    take(a1, b1)
    second = []
    for who, span, device in ((i, early, to_y), (xn, early, to_y), (i, late, to_x), (yn, late, to_x)):
        block = rows_all.at[s, who, span]
        second.append(put(block, block, device))
    for who, span in ((xn, early), (yn, late)):
        block = rows_all.at[s, who, span]
        core.append(put(block, block, to_core))
    if paired:
        for copy in fetched:
            copy.wait()
        for m in range(n):
            passed[m].wait_recv()
            held = totals[m][...].astype(WIDE) + extras[m][...].astype(WIDE)
            totals[m][...] = held.astype(LOW)
            reduce.append(put(totals[m], slots[m].at[1], {"fsdp": planes - 1 - z}))
            reduce.append(put(part_of(m, partner), slots[m].at[0], {"fsdp": partner}))
    take(ha, hb)
    block = head.at[pl.ds(pl.multiple_of(s * 2 * side, 16), 2 * side)]
    core.append(put(block, block, to_core))
    take(*second)
    for who, span in ((yn, early), (diag, early), (xn, late), (diag, late)):
        block = rows_all.at[s, who, span]
        core.append(put(block, block, to_core))
    take(*reduce)
    take(*core)
    for copy in sent:
        copy.wait_send()


def exchange(planes, row_grads, pieces, parts):
    piece, vocab = pieces[0].shape
    shape = jax.ShapeDtypeStruct
    outs = [shape((2, 4, planes) + row_grads.shape, LOW), shape((16 * piece, vocab), LOW)]
    blocks = [(p.shape[0] // planes, p.shape[1]) for p in parts]
    paired = planes == 4
    outs += [shape((2 if paired else planes - 1,) + b, LOW) for b in blocks]
    copies = (planes - 1) * (1 + len(parts)) + 2 + 2 + 2 + 4
    anywhere = pl.BlockSpec(memory_space=pl.ANY)
    result = pl.pallas_call(
        functools.partial(exchange_kernel, planes),
        out_shape=outs,
        in_specs=[pl.BlockSpec(memory_space=pltpu.VMEM)] * 3 + [anywhere] * len(parts),
        out_specs=[anywhere] * len(outs),
        scratch_shapes=[pltpu.SemaphoreType.DMA((copies,))] * 2
        + [pltpu.SemaphoreType.DMA((8,))] * 2
        + [pltpu.SemaphoreType.DMA((3 + len(parts),))]
        + ([pltpu.VMEM(b, LOW) for b in blocks] * 2 if paired else []),
        compiler_params=pltpu.CompilerParams(
            collective_id=2, has_side_effects=True, vmem_limit_bytes=16 << 20
        ),
        name="exchange",
    )(row_grads, *pieces, *parts)
    return result[0], result[1], result[2:]


def block_of(vocab_rows):
    return 800 if vocab_rows % 800 == 0 else 400


def chunk_of(lists):
    return 32 if lists <= 64 else 16


def start_chunks(lists, length, stride, step, steps, starts, rows_hbm, buffer, sem):
    chunk = chunk_of(lists)

    def one(k, carry):
        at = jnp.minimum(starts[k * steps + step] // 16 * 16, length - chunk)
        src = rows_hbm.at[pl.ds(pl.multiple_of(k * stride + at, 16), chunk)]
        pltpu.make_async_copy(src, buffer.at[pl.ds(pl.multiple_of(k * chunk, 16), chunk)], sem).start()
        return carry

    lax.fori_loop(0, lists, one, 0)


def block_grad(
    lists, length, steps, step, starts, passes, bases, rows_hbm, ids_ref, near_ref, buffers, hot, wide_hot, grad, sems
):
    chunk = chunk_of(lists)
    slot = step % 2
    spare = buffers.at[2]
    width = grad.shape[0]
    stride = rows_hbm.shape[0] // lists

    @pl.when(step == 0)
    def _():
        start_chunks(lists, length, stride, 0, steps, starts, rows_hbm, buffers.at[0], sems.at[0])

    @pl.when(step + 1 < steps)
    def _():
        start_chunks(lists, length, stride, step + 1, steps, starts, rows_hbm, buffers.at[1 - slot], sems.at[1 - slot])

    pltpu.make_async_copy(buffers.at[slot], buffers.at[slot], sems.at[slot]).wait()
    lanes = lax.broadcasted_iota(jnp.int32, (chunk, width), 1) + bases[step]
    within = lax.broadcasted_iota(jnp.int32, (chunk, width), 0)

    def mark(shifted):
        def one(k, carry):
            begin = starts[k * steps + step] // 16 * 16 + shifted
            at = jnp.minimum(begin, length - chunk)
            ids = ids_ref[pl.ds(pl.multiple_of(k * length + at, 16), chunk), :]
            same = (ids == lanes) & (within >= begin - at)
            hot[pl.ds(pl.multiple_of(k * chunk, 16), chunk), :] = same.astype(WIDE).astype(LOW)
            return carry

        lax.fori_loop(0, lists, one, 0)

    down = lax.broadcasted_iota(jnp.int32, (width, lists * chunk), 0) + bases[step]
    wide_hot[...] = (down == near_ref[0]).astype(WIDE).astype(LOW)
    grad[...] = jnp.dot(wide_hot[...], buffers[slot], preferred_element_type=WIDE)

    def more(p, carry):
        mark(p * chunk)

        def one(k, inner):
            begin = starts[k * steps + step] // 16 * 16 + p * chunk
            at = jnp.minimum(begin, length - chunk)
            src = rows_hbm.at[pl.ds(pl.multiple_of(k * stride + at, 16), chunk)]
            pltpu.make_async_copy(
                src, spare.at[pl.ds(pl.multiple_of(k * chunk, 16), chunk)], sems.at[2]
            ).start()
            return inner

        lax.fori_loop(0, lists, one, 0)
        pltpu.make_async_copy(spare, spare, sems.at[2]).wait()
        grad[...] += contract_rows(hot[...], spare[...])
        return carry

    lax.fori_loop(1, passes[step], more, 0)


def table_square_kernel(lists, length, steps, starts, passes, bases, rows_hbm, ids_ref, near_ref, out, buffers, hot, wide_hot, grad, sems):
    step = pl.program_id(0)
    block_grad(lists, length, steps, step, starts, passes, bases, rows_hbm, ids_ref, near_ref, buffers, hot, wide_hot, grad, sems)
    part = jnp.sum((grad[...] * grad[...]).reshape(-1, 8, D), axis=0)
    part = jnp.where(passes[step] > 0, part, 0.0)

    @pl.when(step == 0)
    def _():
        out[...] = part

    @pl.when(step > 0)
    def _():
        out[...] += part


def table_adam_kernel(
    lists, length, steps, rate, decay, starts, passes, bases, clip, rows_hbm, ids_ref, near_ref, w, m, v, w_new, m_new, v_new, low, buffers, hot, wide_hot, grad, sems
):
    step = pl.program_id(0)
    block_grad(lists, length, steps, step, starts, passes, bases, rows_hbm, ids_ref, near_ref, buffers, hot, wide_hot, grad, sems)
    weight, mom, sec = adam_update(w[...], grad[...] * clip[0], m[...], v[...], rate, decay)
    w_new[...] = weight
    m_new[...] = mom
    v_new[...] = sec
    low[...] = weight.astype(LOW)


def table_scratch(lists, width):
    chunk = chunk_of(lists)
    return [
        pltpu.VMEM((3, lists * chunk, D), LOW),
        pltpu.VMEM((lists * chunk, width), LOW),
        pltpu.VMEM((width, lists * chunk), LOW),
        pltpu.VMEM((width, D), WIDE),
        pltpu.SemaphoreType.DMA((3,)),
    ]


def chunk_scalars(ids_sorted, bases, width):
    chunk = chunk_of(ids_sorted.shape[0])
    edges = bases[None, :, None]
    starts = jnp.sum((ids_sorted[:, None, :] < edges).astype(jnp.int32), axis=-1)
    ends = jnp.sum((ids_sorted[:, None, :] < edges + width).astype(jnp.int32), axis=-1)
    passes = jnp.max((ends - starts // 16 * 16 + chunk - 1) // chunk, axis=0)
    lists, length = ids_sorted.shape
    groups = length // 16
    begin = (starts // 16).T
    at = jnp.minimum(begin, groups - chunk // 16)
    by_group = ids_sorted.reshape(lists, groups, 16).transpose(1, 0, 2).reshape(groups, -1)
    widen = jnp.arange(lists * 16)[None, :] // 16 == jnp.arange(lists)[:, None]
    both = jnp.concatenate([at, begin], axis=0).astype(LOW)
    both = jnp.dot(both, widen.astype(LOW), preferred_element_type=WIDE).astype(jnp.int32)
    both = lax.optimization_barrier(both)
    steps = begin.shape[0]
    pieces = []
    for k in range(chunk // 16):
        wanted = both[:steps] + k
        found = jnp.zeros(wanted.shape, jnp.int32)
        for g in range(groups):
            found = jnp.where(wanted == g, by_group[g][None], found)
        found = jnp.where(wanted >= both[steps:], found, -(1 << 30))
        pieces.append(lax.optimization_barrier(found).reshape(-1, lists, 16))
    near = jnp.stack(pieces, axis=2).reshape(begin.shape[0], 1, -1)
    return starts.reshape(-1), jnp.maximum(passes, 1), near


def table_square(ids_sorted, ids_column, rows_flat, rank, ranks, vocab_rows):
    lists, length = ids_sorted.shape
    width = block_of(vocab_rows)
    total = vocab_rows // width
    steps = -(-total // ranks)
    blocks = rank + ranks * jnp.arange(steps, dtype=jnp.int32)
    bases = blocks * width
    starts, passes, near = chunk_scalars(ids_sorted, bases, width)
    passes = jnp.where(blocks < total, passes, 0)
    out = pl.pallas_call(
        functools.partial(table_square_kernel, lists, length, steps),
        grid_spec=pltpu.PrefetchScalarGridSpec(
            num_scalar_prefetch=3,
            grid=(steps,),
            in_specs=[
                pl.BlockSpec(memory_space=pl.ANY),
                pl.BlockSpec(
                    (lists * length, 1), lambda g, *_: (0, 0), pipeline_mode=pl.Buffered(1)
                ),
                pl.BlockSpec((1, 1, near.shape[2]), lambda g, *_: (g, 0, 0)),
            ],
            out_specs=pl.BlockSpec((8, D), lambda g, *_: (0, 0)),
            scratch_shapes=table_scratch(lists, width),
        ),
        out_shape=jax.ShapeDtypeStruct((8, D), WIDE),
        compiler_params=pltpu.CompilerParams(vmem_limit_bytes=56 << 20),
        name="table_square",
    )(starts, passes, bases, rows_flat, ids_column, near)
    return jnp.sum(out)


def table_adam(ids_sorted, ids_column, rows_flat, clip_scale, table, mom, sec, rate, decay):
    lists, length = ids_sorted.shape
    vocab_rows = table.shape[0]
    width = block_of(vocab_rows)
    steps = vocab_rows // width
    bases = jnp.arange(steps, dtype=jnp.int32) * width
    starts, passes, near = chunk_scalars(ids_sorted, bases, width)
    block = pl.BlockSpec((width, D), lambda g, *_: (g, 0))
    wide = jax.ShapeDtypeStruct(table.shape, WIDE)
    return pl.pallas_call(
        functools.partial(table_adam_kernel, lists, length, steps, rate, decay),
        grid_spec=pltpu.PrefetchScalarGridSpec(
            num_scalar_prefetch=4,
            grid=(steps,),
            in_specs=[
                pl.BlockSpec(memory_space=pl.ANY),
                pl.BlockSpec(
                    (lists * length, 1), lambda g, *_: (0, 0), pipeline_mode=pl.Buffered(1)
                ),
                pl.BlockSpec((1, 1, near.shape[2]), lambda g, *_: (g, 0, 0)),
                block,
                block,
                block,
            ],
            out_specs=[block] * 4,
            scratch_shapes=table_scratch(lists, width),
        ),
        out_shape=[wide, wide, wide, jax.ShapeDtypeStruct(table.shape, LOW)],
        compiler_params=pltpu.CompilerParams(vmem_limit_bytes=60 << 20),
        cost_estimate=pl.CostEstimate(
            flops=steps * 2 * width * lists * chunk_of(lists) * D,
            bytes_accessed=table.size * 26,
            transcendentals=table.size,
        ),
        name="table_adam",
    )(starts, passes, bases, clip_scale.reshape(1), rows_flat, ids_column, near, table, mom, sec)


HEAD_BLOCK = 800


def head_adam_kernel(rate, decay, clip, grad, w, m, v, w_new, m_new, v_new, low):
    scaled = grad[...].astype(WIDE) * clip[0]
    weight, mom, sec = adam_update(w[...], scaled, m[...], v[...], rate, decay)
    w_new[...] = weight
    m_new[...] = mom
    v_new[...] = sec
    low[...] = weight.astype(LOW)


def head_adam(grad, clip_scale, head, mom, sec, rate, decay):
    vocab = head.shape[1]
    block = pl.BlockSpec((HEAD_BLOCK, D), lambda g, *_: (g, 0))
    wide = jax.ShapeDtypeStruct((vocab, D), WIDE)
    results = pl.pallas_call(
        functools.partial(head_adam_kernel, rate, decay),
        grid_spec=pltpu.PrefetchScalarGridSpec(
            num_scalar_prefetch=1,
            grid=(-(-vocab // HEAD_BLOCK),),
            in_specs=[block] * 4,
            out_specs=[block] * 4,
        ),
        out_shape=[wide, wide, wide, jax.ShapeDtypeStruct((vocab, D), LOW)],
        compiler_params=pltpu.CompilerParams(vmem_limit_bytes=56 << 20),
        cost_estimate=pl.CostEstimate(
            flops=head.size * 20, bytes_accessed=head.size * 28, transcendentals=head.size
        ),
        name="head_adam",
    )(clip_scale.reshape(1), grad, head.T, mom.T, sec.T)
    return [item.T for item in results]


def small_gather_kernel(axes, sizes, *refs):
    n = (len(refs) - 2) // 2
    blocks, outs, send, recv = refs[:n], refs[n : 2 * n], refs[2 * n], refs[2 * n + 1]
    mine = [lax.axis_index(axis) for axis in axes]
    slot = 0
    for index, size in zip(mine, sizes):
        slot = slot * size + index
    offsets = [()]
    for size in sizes:
        offsets = [o + (k,) for o in offsets for k in range(size)]
    peers = [
        {axis: (index + k) % size for axis, index, size, k in zip(axes, mine, sizes, offset)}
        for offset in offsets[1:]
    ]
    barrier = pltpu.get_barrier_semaphore()
    for peer in peers:
        pl.semaphore_signal(barrier, inc=1, device_id=peer, device_id_type=MESH)
    pl.semaphore_wait(barrier, len(peers))
    copies = []
    for m in range(n):
        for k, peer in enumerate(peers):
            copy = pltpu.make_async_remote_copy(
                src_ref=blocks[m],
                dst_ref=outs[m].at[slot],
                send_sem=send.at[m * len(peers) + k],
                recv_sem=recv.at[m * len(peers) + k],
                device_id=peer,
                device_id_type=MESH,
            )
            copy.start()
            copies.append(copy)
        outs[m][slot] = blocks[m][...]
    for copy in copies:
        copy.wait()


def small_gather(blocks, axes, identity):
    sizes = [lax.axis_size(axis) for axis in axes]
    count = math.prod(sizes)
    copies = (count - 1) * len(blocks)
    whole = pl.BlockSpec(memory_space=pltpu.VMEM)
    return pl.pallas_call(
        functools.partial(small_gather_kernel, axes, sizes),
        out_shape=[jax.ShapeDtypeStruct((count,) + b.shape, b.dtype) for b in blocks],
        in_specs=[whole] * len(blocks),
        out_specs=[whole] * len(blocks),
        scratch_shapes=[pltpu.SemaphoreType.DMA((copies,))] * 2,
        compiler_params=pltpu.CompilerParams(collective_id=identity, has_side_effects=True),
        name=f"small_gather_{identity}",
    )(*blocks)


def finish_kernel(n, me, *refs):
    parts, slots, pieces = refs[:n], refs[n : 2 * n], refs[2 * n : 2 * n + 2]
    shards, out = refs[2 * n + 2 : 3 * n + 2], refs[3 * n + 2]
    total = jnp.zeros((), WIDE)
    for m in range(n):
        held = parts[m][...].astype(WIDE)
        for k in range(slots[m].shape[0]):
            held = held + slots[m][k].astype(WIDE)
        low = held.astype(LOW)
        shards[m][...] = low
        held = low.astype(WIDE)
        total = total + jnp.sum(held * held)
    for piece in pieces:
        held = piece[...].astype(WIDE)
        total = total + jnp.sum(held * held)
    out[...] = jnp.full(out.shape, total, WIDE)


def finish(me, parts, slots, pieces):
    blocks = [slot.shape[1:] for slot in slots]
    whole = lambda shape: pl.BlockSpec(shape, lambda g, *_: (0,) * len(shape))
    results = pl.pallas_call(
        functools.partial(finish_kernel, len(parts)),
        grid_spec=pltpu.PrefetchScalarGridSpec(
            num_scalar_prefetch=1,
            grid=(1,),
            in_specs=[pl.BlockSpec(block, lambda g, me: (me[0], 0)) for block in blocks]
            + [whole(item.shape) for item in list(slots) + list(pieces)],
            out_specs=[whole(block) for block in blocks] + [whole((8, 128))],
        ),
        out_shape=[jax.ShapeDtypeStruct(block, LOW) for block in blocks]
        + [jax.ShapeDtypeStruct((8, 128), WIDE)],
        compiler_params=pltpu.CompilerParams(vmem_limit_bytes=40 << 20),
        name="finish",
    )(me.astype(jnp.int32).reshape(1), *parts, *slots, *pieces)
    return list(results[:-1]), results[-1][0, 0]


def per_device(
    token_ids,
    next_ids,
    seq_lengths,
    embedding,
    embedding_mom,
    embedding_sec,
    head_table,
    head_mom,
    head_sec,
    w_qkv,
    qkv_mom,
    qkv_sec,
    w_out,
    out_mom,
    out_sec,
    w_gateup,
    gateup_mom,
    gateup_sec,
    w_down,
    down_mom,
    down_sec,
    gains,
    gains_mom,
    gains_sec,
):
    planes = lax.axis_size("fsdp")
    replicas = lax.axis_size("dp")
    first = lax.axis_index("section") == 0
    first_f = first.astype(WIDE)
    me = lax.axis_index("fsdp")
    token_total = jnp.sum(seq_lengths).astype(WIDE)
    tokens = MB * ROW

    my_ids = jnp.stack([token_ids.reshape(-1), next_ids.reshape(-1)])
    ids_all, gains_all = small_gather([my_ids, gains[0]], ("dp", "fsdp"), 3)
    ids_all = ids_all.reshape(replicas, planes, 2, tokens)
    gains_full = gains_all[:planes].transpose(1, 0, 2).reshape(3, D)
    gains_full = lax.optimization_barrier(gains_full.astype(LOW)).astype(WIDE)
    group_ids = pick(ids_all, lax.axis_index("dp"))
    rel_ids = jnp.stack([pick(group_ids, (me - step) % planes) for step in range(planes)])
    my_kind = jnp.where(first, rel_ids[:, 0], rel_ids[:, 1])
    vocab_rows = embedding.shape[0]
    vocab_start = me * vocab_rows
    local = my_kind - vocab_start
    inside = (local >= 0) & (local < vocab_rows)
    found = jnp.take(embedding, jnp.clip(local, 0, vocab_rows - 1), axis=0)
    found = lax.optimization_barrier(jnp.where(inside[..., None], found, 0.0).astype(LOW))
    looked = found[0].astype(WIDE)
    for step in range(1, planes):
        looked = looked + shift(found[step], "fsdp", planes - step).astype(WIDE)
    next_embed = swap(looked.astype(LOW), "section", 1).astype(WIDE)

    lists = ids_all.transpose(2, 0, 1, 3).reshape(-1, tokens) - vocab_start
    place = jnp.arange(tokens)
    before = (lists[:, None, :] < lists[:, :, None]) | (
        (lists[:, None, :] == lists[:, :, None]) & (place[None, None, :] < place[None, :, None])
    )
    ranks = jnp.sum(before.astype(jnp.int32), axis=-1)
    sorted_ids = jnp.sum(
        jnp.where(ranks[:, None, :] == place[None, :, None], lists[:, None, :], 0), axis=-1
    )
    own_list = (
        lax.axis_index("section") * replicas + lax.axis_index("dp")
    ) * planes + me
    arrange = (pick(ranks, own_list)[None, :] == place[:, None]).astype(LOW)

    full = gather_weights(
        planes,
        replicas,
        [w_qkv[0].astype(LOW), w_out[0].astype(LOW), w_gateup[0].astype(LOW), w_down[0].astype(LOW)],
    )
    layer_weights = (full[0], full[1], full[2], full[3], gains_full[0], gains_full[1])
    head_gain = gains_full[2]

    first_out, _ = layer_fwd(looked, layer_weights)
    middle = swap(first_out.astype(LOW), "section", 1).astype(WIDE)
    layer_in = jnp.where(first, looked, middle)
    layer_out, saved = layer_fwd(layer_in, layer_weights)
    final_state = norm_fwd(layer_out, head_gain)
    arrived = swap(final_state.astype(LOW), "section", 1).astype(WIDE)
    merged_in = jnp.where(first, arrived + next_embed, layer_out)
    head_in = norm_fwd(merged_in, head_gain)

    lengths = seq_lengths.reshape(replicas, planes, MB)[lax.axis_index("dp")]
    lengths = jnp.stack([pick(lengths, (me - step) % planes) for step in range(planes)])
    targets_main = rel_ids[:, 1].reshape(planes, MB, ROW)
    shifted = jnp.concatenate([targets_main[..., 1:], targets_main[..., :1]], axis=-1)
    targets = jnp.where(first, shifted, targets_main)
    limit = lengths - first.astype(jnp.int32)
    positions = jnp.arange(ROW, dtype=jnp.int32)
    weights_tok = (positions < limit[..., None]).astype(WIDE) * jnp.where(first, MTP_WEIGHT, 1.0)
    left = [saved[0], saved[6], saved[8]]
    left_all = spread(
        lambda index: jnp.concatenate(left + [sub_quarter(saved[10], planes, index)], axis=1)
    )
    loss_part, mine, theirs, grad_in = head_pass(
        head_in.astype(LOW),
        targets.reshape(-1),
        weights_tok.reshape(-1),
        head_table.T,
        vocab_start,
        token_total,
    )
    sorted_ids, loss_part = lax.optimization_barrier((sorted_ids, loss_part))
    merged_grad, mtp_gain = norm_back(merged_in, head_gain, grad_in)
    merged_low = merged_grad.astype(LOW)
    sent = swap(merged_low, "section", 1).astype(WIDE)
    top_grad, top_gain = norm_back(layer_out, head_gain, grad_in + sent)
    head_gain_grad = jnp.where(first, mtp_gain, top_gain)
    half = add_low(mine, swap(theirs, "section", 1))
    top_grad, left_all = lax.optimization_barrier((top_grad, left_all))
    below, _, _ = layer_back(layer_in, layer_weights, saved, top_grad)
    below, half = lax.optimization_barrier((below.astype(LOW), half))
    side = half.shape[0] // 2
    piece_a, piece_b = keep_half(half[:side], 1), keep_half(half[side:], 2)
    upstream = jnp.where(first, swap(below, "section", 1).astype(WIDE), top_grad)
    grad_inputs, right, gain_parts = layer_back(layer_in, layer_weights, saved, upstream)
    grad_packed, after_low, grad_gu, upstream_low = right
    after_low, piece_a, piece_b = lax.optimization_barrier((after_low, piece_a, piece_b))
    piece_a, piece_b = keep_half(piece_a, 2), keep_half(piece_b, 1)
    early = spread(
        lambda index: jnp.concatenate([upstream_low, quarter(grad_gu, index)], axis=1)
    )
    late = spread(
        lambda index: jnp.concatenate([quarter(after_low, index), quarter(grad_packed, index)], axis=1)
    )
    cut = D // SHARE
    parts = [
        contract_rows(left_all[:, 2 * D : 3 * D], early[:, D:]),
        contract_rows(left_all[:, 3 * D :], early[:, :D]),
        contract_rows(left_all[:, :D], late[:, cut:]),
        contract_rows(left_all[:, D : 2 * D], late[:, :cut]),
    ]
    parts = [part.astype(LOW) for part in parts]
    gains_grad = jnp.stack([gain_parts[0], gain_parts[1], head_gain_grad])

    row_grads = jnp.where(first, grad_inputs.astype(LOW), sent.astype(LOW))
    row_grads = jnp.dot(arrange, row_grads, preferred_element_type=WIDE).astype(LOW)
    row_grads = jnp.concatenate(
        [row_grads, gains_grad.astype(LOW), jnp.zeros((13, D), LOW)], axis=0
    )
    rows_all, grad_head, slots = exchange(planes, row_grads, (piece_a, piece_b), parts)
    rows_flat = rows_all.reshape(-1, D)
    gains_grad = pick(rows_all[:, :, :, tokens : tokens + 3], lax.axis_index("section"))
    gains_grad = jnp.sum(gains_grad.astype(WIDE), axis=(0, 1))
    gains_grad = lax.dynamic_slice_in_dim(gains_grad, me * (D // planes), D // planes, 1)
    ids_column = sorted_ids.reshape(-1, 1)

    shards, shard_squares = finish(me, parts, slots, (piece_a, piece_b))
    group = lax.axis_index("section") * replicas + lax.axis_index("dp")
    squares = table_square(sorted_ids, ids_column, rows_flat, group, 2 * replicas, vocab_rows)
    squares = squares + shard_squares + jnp.sum(gains_grad * gains_grad) / replicas
    totals = jnp.stack([squares, loss_part / planes])[:, None] * jnp.ones((1, 128), WIDE)
    totals = jnp.sum(small_gather([totals], ("section", "dp", "fsdp"), 4)[0], axis=0)[:, 0]
    grad_norm = jnp.sqrt(totals[0])
    loss_total = totals[1]
    clip_scale = CLIP / jnp.maximum(grad_norm, CLIP)

    shards, clip_scale = lax.optimization_barrier((shards, clip_scale))
    widths = [0, 2 * D, 3 * D, 3 * D + 3 * cut, 4 * D]
    packed = jnp.concatenate(shards, axis=1)
    rank = plane_rank()
    others = [packed] + [swap(packed, "dp", mask) for mask in range(1, SHARE)]
    layer_grads = [
        in_order([other[:, lo:hi] for other in others], rank, 0 if index == 1 else 1).astype(WIDE)
        for index, (lo, hi) in enumerate(zip(widths[:-1], widths[1:]))
    ]
    params = (w_qkv[0], w_out[0], w_gateup[0], w_down[0], gains[0])
    grads_all = (
        layer_grads[2],
        layer_grads[3],
        layer_grads[0],
        layer_grads[1],
        gains_grad,
    )
    moments = (
        (qkv_mom[0], qkv_sec[0]),
        (out_mom[0], out_sec[0]),
        (gateup_mom[0], gateup_sec[0]),
        (down_mom[0], down_sec[0]),
        (gains_mom[0], gains_sec[0]),
    )
    rates = (0.03, 0.12, 0.03, 0.03, 0.6)
    decays = (0.1, 0.1, 0.1, 0.1, 0.0)
    outputs = [loss_total, token_total, grad_norm]
    outputs += table_adam(
        sorted_ids,
        ids_column,
        rows_flat,
        clip_scale,
        embedding,
        embedding_mom,
        embedding_sec,
        0.6,
        0.1,
    )
    outputs += head_adam(grad_head, clip_scale, head_table, head_mom, head_sec, 0.03, 0.1)
    for index in range(5):
        weight_new, mom_new, sec_new = adam_update(
            params[index],
            grads_all[index] * clip_scale,
            moments[index][0],
            moments[index][1],
            rates[index],
            decays[index],
        )
        outputs.extend([weight_new[None], mom_new[None], sec_new[None]])
        if index < 4:
            outputs.append(weight_new.astype(LOW)[None])
    return tuple(outputs)


def solution(mesh):
    placed = (
        P(("dp", "fsdp"), None),
        P(("dp", "fsdp"), None),
        P(),
        P("fsdp", None),
        P("fsdp", None),
        P("fsdp", None),
        P(None, "fsdp"),
        P(None, "fsdp"),
        P(None, "fsdp"),
        P("section", "fsdp", None),
        P("section", "fsdp", None),
        P("section", "fsdp", None),
        P("section", "fsdp", None),
        P("section", "fsdp", None),
        P("section", "fsdp", None),
        P("section", "fsdp", None),
        P("section", "fsdp", None),
        P("section", "fsdp", None),
        P("section", "fsdp", None),
        P("section", "fsdp", None),
        P("section", "fsdp", None),
        P("section", None, "fsdp"),
        P("section", None, "fsdp"),
        P("section", None, "fsdp"),
    )
    return jax.shard_map(
        per_device,
        mesh=mesh,
        in_specs=placed,
        out_specs=(
            P(),
            P(),
            P(),
            P("fsdp", None),
            P("fsdp", None),
            P("fsdp", None),
            P("fsdp", None),
            P(None, "fsdp"),
            P(None, "fsdp"),
            P(None, "fsdp"),
            P(None, "fsdp"),
            P("section", "fsdp", None),
            P("section", "fsdp", None),
            P("section", "fsdp", None),
            P("section", "fsdp", None),
            P("section", "fsdp", None),
            P("section", "fsdp", None),
            P("section", "fsdp", None),
            P("section", "fsdp", None),
            P("section", "fsdp", None),
            P("section", "fsdp", None),
            P("section", "fsdp", None),
            P("section", "fsdp", None),
            P("section", "fsdp", None),
            P("section", "fsdp", None),
            P("section", "fsdp", None),
            P("section", "fsdp", None),
            P("section", None, "fsdp"),
            P("section", None, "fsdp"),
            P("section", None, "fsdp"),
        ),
        check_vma=False,
    )
```

```python
import functools
import math

import jax
import jax.numpy as jnp
from jax import lax
from jax.experimental import pallas as pl
from jax.experimental.pallas import tpu as pltpu
from jax.sharding import PartitionSpec as P

D = 768
HEADS = 12
HEAD_DIM = 64
FF = 3072
ROW = 128
MB = 2
STEP_COUNT = 10
SHARE = 4


EPS = 1e-05
MTP_WEIGHT = 0.3
CLIP = 0.01
BETA1 = 0.9
BETA2 = 0.95
ADAM_EPS = 1e-08
LOW = jnp.bfloat16
WIDE = jnp.float32

AHEAD = 2
MESH = pl.DeviceIdType.MESH

def weights_kernel(planes, units, rows, *refs):
    n = len(rows)
    own, full = refs[:n], refs[n : 2 * n]
    send, recv, local = refs[2 * n :]
    z = lax.axis_index("fsdp")
    i = lax.axis_index("dp")
    x, y = i % 2, i // 2
    q = i
    xn, yn = i + 1 - 2 * x, (i + 2) % 4
    near, far = z + 1 - 2 * (z % 2), planes - 1 - z
    beyond = planes - 1 - near
    to_x, to_y, to_near, to_far = {"dp": xn}, {"dp": yn}, {"fsdp": near}, {"fsdp": far}
    barrier = pltpu.get_barrier_semaphore()
    for device in (to_x, to_y, to_near, to_far):
        pl.semaphore_signal(barrier, inc=1, device_id=device, device_id_type=MESH)
    pl.semaphore_wait(barrier, 4)
    keep = []
    for m in range(n):
        c = pltpu.make_async_copy(
            own[m], full[m].at[pl.ds(pl.multiple_of(z * rows[m], 16), rows[m]), :], local.at[m]
        )
        c.start()
        keep.append(c)
    started = []

    def put(src, dst, k, device):
        copy = pltpu.make_async_remote_copy(
            src_ref=src,
            dst_ref=dst,
            send_sem=send.at[k],
            recv_sem=recv.at[k],
            device_id=device,
            device_id_type=MESH,
        )
        copy.start()
        started.append(copy)
        return copy

    def block(u, plane, part):
        m, cols, _ = units[u]
        r = rows[m] // 4
        return full[m].at[pl.ds(pl.multiple_of(plane * rows[m] + part * r, 16), r), pl.ds(*cols)]

    sources = (near, far, beyond)
    zs, seconds, thirds = {}, {}, []
    total = len(units)

    def first(u):
        m, cols, _ = units[u]
        r = rows[m] // 4
        src = own[m].at[pl.ds(pl.multiple_of(q * r, 16), r), pl.ds(*cols)]
        zs[u, 0] = put(src, block(u, z, q), 12 * u, to_near)
        zs[u, 1] = put(src, block(u, z, q), 12 * u + 1, to_far)

    def onward(u):
        zs[u, 1].wait_recv()
        zs[u, 2] = put(block(u, far, q), block(u, far, q), 12 * u + 2, to_near)

    def second(u, j):
        if j != 1:
            zs[u, j].wait_recv()
        b = block(u, sources[j], q)
        seconds[u, j] = put(b, b, 12 * u + 3 + j, to_y if units[u][2] else to_x)

    def third(u, j):
        seconds[u, j].wait_recv()
        order = units[u][2]
        for w, part in enumerate((q, yn if order else xn)):
            b = block(u, sources[j], part)
            thirds.append(put(b, b, 12 * u + 6 + 2 * j + w, to_x if order else to_y))

    pairs = [(u, u + 1) for u in range(0, total, 2)]
    for ahead in range(AHEAD):
        for u in pairs[ahead]:
            first(u)
    for t in range(len(pairs) + 2):
        if t < len(pairs):
            for u in pairs[t]:
                onward(u)
            if t + AHEAD < len(pairs):
                for u in pairs[t + AHEAD]:
                    first(u)
            for j in (0, 1):
                for u in pairs[t]:
                    second(u, j)
        if 1 <= t <= len(pairs):
            for u in pairs[t - 1]:
                second(u, 2)
            for j in (0, 1):
                for u in pairs[t - 1]:
                    third(u, j)
        if t >= 2:
            for u in pairs[t - 2]:
                third(u, 2)
    for c in thirds:
        c.wait_recv()
    for c in started:
        c.wait_send()
    for c in keep:
        c.wait()


def gather_weights(planes, replicas, shards):
    rows = [w.shape[0] for w in shards]
    if planes != 4 or replicas != 4 or any(r % (SHARE * 16) for r in rows):
        return [lax.all_gather(w, "fsdp", axis=0, tiled=True) for w in shards]
    units = []
    for m, w in enumerate(shards):
        width = w.shape[1]
        parts = 4 if width > 4096 else 2
        step = width // parts
        for p in range(parts):
            units.append((m, (p * step, step), p % 2))
    copies = len(units) * 12
    return pl.pallas_call(
        functools.partial(weights_kernel, planes, units, rows),
        out_shape=[jax.ShapeDtypeStruct((planes * w.shape[0], w.shape[1]), w.dtype) for w in shards],
        in_specs=[pl.BlockSpec(memory_space=pltpu.VMEM)] * len(shards),
        out_specs=[pl.BlockSpec(memory_space=pl.ANY)] * len(shards),
        scratch_shapes=[pltpu.SemaphoreType.DMA((copies,)), pltpu.SemaphoreType.DMA((copies,)), pltpu.SemaphoreType.DMA((len(shards),))],
        compiler_params=pltpu.CompilerParams(collective_id=1, has_side_effects=True),
        name="gather_weights",
    )(*shards)


def norm_fwd(values, scale_gain):
    inverse = lax.rsqrt(jnp.mean(values * values, axis=-1, keepdims=True) + EPS)
    return values * inverse * scale_gain


def norm_back(values, scale_gain, upstream):
    _, pullback = jax.vjp(norm_fwd, values, scale_gain)
    return pullback(upstream)


def rope_tables(row_count, head_width):
    half_width = head_width // 2
    position = jnp.arange(row_count, dtype=jnp.float32)[:, None]
    frequency = 10000.0 ** (-jnp.arange(half_width, dtype=jnp.float32) / half_width)
    angles = position * frequency[None, :]
    return (jnp.cos(angles), jnp.sin(angles))


def rotate(values, cosine, sine_table):
    half_width = values.shape[-1] // 2
    first, second = (values[..., :half_width], values[..., half_width:])
    return jnp.concatenate(
        [first * cosine - second * sine_table, second * cosine + first * sine_table], axis=-1
    )


def contract_rows(left, right):
    return lax.dot_general(
        left, right, (((0,), (0,)), ((), ())), preferred_element_type=jnp.float32
    )


def contract_cols(left, right):
    return lax.dot_general(
        left, right, (((1,), (1,)), ((), ())), preferred_element_type=jnp.float32
    )


def swiglu(gate_up):
    return jax.nn.silu(gate_up[:, :FF]) * gate_up[:, FF:]


def shift(block, axis, distance):
    count = lax.axis_size(axis)
    return lax.ppermute(block, axis, [(i, (i + distance) % count) for i in range(count)])


def swap(block, axis, mask):
    count = lax.axis_size(axis)
    return lax.ppermute(block, axis, [(i, i ^ mask) for i in range(count)])


def pick(array, index, axis=0):
    return lax.dynamic_index_in_dim(array, index, axis, keepdims=False)


def layer_fwd(inputs, weights):
    w_qkv, w_out, w_gateup, w_down, attn_gain, ffn_gain = weights
    normed = norm_fwd(inputs, attn_gain).astype(LOW)
    packed = jnp.dot(normed, w_qkv, preferred_element_type=WIDE)
    split = packed.reshape(MB, ROW, 3, HEADS, HEAD_DIM).transpose(2, 0, 3, 1, 4)
    split = split.reshape(3, MB * HEADS, ROW, HEAD_DIM)
    cosine, sine_table = rope_tables(ROW, HEAD_DIM)
    queries = rotate(split[0], cosine, sine_table).astype(LOW)
    keys_rot = rotate(split[1], cosine, sine_table).astype(LOW)
    values_low = split[2].astype(LOW)
    scores = jnp.einsum(
        "hqd,hkd->hqk", queries, keys_rot, preferred_element_type=WIDE
    ) * HEAD_DIM ** (-0.5)
    position = jnp.arange(ROW)
    causal = position[:, None] >= position[None, :]
    scores = jnp.where(causal[None], scores, -1e30)
    shifted = jnp.exp(scores - jnp.max(scores, axis=-1, keepdims=True))
    probs = shifted / jnp.sum(shifted, axis=-1, keepdims=True)
    probs_low = probs.astype(LOW)
    mixed = jnp.einsum("hqk,hkd->hqd", probs_low, values_low, preferred_element_type=WIDE)
    mixed = mixed.reshape(MB, HEADS, ROW, HEAD_DIM).transpose(0, 2, 1, 3)
    mixed_low = mixed.reshape(MB * ROW, D).astype(LOW)
    after_attn = inputs + jnp.dot(mixed_low, w_out, preferred_element_type=WIDE)
    normed_ffn = norm_fwd(after_attn, ffn_gain).astype(LOW)
    gate_up = jnp.dot(normed_ffn, w_gateup, preferred_element_type=WIDE)
    hidden = swiglu(gate_up).astype(LOW)
    output = after_attn + jnp.dot(hidden, w_down, preferred_element_type=WIDE)
    saved = (
        normed,
        queries,
        keys_rot,
        values_low,
        probs,
        probs_low,
        mixed_low,
        after_attn,
        normed_ffn,
        gate_up,
        hidden,
    )
    return (output, saved)


def layer_back(inputs, weights, saved, upstream):
    w_qkv, w_out, w_gateup, w_down, attn_gain, ffn_gain = weights
    (
        normed,
        queries,
        keys_rot,
        values_low,
        probs,
        probs_low,
        mixed_low,
        after_attn,
        normed_ffn,
        gate_up,
        hidden,
    ) = saved
    upstream_low = upstream.astype(LOW)
    grad_hidden = contract_cols(upstream_low, w_down)
    _, pullback = jax.vjp(swiglu, gate_up)
    grad_gu = pullback(grad_hidden)[0].astype(LOW)
    grad_nffn = contract_cols(grad_gu, w_gateup)
    back_ffn, grad_ffn_gain = norm_back(after_attn, ffn_gain, grad_nffn)
    grad_after = upstream + back_ffn
    after_low = grad_after.astype(LOW)
    grad_mixed = contract_cols(after_low, w_out).astype(LOW)
    grad_mixed = grad_mixed.reshape(MB, ROW, HEADS, HEAD_DIM).transpose(0, 2, 1, 3)
    grad_mixed = grad_mixed.reshape(MB * HEADS, ROW, HEAD_DIM)
    grad_probs = jnp.einsum("hqd,hkd->hqk", grad_mixed, values_low, preferred_element_type=WIDE)
    grad_values = jnp.einsum("hqk,hqd->hkd", probs_low, grad_mixed, preferred_element_type=WIDE)
    grad_scores = probs * (grad_probs - jnp.sum(probs * grad_probs, axis=-1, keepdims=True))
    grad_scores = grad_scores.astype(LOW)
    scale_attn = HEAD_DIM ** (-0.5)
    grad_query = (
        jnp.einsum("hqk,hkd->hqd", grad_scores, keys_rot, preferred_element_type=WIDE)
        * scale_attn
    )
    grad_key = (
        jnp.einsum("hqk,hqd->hkd", grad_scores, queries, preferred_element_type=WIDE)
        * scale_attn
    )
    cosine, sine_table = rope_tables(ROW, HEAD_DIM)
    grad_query = rotate(grad_query, cosine, -sine_table)
    grad_key = rotate(grad_key, cosine, -sine_table)
    grad_packed = jnp.stack([grad_query, grad_key, grad_values]).astype(LOW)
    grad_packed = grad_packed.reshape(3, MB, HEADS, ROW, HEAD_DIM).transpose(1, 3, 0, 2, 4)
    grad_packed = grad_packed.reshape(MB * ROW, 3 * D)
    grad_normed = contract_cols(grad_packed, w_qkv)
    back_attn, grad_attn_gain = norm_back(inputs, attn_gain, grad_normed)
    grad_inputs = grad_after + back_attn
    return (
        grad_inputs,
        (grad_packed, after_low, grad_gu, upstream_low),
        (grad_attn_gain, grad_ffn_gain),
    )


def plane_rank():
    return lax.axis_index("dp")


def quarter(block, index):
    width = block.shape[1] // SHARE
    return lax.dynamic_slice_in_dim(block, index * width, width, 1)


def sub_quarter(block, planes, index):
    rows, width = block.shape
    split = block.reshape(rows, planes, SHARE, width // planes // SHARE)
    return lax.dynamic_index_in_dim(split, index, 2, keepdims=False).reshape(rows, -1)


def spread(make):
    rank = plane_rank()
    own = make(rank)
    rows = own.shape[0]
    full = lax.dynamic_update_slice(jnp.zeros((SHARE * rows, own.shape[1]), LOW), own, (0, 0))
    for mask in range(1, SHARE):
        piece = swap(make(rank ^ mask), "dp", mask)
        full = lax.dynamic_update_slice(full, piece, (mask * rows, 0))
    return full


def in_order(pieces, rank, axis):
    low = rank % 2 == 0
    top = rank // 2 == 0
    pairs = []
    for k in (0, 2):
        pairs.append(
            (jnp.where(low, pieces[k], pieces[k + 1]), jnp.where(low, pieces[k + 1], pieces[k]))
        )
    lower = [jnp.where(top, pairs[0][j], pairs[1][j]) for j in range(2)]
    upper = [jnp.where(top, pairs[1][j], pairs[0][j]) for j in range(2)]
    return jnp.concatenate(lower + upper, axis=axis)


def relative_blocks():
    s = lax.axis_index("section")
    i = lax.axis_index("dp")
    x, y = i % 2, i // 2
    blocks = []
    for es in (0, 1):
        for kind in (0, 1):
            for e1 in (0, 1):
                for e2 in (0, 1):
                    a, b = (x, y) if kind == 0 else (y, x)
                    within = ((a + e1) % 2) * 2 + (b + e2) % 2
                    blocks.append(((s + es) % 2) * 8 + kind * 4 + within)
    return jnp.stack(blocks).astype(jnp.int32)


TOKENS = 256


def head_piece(vocab):
    return -(-vocab // 256) * 16


def table_block(vocab, base, h_ref):
    inside = lax.broadcasted_iota(jnp.int32, h_ref.shape, 0) + base < vocab
    return jnp.where(inside, h_ref[...], 0.0).astype(LOW)


def head_scores(vocab, base, table, rows):
    logits = contract_cols(table, rows)
    index = lax.broadcasted_iota(jnp.int32, logits.shape, 0) + base
    return jnp.where(index < vocab, logits, -1e30), index


def head_stats_kernel(vocab, h_ref, rows_ref, target_ref, out):
    step = pl.program_id(0)
    base = step * h_ref.shape[0]
    table = table_block(vocab, base, h_ref)

    @pl.when(step == 0)
    def _():
        out[0:1, :] = jnp.full((1, out.shape[1]), -1e30, WIDE)
        out[1:3, :] = jnp.zeros((2, out.shape[1]), WIDE)

    for c in range(rows_ref.shape[0] // TOKENS):
        span = slice(c * TOKENS, (c + 1) * TOKENS)
        logits, index = head_scores(vocab, base, table, rows_ref[span, :])
        before = out[0:1, span]
        peak = jnp.maximum(before, jnp.max(logits, axis=0, keepdims=True))
        summed = jnp.sum(jnp.exp(logits - peak), axis=0, keepdims=True)
        picked = jnp.sum(jnp.where(index == target_ref[:, span], logits, 0.0), axis=0, keepdims=True)
        out[0:1, span] = peak
        out[1:2, span] = out[1:2, span] * jnp.exp(before - peak) + summed
        out[2:3, span] += picked


def once(shape):
    return pl.BlockSpec(shape, lambda g, *_: (0,) * len(shape), pipeline_mode=pl.Buffered(1))


def head_stats(head, rows, targets):
    vocab, count = head.shape[0], rows.shape[0]
    piece = head_piece(vocab)
    return pl.pallas_call(
        functools.partial(head_stats_kernel, vocab),
        grid=(-(-vocab // piece),),
        in_specs=[pl.BlockSpec((piece, D), lambda g: (g, 0)), once((count, D)), once((1, count))],
        out_specs=pl.BlockSpec((8, count), lambda g: (0, 0)),
        out_shape=jax.ShapeDtypeStruct((8, count), WIDE),
        compiler_params=pltpu.CompilerParams(vmem_limit_bytes=50 << 20),
        cost_estimate=pl.CostEstimate(
            flops=2 * vocab * count * D, bytes_accessed=vocab * D * 4, transcendentals=vocab * count
        ),
        name="head_stats",
    )(head, rows, targets)


def head_grads_kernel(vocab, order, h_ref, rows_ref, target_ref, lse_ref, factor_ref, mine_ref, theirs_ref, c_ref, flipped, delta):
    step = pl.program_id(0)
    base = order[step] * h_ref.shape[0]
    table = table_block(vocab, base, h_ref)
    flipped[...] = table.astype(WIDE).T.astype(LOW)

    @pl.when(step == 0)
    def _():
        c_ref[...] = jnp.zeros(c_ref.shape, WIDE)

    for c in range(rows_ref.shape[0] // TOKENS):
        span = slice(c * TOKENS, (c + 1) * TOKENS)
        logits, index = head_scores(vocab, base, table, rows_ref[span, :])
        onehot = (index == target_ref[:, span]).astype(WIDE)
        delta[:, span] = (
            (jnp.exp(logits - lse_ref[:, span]) - onehot) * factor_ref[:, span]
        ).astype(LOW)
    block = jnp.dot(delta[...], rows_ref[...], preferred_element_type=WIDE).astype(LOW)

    @pl.when(step < 8)
    def _():
        mine_ref[...] = block

    @pl.when(step >= 8)
    def _():
        theirs_ref[...] = block

    for c in range(rows_ref.shape[0] // TOKENS):
        span = slice(c * TOKENS, (c + 1) * TOKENS)
        c_ref[:, span] += jnp.dot(flipped[...], delta[:, span], preferred_element_type=WIDE)


def head_grads(head, rows, targets, lse, factor):
    vocab, count = head.shape[0], rows.shape[0]
    piece = head_piece(vocab)
    return pl.pallas_call(
        functools.partial(head_grads_kernel, vocab),
        grid_spec=pltpu.PrefetchScalarGridSpec(
            num_scalar_prefetch=1,
            grid=(16,),
            in_specs=[
                pl.BlockSpec((piece, D), lambda g, order: (order[g], 0)),
                once((count, D)),
                once((1, count)),
                once((1, count)),
                once((1, count)),
            ],
            out_specs=[
                pl.BlockSpec((piece, D), lambda g, order: (jnp.minimum(g, 7), 0)),
                pl.BlockSpec((piece, D), lambda g, order: (jnp.maximum(g - 8, 0), 0)),
                pl.BlockSpec((D, count), lambda g, order: (0, 0)),
            ],
            scratch_shapes=[pltpu.VMEM((D, piece), LOW), pltpu.VMEM((piece, count), LOW)],
        ),
        out_shape=[
            jax.ShapeDtypeStruct((8 * piece, D), LOW),
            jax.ShapeDtypeStruct((8 * piece, D), LOW),
            jax.ShapeDtypeStruct((D, count), WIDE),
        ],
        compiler_params=pltpu.CompilerParams(vmem_limit_bytes=56 << 20),
        cost_estimate=pl.CostEstimate(
            flops=6 * vocab * count * D, bytes_accessed=vocab * D * 8, transcendentals=vocab * count
        ),
        name="head_grads",
    )(relative_blocks(), head, rows, targets, lse, factor)


def head_pass(rows_low, targets, weights_tok, head, vocab_start, token_total):
    planes = lax.axis_size("fsdp")
    gathered = jnp.concatenate(
        [rows_low] + [shift(rows_low, "fsdp", step) for step in range(1, planes)], axis=0
    )
    local = targets - vocab_start
    local = jnp.where((local >= 0) & (local < head.shape[0]), local, -1)[None, :]
    stats = head_stats(head, gathered, local)[:3].reshape(3, planes, -1)
    parts = [stats] + [
        jnp.roll(shift(stats, "fsdp", step), step, axis=1) for step in range(1, planes)
    ]
    parts = jnp.stack(parts)
    peak = jnp.max(parts[:, 0], axis=0)
    total = jnp.sum(parts[:, 1] * jnp.exp(parts[:, 0] - peak[None]), axis=0)
    lse = (peak + jnp.log(total)).reshape(-1)
    loss_part = jnp.sum((lse - jnp.sum(parts[:, 2], axis=0).reshape(-1)) * weights_tok)
    factor = weights_tok / token_total
    mine, theirs, partial = head_grads(head, gathered, local, lse[None, :], factor[None, :])
    partial = partial.T.reshape(planes, -1, D)
    grad_rows = partial[0]
    for step in range(1, planes):
        grad_rows = grad_rows + shift(partial[step].astype(LOW), "fsdp", planes - step).astype(WIDE)
    return (loss_part, mine, theirs, grad_rows)


def add_low(one, other):
    return (one.astype(WIDE) + other.astype(WIDE)).astype(LOW)


def keep_half(block, mask):
    half = block.shape[0] // 2
    return add_low(block[:half], swap(block[half:], "dp", mask))


def adam_update(weight, grad, first_mom, second_mom, rate, decay):
    mom_new = BETA1 * first_mom + (1.0 - BETA1) * grad
    sec_new = BETA2 * second_mom + (1.0 - BETA2) * grad * grad
    mom_hat = mom_new / (1.0 - BETA1**STEP_COUNT)
    sec_hat = sec_new / (1.0 - BETA2**STEP_COUNT)
    weight_new = weight - rate * (mom_hat / (jnp.sqrt(sec_hat) + ADAM_EPS) + decay * weight)
    return (weight_new, mom_new, sec_new)


def exchange_kernel(planes, rows_ref, pa, pb, *refs):
    paired = planes == 4
    n = (len(refs) - 7) // (4 if paired else 2)
    parts, rows_all, head, slots = refs[:n], refs[n], refs[n + 1], refs[n + 2 : 2 * n + 2]
    send, recv, core_send, core_recv, local = refs[2 * n + 2 : 2 * n + 7]
    totals, extras = refs[2 * n + 7 : 3 * n + 7], refs[3 * n + 7 :]
    s = lax.axis_index("section")
    i = lax.axis_index("dp")
    z = lax.axis_index("fsdp")
    x, y = i % 2, i // 2
    xn, yn, diag = i + 1 - 2 * x, (i + 2) % 4, 3 - i
    partner = z + 1 - 2 * (z % 2)
    to_x, to_y, to_core = {"dp": xn}, {"dp": yn}, {"section": 1 - s}
    barrier = pltpu.get_barrier_semaphore()
    for device in [to_x, to_y, to_core] + [{"fsdp": (z + k) % planes} for k in range(1, planes)]:
        pl.semaphore_signal(barrier, inc=1, device_id=device, device_id_type=MESH)
    pl.semaphore_wait(barrier, planes + 2)
    counts = [0, 0]
    sent = []

    def put(src, dst, device):
        over = device is to_core
        k = counts[over]
        counts[over] += 1
        copy = pltpu.make_async_remote_copy(
            src_ref=src,
            dst_ref=dst,
            send_sem=(core_send if over else send).at[k],
            recv_sem=(core_recv if over else recv).at[k],
            device_id=device,
            device_id_type=MESH,
        )
        copy.start()
        sent.append(copy)
        return copy

    def take(*copies):
        for copy in copies:
            copy.wait_recv()

    piece = pa.shape[0]
    side = 4 * piece

    def head_a(xx, yy, count):
        return head.at[pl.ds(pl.multiple_of(s * 2 * side + xx * 2 * piece + yy * piece, 16), count)]

    def head_b(xx, yy, count):
        return head.at[
            pl.ds(pl.multiple_of(s * 2 * side + side + yy * 2 * piece + xx * piece, 16), count)
        ]

    own = []
    for k, (src, dst) in enumerate(
        [(rows_ref, rows_all.at[s, i, z]), (pa, head_a(x, y, piece)), (pb, head_b(x, y, piece))]
    ):
        copy = pltpu.make_async_copy(src, dst, local.at[k])
        copy.start()
        own.append(copy)
    reduce = []

    def part_of(m, plane):
        height = slots[m].shape[1]
        return parts[m].at[pl.ds(pl.multiple_of(plane * height, 16), height)]

    fetched, passed = [], []
    if paired:
        for m in range(n):
            copy = pltpu.make_async_copy(part_of(m, planes - 1 - z), totals[m], local.at[3 + m])
            copy.start()
            fetched.append(copy)
    near = [put(rows_ref, rows_all.at[s, i, z], {"fsdp": (z + k) % planes}) for k in range(1, planes)]
    head1 = [put(pa, head_a(x, y, piece), to_y), put(pb, head_b(x, y, piece), to_x)]
    if not paired:
        for m in range(n):
            for k in range(1, planes):
                target = (z + k) % planes
                reduce.append(put(part_of(m, target), slots[m].at[k - 1], {"fsdp": target}))
    for copy in own:
        copy.wait()
    take(*near)
    if paired:
        for m in range(n):
            passed.append(put(part_of(m, planes - 1 - partner), extras[m], {"fsdp": partner}))
    mid = planes // 2
    early, late = pl.ds(0, mid), pl.ds(mid, planes - mid)
    a1 = put(rows_all.at[s, i, early], rows_all.at[s, i, early], to_x)
    b1 = put(rows_all.at[s, i, late], rows_all.at[s, i, late], to_y)
    core = [put(rows_all.at[s, i], rows_all.at[s, i], to_core)]
    take(*head1)
    block = head_a(x, 0, 2 * piece)
    ha = put(block, block, to_x)
    block = head_b(0, y, 2 * piece)
    hb = put(block, block, to_y)
    take(a1, b1)
    second = []
    for who, span, device in ((i, early, to_y), (xn, early, to_y), (i, late, to_x), (yn, late, to_x)):
        block = rows_all.at[s, who, span]
        second.append(put(block, block, device))
    for who, span in ((xn, early), (yn, late)):
        block = rows_all.at[s, who, span]
        core.append(put(block, block, to_core))
    if paired:
        for copy in fetched:
            copy.wait()
        for m in range(n):
            passed[m].wait_recv()
            held = totals[m][...].astype(WIDE) + extras[m][...].astype(WIDE)
            totals[m][...] = held.astype(LOW)
            reduce.append(put(totals[m], slots[m].at[1], {"fsdp": planes - 1 - z}))
            reduce.append(put(part_of(m, partner), slots[m].at[0], {"fsdp": partner}))
    take(ha, hb)
    block = head.at[pl.ds(pl.multiple_of(s * 2 * side, 16), 2 * side)]
    core.append(put(block, block, to_core))
    take(*second)
    for who, span in ((yn, early), (diag, early), (xn, late), (diag, late)):
        block = rows_all.at[s, who, span]
        core.append(put(block, block, to_core))
    take(*reduce)
    take(*core)
    for copy in sent:
        copy.wait_send()


def exchange(planes, row_grads, pieces, parts):
    piece, vocab = pieces[0].shape
    shape = jax.ShapeDtypeStruct
    outs = [shape((2, 4, planes) + row_grads.shape, LOW), shape((16 * piece, vocab), LOW)]
    blocks = [(p.shape[0] // planes, p.shape[1]) for p in parts]
    paired = planes == 4
    outs += [shape((2 if paired else planes - 1,) + b, LOW) for b in blocks]
    copies = (planes - 1) * (1 + len(parts)) + 2 + 2 + 2 + 4
    anywhere = pl.BlockSpec(memory_space=pl.ANY)
    result = pl.pallas_call(
        functools.partial(exchange_kernel, planes),
        out_shape=outs,
        in_specs=[pl.BlockSpec(memory_space=pltpu.VMEM)] * 3 + [anywhere] * len(parts),
        out_specs=[anywhere] * len(outs),
        scratch_shapes=[pltpu.SemaphoreType.DMA((copies,))] * 2
        + [pltpu.SemaphoreType.DMA((8,))] * 2
        + [pltpu.SemaphoreType.DMA((3 + len(parts),))]
        + ([pltpu.VMEM(b, LOW) for b in blocks] * 2 if paired else []),
        compiler_params=pltpu.CompilerParams(
            collective_id=2, has_side_effects=True, vmem_limit_bytes=16 << 20
        ),
        name="exchange",
    )(row_grads, *pieces, *parts)
    return result[0], result[1], result[2:]


def block_of(vocab_rows):
    return 800 if vocab_rows % 800 == 0 else 400


def chunk_of(lists):
    return 32 if lists <= 64 else 16


def start_chunks(lists, length, stride, step, steps, starts, rows_hbm, buffer, sem):
    chunk = chunk_of(lists)

    def one(k, carry):
        at = jnp.minimum(starts[k * steps + step] // 16 * 16, length - chunk)
        src = rows_hbm.at[pl.ds(pl.multiple_of(k * stride + at, 16), chunk)]
        pltpu.make_async_copy(src, buffer.at[pl.ds(pl.multiple_of(k * chunk, 16), chunk)], sem).start()
        return carry

    lax.fori_loop(0, lists, one, 0)


def block_grad(
    lists, length, steps, step, starts, passes, bases, rows_hbm, ids_ref, near_ref, buffers, hot, wide_hot, grad, sems
):
    chunk = chunk_of(lists)
    slot = step % 2
    spare = buffers.at[2]
    width = grad.shape[0]
    stride = rows_hbm.shape[0] // lists

    @pl.when(step == 0)
    def _():
        start_chunks(lists, length, stride, 0, steps, starts, rows_hbm, buffers.at[0], sems.at[0])

    @pl.when(step + 1 < steps)
    def _():
        start_chunks(lists, length, stride, step + 1, steps, starts, rows_hbm, buffers.at[1 - slot], sems.at[1 - slot])

    pltpu.make_async_copy(buffers.at[slot], buffers.at[slot], sems.at[slot]).wait()
    lanes = lax.broadcasted_iota(jnp.int32, (chunk, width), 1) + bases[step]
    within = lax.broadcasted_iota(jnp.int32, (chunk, width), 0)

    def mark(shifted):
        def one(k, carry):
            begin = starts[k * steps + step] // 16 * 16 + shifted
            at = jnp.minimum(begin, length - chunk)
            ids = ids_ref[pl.ds(pl.multiple_of(k * length + at, 16), chunk), :]
            same = (ids == lanes) & (within >= begin - at)
            hot[pl.ds(pl.multiple_of(k * chunk, 16), chunk), :] = same.astype(WIDE).astype(LOW)
            return carry

        lax.fori_loop(0, lists, one, 0)

    down = lax.broadcasted_iota(jnp.int32, (width, lists * chunk), 0) + bases[step]
    wide_hot[...] = (down == near_ref[0]).astype(WIDE).astype(LOW)
    grad[...] = jnp.dot(wide_hot[...], buffers[slot], preferred_element_type=WIDE)

    def more(p, carry):
        mark(p * chunk)

        def one(k, inner):
            begin = starts[k * steps + step] // 16 * 16 + p * chunk
            at = jnp.minimum(begin, length - chunk)
            src = rows_hbm.at[pl.ds(pl.multiple_of(k * stride + at, 16), chunk)]
            pltpu.make_async_copy(
                src, spare.at[pl.ds(pl.multiple_of(k * chunk, 16), chunk)], sems.at[2]
            ).start()
            return inner

        lax.fori_loop(0, lists, one, 0)
        pltpu.make_async_copy(spare, spare, sems.at[2]).wait()
        grad[...] += contract_rows(hot[...], spare[...])
        return carry

    lax.fori_loop(1, passes[step], more, 0)


def table_square_kernel(lists, length, steps, starts, passes, bases, rows_hbm, ids_ref, near_ref, out, buffers, hot, wide_hot, grad, sems):
    step = pl.program_id(0)
    block_grad(lists, length, steps, step, starts, passes, bases, rows_hbm, ids_ref, near_ref, buffers, hot, wide_hot, grad, sems)
    part = jnp.sum((grad[...] * grad[...]).reshape(-1, 8, D), axis=0)
    part = jnp.where(passes[step] > 0, part, 0.0)

    @pl.when(step == 0)
    def _():
        out[...] = part

    @pl.when(step > 0)
    def _():
        out[...] += part


def table_adam_kernel(
    lists, length, steps, rate, decay, starts, passes, bases, clip, rows_hbm, ids_ref, near_ref, w, m, v, w_new, m_new, v_new, low, buffers, hot, wide_hot, grad, sems
):
    step = pl.program_id(0)
    block_grad(lists, length, steps, step, starts, passes, bases, rows_hbm, ids_ref, near_ref, buffers, hot, wide_hot, grad, sems)
    weight, mom, sec = adam_update(w[...], grad[...] * clip[0], m[...], v[...], rate, decay)
    w_new[...] = weight
    m_new[...] = mom
    v_new[...] = sec
    low[...] = weight.astype(LOW)


def table_scratch(lists, width):
    chunk = chunk_of(lists)
    return [
        pltpu.VMEM((3, lists * chunk, D), LOW),
        pltpu.VMEM((lists * chunk, width), LOW),
        pltpu.VMEM((width, lists * chunk), LOW),
        pltpu.VMEM((width, D), WIDE),
        pltpu.SemaphoreType.DMA((3,)),
    ]


def chunk_scalars(ids_sorted, bases, width):
    chunk = chunk_of(ids_sorted.shape[0])
    edges = bases[None, :, None]
    starts = jnp.sum((ids_sorted[:, None, :] < edges).astype(jnp.int32), axis=-1)
    ends = jnp.sum((ids_sorted[:, None, :] < edges + width).astype(jnp.int32), axis=-1)
    passes = jnp.max((ends - starts // 16 * 16 + chunk - 1) // chunk, axis=0)
    lists, length = ids_sorted.shape
    groups = length // 16
    begin = (starts // 16).T
    at = jnp.minimum(begin, groups - chunk // 16)
    by_group = ids_sorted.reshape(lists, groups, 16).transpose(1, 0, 2).reshape(groups, -1)
    widen = jnp.arange(lists * 16)[None, :] // 16 == jnp.arange(lists)[:, None]
    both = jnp.concatenate([at, begin], axis=0).astype(LOW)
    both = jnp.dot(both, widen.astype(LOW), preferred_element_type=WIDE).astype(jnp.int32)
    both = lax.optimization_barrier(both)
    steps = begin.shape[0]
    pieces = []
    for k in range(chunk // 16):
        wanted = both[:steps] + k
        found = jnp.zeros(wanted.shape, jnp.int32)
        for g in range(groups):
            found = jnp.where(wanted == g, by_group[g][None], found)
        found = jnp.where(wanted >= both[steps:], found, -(1 << 30))
        pieces.append(lax.optimization_barrier(found).reshape(-1, lists, 16))
    near = jnp.stack(pieces, axis=2).reshape(begin.shape[0], 1, -1)
    return starts.reshape(-1), jnp.maximum(passes, 1), near


def table_square(ids_sorted, ids_column, rows_flat, rank, ranks, vocab_rows):
    lists, length = ids_sorted.shape
    width = block_of(vocab_rows)
    total = vocab_rows // width
    steps = -(-total // ranks)
    blocks = rank + ranks * jnp.arange(steps, dtype=jnp.int32)
    bases = blocks * width
    starts, passes, near = chunk_scalars(ids_sorted, bases, width)
    passes = jnp.where(blocks < total, passes, 0)
    out = pl.pallas_call(
        functools.partial(table_square_kernel, lists, length, steps),
        grid_spec=pltpu.PrefetchScalarGridSpec(
            num_scalar_prefetch=3,
            grid=(steps,),
            in_specs=[
                pl.BlockSpec(memory_space=pl.ANY),
                pl.BlockSpec(
                    (lists * length, 1), lambda g, *_: (0, 0), pipeline_mode=pl.Buffered(1)
                ),
                pl.BlockSpec((1, 1, near.shape[2]), lambda g, *_: (g, 0, 0)),
            ],
            out_specs=pl.BlockSpec((8, D), lambda g, *_: (0, 0)),
            scratch_shapes=table_scratch(lists, width),
        ),
        out_shape=jax.ShapeDtypeStruct((8, D), WIDE),
        compiler_params=pltpu.CompilerParams(vmem_limit_bytes=56 << 20),
        name="table_square",
    )(starts, passes, bases, rows_flat, ids_column, near)
    return jnp.sum(out)


def table_adam(ids_sorted, ids_column, rows_flat, clip_scale, table, mom, sec, rate, decay):
    lists, length = ids_sorted.shape
    vocab_rows = table.shape[0]
    width = block_of(vocab_rows)
    steps = vocab_rows // width
    bases = jnp.arange(steps, dtype=jnp.int32) * width
    starts, passes, near = chunk_scalars(ids_sorted, bases, width)
    block = pl.BlockSpec((width, D), lambda g, *_: (g, 0))
    wide = jax.ShapeDtypeStruct(table.shape, WIDE)
    return pl.pallas_call(
        functools.partial(table_adam_kernel, lists, length, steps, rate, decay),
        grid_spec=pltpu.PrefetchScalarGridSpec(
            num_scalar_prefetch=4,
            grid=(steps,),
            in_specs=[
                pl.BlockSpec(memory_space=pl.ANY),
                pl.BlockSpec(
                    (lists * length, 1), lambda g, *_: (0, 0), pipeline_mode=pl.Buffered(1)
                ),
                pl.BlockSpec((1, 1, near.shape[2]), lambda g, *_: (g, 0, 0)),
                block,
                block,
                block,
            ],
            out_specs=[block] * 4,
            scratch_shapes=table_scratch(lists, width),
        ),
        out_shape=[wide, wide, wide, jax.ShapeDtypeStruct(table.shape, LOW)],
        compiler_params=pltpu.CompilerParams(vmem_limit_bytes=60 << 20),
        cost_estimate=pl.CostEstimate(
            flops=steps * 2 * width * lists * chunk_of(lists) * D,
            bytes_accessed=table.size * 26,
            transcendentals=table.size,
        ),
        name="table_adam",
    )(starts, passes, bases, clip_scale.reshape(1), rows_flat, ids_column, near, table, mom, sec)


HEAD_BLOCK = 800


def head_adam_kernel(rate, decay, clip, grad, w, m, v, w_new, m_new, v_new, low):
    scaled = grad[...].astype(WIDE) * clip[0]
    weight, mom, sec = adam_update(w[...], scaled, m[...], v[...], rate, decay)
    w_new[...] = weight
    m_new[...] = mom
    v_new[...] = sec
    low[...] = weight.astype(LOW)


def head_adam(grad, clip_scale, head, mom, sec, rate, decay):
    vocab = head.shape[1]
    block = pl.BlockSpec((HEAD_BLOCK, D), lambda g, *_: (g, 0))
    wide = jax.ShapeDtypeStruct((vocab, D), WIDE)
    results = pl.pallas_call(
        functools.partial(head_adam_kernel, rate, decay),
        grid_spec=pltpu.PrefetchScalarGridSpec(
            num_scalar_prefetch=1,
            grid=(-(-vocab // HEAD_BLOCK),),
            in_specs=[block] * 4,
            out_specs=[block] * 4,
        ),
        out_shape=[wide, wide, wide, jax.ShapeDtypeStruct((vocab, D), LOW)],
        compiler_params=pltpu.CompilerParams(vmem_limit_bytes=56 << 20),
        cost_estimate=pl.CostEstimate(
            flops=head.size * 20, bytes_accessed=head.size * 28, transcendentals=head.size
        ),
        name="head_adam",
    )(clip_scale.reshape(1), grad, head.T, mom.T, sec.T)
    return [item.T for item in results]


def small_gather_kernel(axes, sizes, *refs):
    n = (len(refs) - 2) // 2
    blocks, outs, send, recv = refs[:n], refs[n : 2 * n], refs[2 * n], refs[2 * n + 1]
    mine = [lax.axis_index(axis) for axis in axes]
    slot = 0
    for index, size in zip(mine, sizes):
        slot = slot * size + index
    offsets = [()]
    for size in sizes:
        offsets = [o + (k,) for o in offsets for k in range(size)]
    peers = [
        {axis: (index + k) % size for axis, index, size, k in zip(axes, mine, sizes, offset)}
        for offset in offsets[1:]
    ]
    barrier = pltpu.get_barrier_semaphore()
    for peer in peers:
        pl.semaphore_signal(barrier, inc=1, device_id=peer, device_id_type=MESH)
    pl.semaphore_wait(barrier, len(peers))
    copies = []
    for m in range(n):
        for k, peer in enumerate(peers):
            copy = pltpu.make_async_remote_copy(
                src_ref=blocks[m],
                dst_ref=outs[m].at[slot],
                send_sem=send.at[m * len(peers) + k],
                recv_sem=recv.at[m * len(peers) + k],
                device_id=peer,
                device_id_type=MESH,
            )
            copy.start()
            copies.append(copy)
        outs[m][slot] = blocks[m][...]
    for copy in copies:
        copy.wait()


def small_gather(blocks, axes, identity):
    sizes = [lax.axis_size(axis) for axis in axes]
    count = math.prod(sizes)
    copies = (count - 1) * len(blocks)
    whole = pl.BlockSpec(memory_space=pltpu.VMEM)
    return pl.pallas_call(
        functools.partial(small_gather_kernel, axes, sizes),
        out_shape=[jax.ShapeDtypeStruct((count,) + b.shape, b.dtype) for b in blocks],
        in_specs=[whole] * len(blocks),
        out_specs=[whole] * len(blocks),
        scratch_shapes=[pltpu.SemaphoreType.DMA((copies,))] * 2,
        compiler_params=pltpu.CompilerParams(collective_id=identity, has_side_effects=True),
        name=f"small_gather_{identity}",
    )(*blocks)


def finish_kernel(n, me, *refs):
    parts, slots, pieces = refs[:n], refs[n : 2 * n], refs[2 * n : 2 * n + 2]
    shards, out = refs[2 * n + 2 : 3 * n + 2], refs[3 * n + 2]
    total = jnp.zeros((), WIDE)
    for m in range(n):
        held = parts[m][...].astype(WIDE)
        for k in range(slots[m].shape[0]):
            held = held + slots[m][k].astype(WIDE)
        low = held.astype(LOW)
        shards[m][...] = low
        held = low.astype(WIDE)
        total = total + jnp.sum(held * held)
    for piece in pieces:
        held = piece[...].astype(WIDE)
        total = total + jnp.sum(held * held)
    out[...] = jnp.full(out.shape, total, WIDE)


def finish(me, parts, slots, pieces):
    blocks = [slot.shape[1:] for slot in slots]
    whole = lambda shape: pl.BlockSpec(shape, lambda g, *_: (0,) * len(shape))
    results = pl.pallas_call(
        functools.partial(finish_kernel, len(parts)),
        grid_spec=pltpu.PrefetchScalarGridSpec(
            num_scalar_prefetch=1,
            grid=(1,),
            in_specs=[pl.BlockSpec(block, lambda g, me: (me[0], 0)) for block in blocks]
            + [whole(item.shape) for item in list(slots) + list(pieces)],
            out_specs=[whole(block) for block in blocks] + [whole((8, 128))],
        ),
        out_shape=[jax.ShapeDtypeStruct(block, LOW) for block in blocks]
        + [jax.ShapeDtypeStruct((8, 128), WIDE)],
        compiler_params=pltpu.CompilerParams(vmem_limit_bytes=40 << 20),
        name="finish",
    )(me.astype(jnp.int32).reshape(1), *parts, *slots, *pieces)
    return list(results[:-1]), results[-1][0, 0]


def per_device(
    token_ids,
    next_ids,
    seq_lengths,
    embedding,
    embedding_mom,
    embedding_sec,
    head_table,
    head_mom,
    head_sec,
    w_qkv,
    qkv_mom,
    qkv_sec,
    w_out,
    out_mom,
    out_sec,
    w_gateup,
    gateup_mom,
    gateup_sec,
    w_down,
    down_mom,
    down_sec,
    gains,
    gains_mom,
    gains_sec,
):
    planes = lax.axis_size("fsdp")
    replicas = lax.axis_size("dp")
    first = lax.axis_index("section") == 0
    first_f = first.astype(WIDE)
    me = lax.axis_index("fsdp")
    token_total = jnp.sum(seq_lengths).astype(WIDE)
    tokens = MB * ROW

    my_ids = jnp.stack([token_ids.reshape(-1), next_ids.reshape(-1)])
    ids_all, gains_all = small_gather([my_ids, gains[0]], ("dp", "fsdp"), 3)
    ids_all = ids_all.reshape(replicas, planes, 2, tokens)
    gains_full = gains_all[:planes].transpose(1, 0, 2).reshape(3, D)
    gains_full = lax.optimization_barrier(gains_full.astype(LOW)).astype(WIDE)
    group_ids = pick(ids_all, lax.axis_index("dp"))
    rel_ids = jnp.stack([pick(group_ids, (me - step) % planes) for step in range(planes)])
    my_kind = jnp.where(first, rel_ids[:, 0], rel_ids[:, 1])
    vocab_rows = embedding.shape[0]
    vocab_start = me * vocab_rows
    local = my_kind - vocab_start
    inside = (local >= 0) & (local < vocab_rows)
    found = jnp.take(embedding, jnp.clip(local, 0, vocab_rows - 1), axis=0)
    found = lax.optimization_barrier(jnp.where(inside[..., None], found, 0.0).astype(LOW))
    looked = found[0].astype(WIDE)
    for step in range(1, planes):
        looked = looked + shift(found[step], "fsdp", planes - step).astype(WIDE)
    next_embed = swap(looked.astype(LOW), "section", 1).astype(WIDE)

    lists = ids_all.transpose(2, 0, 1, 3).reshape(-1, tokens) - vocab_start
    place = jnp.arange(tokens)
    before = (lists[:, None, :] < lists[:, :, None]) | (
        (lists[:, None, :] == lists[:, :, None]) & (place[None, None, :] < place[None, :, None])
    )
    ranks = jnp.sum(before.astype(jnp.int32), axis=-1)
    sorted_ids = jnp.sum(
        jnp.where(ranks[:, None, :] == place[None, :, None], lists[:, None, :], 0), axis=-1
    )
    own_list = (
        lax.axis_index("section") * replicas + lax.axis_index("dp")
    ) * planes + me
    arrange = (pick(ranks, own_list)[None, :] == place[:, None]).astype(LOW)

    full = gather_weights(
        planes,
        replicas,
        [w_qkv[0].astype(LOW), w_out[0].astype(LOW), w_gateup[0].astype(LOW), w_down[0].astype(LOW)],
    )
    layer_weights = (full[0], full[1], full[2], full[3], gains_full[0], gains_full[1])
    head_gain = gains_full[2]

    first_out, _ = layer_fwd(looked, layer_weights)
    middle = swap(first_out.astype(LOW), "section", 1).astype(WIDE)
    layer_in = jnp.where(first, looked, middle)
    layer_out, saved = layer_fwd(layer_in, layer_weights)
    final_state = norm_fwd(layer_out, head_gain)
    arrived = swap(final_state.astype(LOW), "section", 1).astype(WIDE)
    merged_in = jnp.where(first, arrived + next_embed, layer_out)
    head_in = norm_fwd(merged_in, head_gain)

    lengths = seq_lengths.reshape(replicas, planes, MB)[lax.axis_index("dp")]
    lengths = jnp.stack([pick(lengths, (me - step) % planes) for step in range(planes)])
    targets_main = rel_ids[:, 1].reshape(planes, MB, ROW)
    shifted = jnp.concatenate([targets_main[..., 1:], targets_main[..., :1]], axis=-1)
    targets = jnp.where(first, shifted, targets_main)
    limit = lengths - first.astype(jnp.int32)
    positions = jnp.arange(ROW, dtype=jnp.int32)
    weights_tok = (positions < limit[..., None]).astype(WIDE) * jnp.where(first, MTP_WEIGHT, 1.0)
    left = [saved[0], saved[6], saved[8]]
    left_all = spread(
        lambda index: jnp.concatenate(left + [sub_quarter(saved[10], planes, index)], axis=1)
    )
    loss_part, mine, theirs, grad_in = head_pass(
        head_in.astype(LOW),
        targets.reshape(-1),
        weights_tok.reshape(-1),
        head_table.T,
        vocab_start,
        token_total,
    )
    sorted_ids, loss_part = lax.optimization_barrier((sorted_ids, loss_part))
    merged_grad, mtp_gain = norm_back(merged_in, head_gain, grad_in)
    merged_low = merged_grad.astype(LOW)
    sent = swap(merged_low, "section", 1).astype(WIDE)
    top_grad, top_gain = norm_back(layer_out, head_gain, grad_in + sent)
    head_gain_grad = jnp.where(first, mtp_gain, top_gain)
    half = add_low(mine, swap(theirs, "section", 1))
    top_grad, left_all = lax.optimization_barrier((top_grad, left_all))
    below, _, _ = layer_back(layer_in, layer_weights, saved, top_grad)
    below, half = lax.optimization_barrier((below.astype(LOW), half))
    side = half.shape[0] // 2
    piece_a, piece_b = keep_half(half[:side], 1), keep_half(half[side:], 2)
    upstream = jnp.where(first, swap(below, "section", 1).astype(WIDE), top_grad)
    grad_inputs, right, gain_parts = layer_back(layer_in, layer_weights, saved, upstream)
    grad_packed, after_low, grad_gu, upstream_low = right
    after_low, piece_a, piece_b = lax.optimization_barrier((after_low, piece_a, piece_b))
    piece_a, piece_b = keep_half(piece_a, 2), keep_half(piece_b, 1)
    early = spread(
        lambda index: jnp.concatenate([upstream_low, quarter(grad_gu, index)], axis=1)
    )
    late = spread(
        lambda index: jnp.concatenate([quarter(after_low, index), quarter(grad_packed, index)], axis=1)
    )
    cut = D // SHARE
    parts = [
        contract_rows(left_all[:, 2 * D : 3 * D], early[:, D:]),
        contract_rows(left_all[:, 3 * D :], early[:, :D]),
        contract_rows(left_all[:, :D], late[:, cut:]),
        contract_rows(left_all[:, D : 2 * D], late[:, :cut]),
    ]
    parts = [part.astype(LOW) for part in parts]
    gains_grad = jnp.stack([gain_parts[0], gain_parts[1], head_gain_grad])

    row_grads = jnp.where(first, grad_inputs.astype(LOW), sent.astype(LOW))
    row_grads = jnp.dot(arrange, row_grads, preferred_element_type=WIDE).astype(LOW)
    row_grads = jnp.concatenate(
        [row_grads, gains_grad.astype(LOW), jnp.zeros((13, D), LOW)], axis=0
    )
    rows_all, grad_head, slots = exchange(planes, row_grads, (piece_a, piece_b), parts)
    rows_flat = rows_all.reshape(-1, D)
    gains_grad = pick(rows_all[:, :, :, tokens : tokens + 3], lax.axis_index("section"))
    gains_grad = jnp.sum(gains_grad.astype(WIDE), axis=(0, 1))
    gains_grad = lax.dynamic_slice_in_dim(gains_grad, me * (D // planes), D // planes, 1)
    ids_column = sorted_ids.reshape(-1, 1)

    shards, shard_squares = finish(me, parts, slots, (piece_a, piece_b))
    group = lax.axis_index("section") * replicas + lax.axis_index("dp")
    squares = table_square(sorted_ids, ids_column, rows_flat, group, 2 * replicas, vocab_rows)
    squares = squares + shard_squares + jnp.sum(gains_grad * gains_grad) / replicas
    totals = jnp.stack([squares, loss_part / planes])[:, None] * jnp.ones((1, 128), WIDE)
    totals = jnp.sum(small_gather([totals], ("section", "dp", "fsdp"), 4)[0], axis=0)[:, 0]
    grad_norm = jnp.sqrt(totals[0])
    loss_total = totals[1]
    clip_scale = CLIP / jnp.maximum(grad_norm, CLIP)

    shards, clip_scale = lax.optimization_barrier((shards, clip_scale))
    widths = [0, 2 * D, 3 * D, 3 * D + 3 * cut, 4 * D]
    packed = jnp.concatenate(shards, axis=1)
    rank = plane_rank()
    others = [packed] + [swap(packed, "dp", mask) for mask in range(1, SHARE)]
    layer_grads = [
        in_order([other[:, lo:hi] for other in others], rank, 0 if index == 1 else 1).astype(WIDE)
        for index, (lo, hi) in enumerate(zip(widths[:-1], widths[1:]))
    ]
    params = (w_qkv[0], w_out[0], w_gateup[0], w_down[0], gains[0])
    grads_all = (
        layer_grads[2],
        layer_grads[3],
        layer_grads[0],
        layer_grads[1],
        gains_grad,
    )
    moments = (
        (qkv_mom[0], qkv_sec[0]),
        (out_mom[0], out_sec[0]),
        (gateup_mom[0], gateup_sec[0]),
        (down_mom[0], down_sec[0]),
        (gains_mom[0], gains_sec[0]),
    )
    rates = (0.03, 0.12, 0.03, 0.03, 0.6)
    decays = (0.1, 0.1, 0.1, 0.1, 0.0)
    outputs = [loss_total, token_total, grad_norm]
    outputs += table_adam(
        sorted_ids,
        ids_column,
        rows_flat,
        clip_scale,
        embedding,
        embedding_mom,
        embedding_sec,
        0.6,
        0.1,
    )
    outputs += head_adam(grad_head, clip_scale, head_table, head_mom, head_sec, 0.03, 0.1)
    for index in range(5):
        weight_new, mom_new, sec_new = adam_update(
            params[index],
            grads_all[index] * clip_scale,
            moments[index][0],
            moments[index][1],
            rates[index],
            decays[index],
        )
        outputs.extend([weight_new[None], mom_new[None], sec_new[None]])
        if index < 4:
            outputs.append(weight_new.astype(LOW)[None])
    return tuple(outputs)


def solution(mesh):
    placed = (
        P(("dp", "fsdp"), None),
        P(("dp", "fsdp"), None),
        P(),
        P("fsdp", None),
        P("fsdp", None),
        P("fsdp", None),
        P(None, "fsdp"),
        P(None, "fsdp"),
        P(None, "fsdp"),
        P("section", "fsdp", None),
        P("section", "fsdp", None),
        P("section", "fsdp", None),
        P("section", "fsdp", None),
        P("section", "fsdp", None),
        P("section", "fsdp", None),
        P("section", "fsdp", None),
        P("section", "fsdp", None),
        P("section", "fsdp", None),
        P("section", "fsdp", None),
        P("section", "fsdp", None),
        P("section", "fsdp", None),
        P("section", None, "fsdp"),
        P("section", None, "fsdp"),
        P("section", None, "fsdp"),
    )
    return jax.shard_map(
        per_device,
        mesh=mesh,
        in_specs=placed,
        out_specs=(
            P(),
            P(),
            P(),
            P("fsdp", None),
            P("fsdp", None),
            P("fsdp", None),
            P("fsdp", None),
            P(None, "fsdp"),
            P(None, "fsdp"),
            P(None, "fsdp"),
            P(None, "fsdp"),
            P("section", "fsdp", None),
            P("section", "fsdp", None),
            P("section", "fsdp", None),
            P("section", "fsdp", None),
            P("section", "fsdp", None),
            P("section", "fsdp", None),
            P("section", "fsdp", None),
            P("section", "fsdp", None),
            P("section", "fsdp", None),
            P("section", "fsdp", None),
            P("section", "fsdp", None),
            P("section", "fsdp", None),
            P("section", "fsdp", None),
            P("section", "fsdp", None),
            P("section", "fsdp", None),
            P("section", "fsdp", None),
            P("section", None, "fsdp"),
            P("section", None, "fsdp"),
            P("section", None, "fsdp"),
        ),
        check_vma=False,
    )
```
